32 devices in a mesh: groups: 2 (over y), res: 4 (over z), col: 2 (over x), seq: 2 (over core).
Axes of the slice: x: 2, y: 2, z: 4, core: 2. Of those that a mesh axis runs over, the one named last changes fastest.
Arguments:
- alignment_states: bfloat16 [128, 128, 256], P(('groups', 'res', 'seq'), 'col'), parts along dimension 0, may hold values from -6 to 6
- standardize_scale: float32 [256], replicated, may hold values from 0.5 to 1.5
- standardize_shift: float32 [256], replicated, may hold values from -3 to 3
- first_factor_coeffs: bfloat16 [256, 32], replicated, may hold values from -0.375 to 0.375
- first_factor_offset: float32 [32], replicated, may hold values from -3 to 3
- second_factor_coeffs: bfloat16 [256, 32], replicated, may hold values from -0.375 to 0.375
- second_factor_offset: float32 [32], replicated, may hold values from -3 to 3
- final_coeffs: bfloat16 [1024, 128], replicated, may hold values from -0.1875 to 0.1875
- final_offset: float32 [128], replicated, may hold values from -3 to 3
Outputs:
- pair: bfloat16 [4, 64, 128, 128], P('groups', ('res', 'seq'), 'col'), parts along dimension 0
The draws below stay inside these ranges and needn't reach their ends.
There are 2 independent parts, one for each index of `groups`. The reference program is written for one: setup_inputs(seed, part) draws one part's arguments, and reference() takes and returns one part's arrays. A program takes and returns all parts, laid end to end along the dimension named above; an argument that names none is the same for every part. Nothing has to cross between parts.
All inputs are finite; a program needn't handle non-finite values.
Results may differ from the reference program's by a relative error of at most 0.0037.
Values may be sent and summed in bfloat16 or wider, within the bound.
No kernel may reach another device: no remote copies, remote signals or barrier semaphores. Data moves between devices by JAX's collectives and lax.ppermute only.
A program may use at most 64 MiB of HBM per device.

```python
import jax
import jax.numpy as jnp
from jax import lax

ALIGN_DIM = 256
HIDDEN_DIM = 32
P_SIZE = 128
RES_DEV = 16
SEQ_DEV = 8
RSPAN = 64
NUM_POSITIONS = 128
NUM_ALIGNED = 64
N_RES = 4
N_COL = 2
N_SEQ = 2


def shard_levels(key, extent, shards, least, top_value):
    level, own = 1.0, jax.random.fold_in(key, 6)
    for axis_at, shards_of in shards:
        draws = jnp.exp(jax.random.uniform(jax.random.fold_in(own, axis_at), (shards_of,), jnp.float32, least / len(shards), top_value / len(shards)))
        level = level * jnp.repeat(draws, extent[axis_at] // shards_of).reshape([-1 if axis == axis_at else 1 for axis in range(len(extent))])
    return level


def gaussian(rng, extent, width, bound, cuts=(), dtype=jnp.bfloat16):
    array = width * jax.random.normal(rng, extent, jnp.float32)
    if cuts:
        array = array * shard_levels(rng, extent, cuts, -0.22, 0.18)
    return jnp.clip(array, -bound, bound).astype(dtype)


def setup_inputs(seed: int = 0, part: int = 0) -> dict:
    splits = jax.random.split(jax.random.key(seed), 10)
    own_keys = jax.random.split(jax.random.fold_in(splits[9], part), 10)
    alignment_states = gaussian(own_keys[0], (NUM_ALIGNED, NUM_POSITIONS, ALIGN_DIM), 1.0, 6.0, ((0, 8), (1, 2)))
    standardize_scale = jnp.clip(1.0 + 0.1 * jax.random.normal(splits[1], (ALIGN_DIM,), jnp.float32), 0.5, 1.5)
    standardize_shift = gaussian(splits[2], (ALIGN_DIM,), 0.5, 3.0, (), jnp.float32)
    first_factor_coeffs = gaussian(splits[3], (ALIGN_DIM, HIDDEN_DIM), ALIGN_DIM ** -0.5, 0.375)
    first_factor_offset = gaussian(splits[4], (HIDDEN_DIM,), 0.5, 3.0, (), jnp.float32)
    second_factor_coeffs = gaussian(splits[5], (ALIGN_DIM, HIDDEN_DIM), ALIGN_DIM ** -0.5, 0.375)
    second_factor_offset = gaussian(splits[6], (HIDDEN_DIM,), 0.5, 3.0, (), jnp.float32)
    final_coeffs = gaussian(splits[7], (HIDDEN_DIM * HIDDEN_DIM, P_SIZE), (HIDDEN_DIM * HIDDEN_DIM) ** -0.5, 0.1875)
    final_offset = gaussian(splits[8], (P_SIZE,), 0.5, 3.0, (), jnp.float32)
    return {"alignment_states": alignment_states, "standardize_scale": standardize_scale, "standardize_shift": standardize_shift, "first_factor_coeffs": first_factor_coeffs, "first_factor_offset": first_factor_offset, "second_factor_coeffs": second_factor_coeffs, "second_factor_offset": second_factor_offset, "final_coeffs": final_coeffs, "final_offset": final_offset}


def affine_map_apply(alignment_states, standardize_scale, standardize_shift, coefficient_table, offset_terms):
    input_tensor = alignment_states.astype(jnp.float32)
    mean = lax.optimization_barrier(jnp.mean(input_tensor, axis=-1, keepdims=True))
    centred = input_tensor - mean
    variance = lax.optimization_barrier(jnp.mean(centred * centred, axis=-1, keepdims=True))
    normed = (centred * lax.rsqrt(variance + 1e-05) * standardize_scale + standardize_shift).astype(jnp.bfloat16)
    normed = lax.optimization_barrier(normed)
    out = jnp.einsum('src,ck->srk', normed.astype(jnp.float32), coefficient_table.astype(jnp.float32)) + offset_terms
    return out.astype(jnp.bfloat16)

def reference(alignment_states, standardize_scale, standardize_shift, first_factor_coeffs, first_factor_offset, second_factor_coeffs, second_factor_offset, final_coeffs, final_offset):
    first_factor_states = affine_map_apply(alignment_states, standardize_scale, standardize_shift, first_factor_coeffs, first_factor_offset)
    second_factor_states = affine_map_apply(alignment_states, standardize_scale, standardize_shift, second_factor_coeffs, second_factor_offset)
    left_five = first_factor_states.astype(jnp.float32).reshape(N_RES, N_SEQ, SEQ_DEV, NUM_POSITIONS, HIDDEN_DIM)
    right_f = second_factor_states.astype(jnp.float32)
    w_flat = final_coeffs.astype(jnp.float32)

    def column_block(start):
        block = lax.dynamic_slice_in_dim(right_f, start, RES_DEV, 1)
        block = block.reshape(N_RES, N_SEQ, SEQ_DEV, RES_DEV, HIDDEN_DIM)
        outer = jnp.einsum('agtic,agtje->gijce', left_five, block).astype(jnp.bfloat16)
        outer = lax.optimization_barrier(outer).astype(jnp.float32)
        outer = outer.reshape(N_SEQ, NUM_POSITIONS, RES_DEV, HIDDEN_DIM * HIDDEN_DIM)
        summed = jnp.einsum('gijk,kp->ijp', outer, w_flat)
        return (summed / NUM_ALIGNED + final_offset).astype(jnp.bfloat16)
    starts = (jnp.arange(NUM_POSITIONS // RES_DEV) * RES_DEV).astype(jnp.int32)
    blocks = lax.map(column_block, starts)
    pair = blocks.transpose(1, 0, 2, 3).reshape(NUM_POSITIONS, NUM_POSITIONS, P_SIZE)
    return pair.reshape(N_COL, RSPAN, NUM_POSITIONS, P_SIZE)
```

```python
import functools

import jax
import jax.numpy as jnp
from jax import lax
from jax.experimental import pallas as pl
from jax.experimental.pallas import tpu as pltpu
from jax.sharding import PartitionSpec as P

LANES = 128
SUBLANES = 8
VMEM = pl.BlockSpec(memory_space=pltpu.VMEM)


def partner(index, step, size):
    return index ^ step if size & (size - 1) == 0 else (index + step) % size


def lane_index(shape):
    return lax.broadcasted_iota(jnp.int32, shape, len(shape) - 1)


def project_kernel(dims, x_ref, scale_ref, shift_ref, w1_ref, b1_ref, w2_ref, b2_ref, *refs):
    n_res, n_col, _, _ = dims
    outs, (rows_scr, lane_scr, right_scr) = refs[:-3], refs[-3:]
    right_out, left_out = outs[0], outs[1]
    z_outs = outs[2 : 2 + n_res - 1]
    x_outs = outs[2 + n_res - 1 :]
    n_s, span, width = x_ref.shape
    chans = w1_ref.shape[1]
    fold = LANES // chans
    half = LANES // 2
    x = x_ref[...].reshape(n_s * span, width).astype(jnp.float32)
    mean = jnp.mean(x, axis=-1, keepdims=True)
    centred = x - mean
    variance = jnp.mean(centred * centred, axis=-1, keepdims=True)
    normed = (centred * lax.rsqrt(variance + 1e-05) * scale_ref[...] + shift_ref[...]).astype(jnp.bfloat16)

    spread = lax.broadcasted_iota(jnp.int32, (chans, LANES), 1) % chans
    spread = (spread == lax.broadcasted_iota(jnp.int32, (chans, LANES), 0)).astype(jnp.bfloat16)
    w1 = jnp.dot(w1_ref[...], spread, preferred_element_type=jnp.float32).astype(jnp.bfloat16)
    b1 = jnp.concatenate([b1_ref[...]] * fold, axis=1)
    rows_scr[...] = jnp.dot(normed, w1, preferred_element_type=jnp.float32) + b1
    n_rows = n_s * span // fold
    owner = lane_index((n_rows, LANES)) // chans
    merged = rows_scr[pl.ds(0, n_rows, stride=fold), :]
    for turn in range(1, fold):
        merged = jnp.where(owner == turn, rows_scr[pl.ds(turn, n_rows, stride=fold), :], merged)
    groups = span // fold
    for s in range(n_s):
        lane_scr[pl.ds(s, groups, stride=n_s), :] = merged[s * groups : (s + 1) * groups]
    left_out[...] = lane_scr[...].astype(jnp.bfloat16)

    eye = lax.broadcasted_iota(jnp.int32, (chans, chans), 0) == lane_index((chans, chans))
    w2 = lax.dot_general(
        eye.astype(jnp.bfloat16), w2_ref[...], (((1,), (1,)), ((), ())), preferred_element_type=jnp.float32
    ).astype(jnp.bfloat16)
    b2 = jnp.sum(jnp.where(eye, b2_ref[...], 0.0), axis=1, keepdims=True)
    right = lax.dot_general(w2, normed, (((1,), (1,)), ((), ())), preferred_element_type=jnp.float32) + b2
    pairs = chans // 2
    low = lane_index((pairs, LANES)) < half
    blocks = span // half
    for tile in range(n_s * span // LANES):
        here = right[:, tile * LANES : (tile + 1) * LANES]
        there = pltpu.roll(here, half, 1)
        for side in range(2):
            s, block = divmod(2 * tile + side, blocks)
            first, second = (here, there) if side == 0 else (there, here)
            right_scr[pl.ds(block * pairs * n_s + s, pairs, stride=n_s), :] = jnp.where(
                low, first[:pairs], second[pairs:]
            )
    right_slab = right_scr[...].astype(jnp.bfloat16)
    right_out[...] = right_slab

    here = lax.axis_index("res")
    n_right = right_slab.shape[0]
    part = left_out.shape[0] // n_res
    for k, out in enumerate(z_outs):
        out[:n_right] = right_slab
        out[n_right:] = left_out[pl.ds(pl.multiple_of(partner(here, k + 1, n_res) * part, part), part), :]
    for k, out in enumerate(x_outs):
        out[...] = left_out[pl.ds(pl.multiple_of(partner(here, k % n_res, n_res) * part, part), part), :]


def pack_kernel(dims, right_ref, left_ref, *refs):
    n_res, n_col, n_seq, step = dims
    ins, out = refs[:-1], refs[-1]
    z_ins, x_ins = ins[: n_res - 1], ins[n_res - 1 :]
    n_right = right_ref.shape[0]
    part = left_ref.shape[0] // n_res
    own = part // n_seq
    other = partner(lax.axis_index("seq"), step, n_seq)
    out[:n_right] = right_ref[...]
    for k, ref in enumerate(z_ins):
        out[(k + 1) * n_right : (k + 2) * n_right] = ref[:n_right]
    base = n_res * n_right
    start = pl.multiple_of(lax.axis_index("res") * part + other * own, own)
    out[base : base + own] = left_ref[pl.ds(start, own), :]
    for k, ref in enumerate(z_ins):
        at = base + (k + 1) * own
        out[at : at + own] = ref[pl.ds(pl.multiple_of(n_right + other * own, own), own), :]
    for k, ref in enumerate(x_ins):
        at = base + (n_res + k) * own
        out[at : at + own] = ref[pl.ds(pl.multiple_of(other * own, own), own), :]


def weight_kernel(w_ref, out_ref, scr):
    chans_sq, width = w_ref.shape
    chans = int(round(chans_sq**0.5))
    scr[...] = w_ref[...].astype(jnp.float32)
    pairs = chans // 2
    fold = LANES // chans
    order = [side * pairs + pair for pair in range(pairs) for side in range(2)]
    for tile in range(chans // fold):
        piece = jnp.concatenate(
            [scr[pl.ds(e, chans, stride=chans), :] for e in order[tile * fold : (tile + 1) * fold]], axis=0
        )
        out_ref[:, tile * LANES : (tile + 1) * LANES] = piece.T.astype(jnp.bfloat16)


def pair_kernel(dims, total, offset_ref, w_ref, right_ref, left_ref, *refs):
    n_res, n_col, n_seq, chans = dims
    out_ref, left_scr, outer_scr = refs[-3], refs[-2], refs[-1]
    ins = refs[:-3]
    z_ins = ins[: n_res - 1]
    x_ins = ins[n_res - 1 : n_res - 1 + (n_col - 1) * n_res]
    s_ins = ins[n_res - 1 + (n_col - 1) * n_res :]
    n_right = right_ref.shape[0]
    part = left_ref.shape[0] // n_res
    own = part // n_seq
    me = lax.axis_index("seq")
    half = LANES // 2
    fold = LANES // chans
    pairs = chans // 2
    rows_dev = out_ref.shape[1]
    turns = rows_dev // fold
    n_s = own // turns

    start = pl.multiple_of(lax.axis_index("res") * part + me * own, own)
    mine = pl.multiple_of(me * own, own)
    rights = [(right_ref, 0)] + [(ref, 0) for ref in z_ins]
    lefts = [[(left_ref, start)] + [(ref, pl.multiple_of(n_right + mine, own)) for ref in z_ins]]
    for u in range(n_col - 1):
        lefts.append([(x_ins[u * n_res + k], mine) for k in range(n_res)])
    for ref in s_ins:
        rights += [(ref, k * n_right) for k in range(n_res)]
        base = n_res * n_right
        for u in range(n_col):
            lefts[u] += [(ref, base + (u * n_res + k) * own) for k in range(n_res)]

    for u in range(n_col):
        slabs = [ref[pl.ds(at, own), :].astype(jnp.float32) for ref, at in lefts[u]]
        for turn in range(turns):
            column = jnp.concatenate([slab[turn * n_s : (turn + 1) * n_s] for slab in slabs], axis=0)
            depth = column.shape[0]
            left_scr[u * LANES : (u + 1) * LANES, turn * depth : (turn + 1) * depth] = column.T.astype(jnp.bfloat16)

    n_blocks = n_right // (pairs * n_s)
    offset = offset_ref[...]
    col = lax.axis_index("col")

    def block_of_columns(block):
        at_block = block * pairs * n_s
        slabs = [ref[pl.ds(at + at_block, pairs * n_s), :].astype(jnp.float32) for ref, at in rights]
        left = left_scr[...]
        for pair in range(pairs):
            here = jnp.concatenate([slab[pair * n_s : (pair + 1) * n_s] for slab in slabs], axis=0)
            there = pltpu.roll(here, half, 1)
            low = lane_index(here.shape) < half
            weights = jnp.concatenate(
                [
                    jnp.concatenate([jnp.where(low, here, 0.0), jnp.where(low, 0.0, there)], axis=0),
                    jnp.concatenate([jnp.where(low, there, 0.0), jnp.where(low, 0.0, here)], axis=0),
                ],
                axis=1,
            ).astype(jnp.bfloat16)
            outer = jnp.dot(left, weights, preferred_element_type=jnp.float32).astype(jnp.bfloat16)
            for side in range(2):
                at = (2 * pair + side) * chans
                for tile in range(n_col * fold):
                    outer_scr[at : at + chans, tile * LANES : (tile + 1) * LANES] = outer[
                        tile * chans : (tile + 1) * chans, side * LANES : (side + 1) * LANES
                    ]
        for u in range(n_col):
            summed = jnp.dot(
                w_ref[...],
                outer_scr[:, u * fold * LANES : (u + 1) * fold * LANES],
                preferred_element_type=jnp.float32,
            )
            to = partner(col, u, n_col) if n_col & (n_col - 1) == 0 else (col - u + n_col) % n_col
            for residue in range(fold):
                piece = summed[:, residue * LANES : (residue + 1) * LANES].T
                piece = (piece / total + offset).astype(jnp.bfloat16)
                for turn in range(turns):
                    out_ref[to, turn * fold + residue, pl.ds(block * half, half), :] = piece[
                        turn * half : (turn + 1) * half
                    ]

    if n_blocks == 1:
        block_of_columns(0)
    else:
        pl.loop(0, n_blocks)(block_of_columns)


def per_device(alignment, scale, shift, w1, b1, w2, b2, w_final, offset):
    n_s, span, width = alignment.shape
    n_res, n_col, n_seq = lax.axis_size("res"), lax.axis_size("col"), lax.axis_size("seq")
    chans, pair_width = w1.shape[1], w_final.shape[1]
    bf16 = jnp.bfloat16
    n_right = span * chans * n_s // LANES
    n_left = span * chans * n_s // LANES
    part = n_left // n_res
    own = part // n_seq
    rows_dev = span // (n_res * n_seq)
    slab = jax.ShapeDtypeStruct((n_right, LANES), bf16)
    z_slab = jax.ShapeDtypeStruct((n_right + part, LANES), bf16)
    x_slab = jax.ShapeDtypeStruct((part, LANES), bf16)
    n_x = (n_col - 1) * n_res
    dims = (n_res, n_col, n_seq)
    params = functools.partial(pltpu.CompilerParams, vmem_limit_bytes=32 * 1024 * 1024)

    made = pl.pallas_call(
        functools.partial(project_kernel, dims + (chans,)),
        out_shape=[slab, slab] + [z_slab] * (n_res - 1) + [x_slab] * n_x,
        in_specs=[VMEM] * 7,
        out_specs=[VMEM] * (2 + n_res - 1 + n_x),
        scratch_shapes=[
            pltpu.VMEM((n_s * span, LANES), jnp.float32),
            pltpu.VMEM((n_left, LANES), jnp.float32),
            pltpu.VMEM((n_right, LANES), jnp.float32),
        ],
        compiler_params=params(),
        name="project",
    )(alignment, scale.reshape(1, -1), shift.reshape(1, -1), w1, b1.reshape(1, -1), w2, b2.reshape(1, -1))
    right, left = made[0], made[1]

    def to_chip(array, step_col, step_res):
        pairs = []
        for r in range(n_res):
            for c in range(n_col):
                to = partner(r, step_res, n_res) * n_col + partner(c, step_col, n_col)
                pairs.append((r * n_col + c, to))
        return lax.ppermute(array, ("res", "col"), pairs)

    z_in = [to_chip(made[2 + k], 0, k + 1) for k in range(n_res - 1)]
    x_in = [to_chip(made[1 + n_res + k], 1 + k // n_res, k % n_res) for k in range(n_x)]

    weights = pl.pallas_call(
        weight_kernel,
        out_shape=jax.ShapeDtypeStruct((pair_width, chans * chans), bf16),
        in_specs=[VMEM],
        out_specs=VMEM,
        scratch_shapes=[pltpu.VMEM((chans * chans, pair_width), jnp.float32)],
        compiler_params=params(),
        name="weights",
    )(w_final)

    s_in = []
    for step in range(1, n_seq):
        packed = pl.pallas_call(
            functools.partial(pack_kernel, dims + (step,)),
            out_shape=jax.ShapeDtypeStruct((n_res * n_right + n_res * n_col * own, LANES), bf16),
            in_specs=[VMEM] * (2 + len(z_in) + len(x_in)),
            out_specs=VMEM,
            compiler_params=params(),
            name="pack",
        )(right, left, *z_in, *x_in)
        s_in.append(lax.ppermute(packed, "seq", [(q, partner(q, step, n_seq)) for q in range(n_seq)]))

    turns = rows_dev * chans // LANES
    depth = turns * n_s * n_res * n_seq
    return pl.pallas_call(
        functools.partial(pair_kernel, dims + (chans,), float(n_s * n_res * n_seq)),
        out_shape=jax.ShapeDtypeStruct((n_col, rows_dev, span, pair_width), bf16),
        in_specs=[VMEM] * (4 + len(z_in) + len(x_in) + len(s_in)),
        out_specs=VMEM,
        scratch_shapes=[
            pltpu.VMEM((n_col * LANES, depth), bf16),
            pltpu.VMEM((chans * chans, n_col * (LANES // chans) * LANES), bf16),
        ],
        compiler_params=params(),
        name="pair",
    )(offset.reshape(1, -1), weights, right, left, *z_in, *x_in, *s_in)


def solution(mesh):
    return jax.shard_map(
        per_device,
        mesh=mesh,
        in_specs=(P(("groups", "res", "seq"), "col", None), P(), P(), P(), P(), P(), P(), P(), P()),
        out_specs=P("groups", ("res", "seq"), "col", None),
        check_vma=False,
    )
```

```python
import functools

import jax
import jax.numpy as jnp
from jax import lax
from jax.experimental import pallas as pl
from jax.experimental.pallas import tpu as pltpu
from jax.sharding import PartitionSpec as P

LANES = 128
SUBLANES = 8
VMEM = pl.BlockSpec(memory_space=pltpu.VMEM)
ANY = pl.BlockSpec(memory_space=pl.ANY)
ACROSS = (((1,), (1,)), ((), ()))


def partner(index, step, size):
    return index ^ step if size & (size - 1) == 0 else (index + step) % size


def lane_index(shape):
    return lax.broadcasted_iota(jnp.int32, shape, len(shape) - 1)


def project_kernel(dims, *refs):
    n_res, n_col, _, _ = dims
    n_in = 7
    sources, outs, scratch = refs[:n_in], refs[n_in : -n_in - 4], refs[-n_in - 4 :]
    landed, (rows_scr, lane_scr, right_scr, sems) = scratch[:n_in], scratch[n_in:]
    copies = [pltpu.make_async_copy(a, b, sems.at[i]) for i, (a, b) in enumerate(zip(sources, landed))]
    for copy in copies:
        copy.start()
    for copy in copies:
        copy.wait()
    x_ref, scale_ref, shift_ref, w1_ref, b1_ref, w2_ref, b2_ref = landed
    right_out, left_out = outs[0], outs[1]
    z_outs = outs[2 : 2 + n_res - 1]
    x_outs = outs[2 + n_res - 1 :]
    n_s, span, width = x_ref.shape
    chans = w1_ref.shape[0]
    fold = LANES // chans
    half = LANES // 2
    x = x_ref[...].reshape(n_s * span, width).astype(jnp.float32)
    mean = jnp.mean(x, axis=-1, keepdims=True)
    centred = x - mean
    variance = jnp.mean(centred * centred, axis=-1, keepdims=True)
    normed = (centred * lax.rsqrt(variance + 1e-05) * scale_ref[...] + shift_ref[...]).astype(jnp.bfloat16)

    w1 = jnp.concatenate([w1_ref[...]] * fold, axis=0)
    b1 = jnp.concatenate([b1_ref[...]] * fold, axis=1)
    rows_scr[...] = lax.dot_general(normed, w1, ACROSS, preferred_element_type=jnp.float32) + b1
    n_rows = n_s * span // fold
    owner = lane_index((n_rows, LANES)) // chans
    merged = rows_scr[pl.ds(0, n_rows, stride=fold), :]
    for turn in range(1, fold):
        merged = jnp.where(owner == turn, rows_scr[pl.ds(turn, n_rows, stride=fold), :], merged)
    groups = span // fold
    for s in range(n_s):
        lane_scr[pl.ds(s, groups, stride=n_s), :] = merged[s * groups : (s + 1) * groups]
    left_out[...] = lane_scr[...].astype(jnp.bfloat16)

    eye = lax.broadcasted_iota(jnp.int32, (chans, chans), 0) == lane_index((chans, chans))
    b2 = jnp.sum(jnp.where(eye, b2_ref[...], 0.0), axis=1, keepdims=True)
    right = lax.dot_general(w2_ref[...], normed, ACROSS, preferred_element_type=jnp.float32) + b2
    pairs = chans // 2
    low = lane_index((pairs, LANES)) < half
    blocks = span // half
    for tile in range(n_s * span // LANES):
        here = right[:, tile * LANES : (tile + 1) * LANES]
        there = pltpu.roll(here, half, 1)
        for side in range(2):
            s, block = divmod(2 * tile + side, blocks)
            first, second = (here, there) if side == 0 else (there, here)
            right_scr[pl.ds(block * pairs * n_s + s, pairs, stride=n_s), :] = jnp.where(
                low, first[:pairs], second[pairs:]
            )
    right_slab = right_scr[...].astype(jnp.bfloat16)
    right_out[...] = right_slab

    here = lax.axis_index("res")
    n_right = right_slab.shape[0]
    part = left_out.shape[0] // n_res
    for k, out in enumerate(z_outs):
        out[:n_right] = right_slab
        out[n_right:] = left_out[pl.ds(pl.multiple_of(partner(here, k + 1, n_res) * part, part), part), :]
    for k, out in enumerate(x_outs):
        out[...] = left_out[pl.ds(pl.multiple_of(partner(here, k % n_res, n_res) * part, part), part), :]


def pack_kernel(dims, right_ref, left_ref, *refs):
    n_res, n_col, n_seq, step = dims
    ins, out = refs[:-1], refs[-1]
    z_ins, x_ins = ins[: n_res - 1], ins[n_res - 1 :]
    n_right = right_ref.shape[0]
    part = left_ref.shape[0] // n_res
    own = part // n_seq
    other = partner(lax.axis_index("seq"), step, n_seq)
    out[:n_right] = right_ref[...]
    for k, ref in enumerate(z_ins):
        out[(k + 1) * n_right : (k + 2) * n_right] = ref[:n_right]
    base = n_res * n_right
    start = pl.multiple_of(lax.axis_index("res") * part + other * own, own)
    out[base : base + own] = left_ref[pl.ds(start, own), :]
    for k, ref in enumerate(z_ins):
        at = base + (k + 1) * own
        out[at : at + own] = ref[pl.ds(pl.multiple_of(n_right + other * own, own), own), :]
    for k, ref in enumerate(x_ins):
        at = base + (n_res + k) * own
        out[at : at + own] = ref[pl.ds(pl.multiple_of(other * own, own), own), :]


def weight_kernel(w_ref, out_ref, scr):
    chans_sq, width = w_ref.shape
    chans = int(round(chans_sq**0.5))
    scr[...] = w_ref[...].astype(jnp.float32)
    pairs = chans // 2
    fold = LANES // chans
    order = [side * pairs + pair for pair in range(pairs) for side in range(2)]
    for tile in range(chans // fold):
        piece = jnp.concatenate(
            [scr[pl.ds(e, chans, stride=chans), :] for e in order[tile * fold : (tile + 1) * fold]], axis=0
        )
        out_ref[:, tile * LANES : (tile + 1) * LANES] = piece.T.astype(jnp.bfloat16)


def pair_kernel(dims, total, offset_ref, w_ref, right_ref, left_ref, *refs):
    n_res, n_col, n_seq, chans = dims
    out_ref, left_scr, outer_scr = refs[-3], refs[-2], refs[-1]
    ins = refs[:-3]
    z_ins = ins[: n_res - 1]
    x_ins = ins[n_res - 1 : n_res - 1 + (n_col - 1) * n_res]
    s_ins = ins[n_res - 1 + (n_col - 1) * n_res :]
    n_right = right_ref.shape[0]
    part = left_ref.shape[0] // n_res
    own = part // n_seq
    me = lax.axis_index("seq")
    half = LANES // 2
    fold = LANES // chans
    pairs = chans // 2
    rows_dev = out_ref.shape[1]
    turns = rows_dev // fold
    n_s = own // turns

    start = pl.multiple_of(lax.axis_index("res") * part + me * own, own)
    mine = pl.multiple_of(me * own, own)
    rights = [(right_ref, 0)] + [(ref, 0) for ref in z_ins]
    lefts = [[(left_ref, start)] + [(ref, pl.multiple_of(n_right + mine, own)) for ref in z_ins]]
    for u in range(n_col - 1):
        lefts.append([(x_ins[u * n_res + k], mine) for k in range(n_res)])
    for ref in s_ins:
        rights += [(ref, k * n_right) for k in range(n_res)]
        base = n_res * n_right
        for u in range(n_col):
            lefts[u] += [(ref, base + (u * n_res + k) * own) for k in range(n_res)]

    for u in range(n_col):
        slabs = [ref[pl.ds(at, own), :].astype(jnp.float32) for ref, at in lefts[u]]
        for turn in range(turns):
            column = jnp.concatenate([slab[turn * n_s : (turn + 1) * n_s] for slab in slabs], axis=0)
            depth = column.shape[0]
            left_scr[u * LANES : (u + 1) * LANES, turn * depth : (turn + 1) * depth] = column.T.astype(jnp.bfloat16)

    n_blocks = n_right // (pairs * n_s)
    offset = offset_ref[...]
    col = lax.axis_index("col")

    def block_of_columns(block):
        at_block = block * pairs * n_s
        slabs = [ref[pl.ds(at + at_block, pairs * n_s), :].astype(jnp.float32) for ref, at in rights]
        left = left_scr[...]
        for pair in range(pairs):
            here = jnp.concatenate([slab[pair * n_s : (pair + 1) * n_s] for slab in slabs], axis=0)
            there = pltpu.roll(here, half, 1)
            low = lane_index(here.shape) < half
            weights = jnp.concatenate(
                [
                    jnp.concatenate([jnp.where(low, here, 0.0), jnp.where(low, 0.0, there)], axis=0),
                    jnp.concatenate([jnp.where(low, there, 0.0), jnp.where(low, 0.0, here)], axis=0),
                ],
                axis=1,
            ).astype(jnp.bfloat16)
            outer = jnp.dot(left, weights, preferred_element_type=jnp.float32).astype(jnp.bfloat16)
            for side in range(2):
                at = (2 * pair + side) * chans
                for tile in range(n_col * fold):
                    outer_scr[at : at + chans, tile * LANES : (tile + 1) * LANES] = outer[
                        tile * chans : (tile + 1) * chans, side * LANES : (side + 1) * LANES
                    ]
        for u in range(n_col):
            summed = jnp.dot(
                w_ref[...],
                outer_scr[:, u * fold * LANES : (u + 1) * fold * LANES],
                preferred_element_type=jnp.float32,
            )
            to = partner(col, u, n_col) if n_col & (n_col - 1) == 0 else (col - u + n_col) % n_col
            for residue in range(fold):
                piece = summed[:, residue * LANES : (residue + 1) * LANES].T
                piece = (piece / total + offset).astype(jnp.bfloat16)
                for turn in range(turns):
                    out_ref[to, turn * fold + residue, pl.ds(block * half, half), :] = piece[
                        turn * half : (turn + 1) * half
                    ]

    if n_blocks == 1:
        block_of_columns(0)
    else:
        pl.loop(0, n_blocks)(block_of_columns)


def per_device(alignment, scale, shift, w1, b1, w2, b2, w_final, offset):
    n_s, span, width = alignment.shape
    n_res, n_col, n_seq = lax.axis_size("res"), lax.axis_size("col"), lax.axis_size("seq")
    chans, pair_width = w1.shape[1], w_final.shape[1]
    bf16 = jnp.bfloat16
    n_right = span * chans * n_s // LANES
    n_left = span * chans * n_s // LANES
    part = n_left // n_res
    own = part // n_seq
    rows_dev = span // (n_res * n_seq)
    slab = jax.ShapeDtypeStruct((n_right, LANES), bf16)
    z_slab = jax.ShapeDtypeStruct((n_right + part, LANES), bf16)
    x_slab = jax.ShapeDtypeStruct((part, LANES), bf16)
    n_x = (n_col - 1) * n_res
    dims = (n_res, n_col, n_seq)
    params = functools.partial(pltpu.CompilerParams, vmem_limit_bytes=32 * 1024 * 1024)

    taken = (alignment, scale.reshape(1, -1), shift.reshape(1, -1), w1.T, b1.reshape(1, -1), w2.T, b2.reshape(1, -1))
    made = pl.pallas_call(
        functools.partial(project_kernel, dims + (chans,)),
        out_shape=[slab, slab] + [z_slab] * (n_res - 1) + [x_slab] * n_x,
        in_specs=[ANY] * len(taken),
        out_specs=[VMEM] * (2 + n_res - 1 + n_x),
        scratch_shapes=[pltpu.VMEM(a.shape, a.dtype) for a in taken]
        + [
            pltpu.VMEM((n_s * span, LANES), jnp.float32),
            pltpu.VMEM((n_left, LANES), jnp.float32),
            pltpu.VMEM((n_right, LANES), jnp.float32),
            pltpu.SemaphoreType.DMA((len(taken),)),
        ],
        compiler_params=params(),
        name="project",
    )(*taken)
    right, left = made[0], made[1]

    def to_chip(array, step_col, step_res):
        pairs = []
        for r in range(n_res):
            for c in range(n_col):
                to = partner(r, step_res, n_res) * n_col + partner(c, step_col, n_col)
                pairs.append((r * n_col + c, to))
        return lax.ppermute(array, ("res", "col"), pairs)

    z_in = [to_chip(made[2 + k], 0, k + 1) for k in range(n_res - 1)]
    x_in = [to_chip(made[1 + n_res + k], 1 + k // n_res, k % n_res) for k in range(n_x)]

    weights = pl.pallas_call(
        weight_kernel,
        out_shape=jax.ShapeDtypeStruct((pair_width, chans * chans), bf16),
        in_specs=[VMEM],
        out_specs=VMEM,
        scratch_shapes=[pltpu.VMEM((chans * chans, pair_width), jnp.float32)],
        compiler_params=params(),
        name="weights",
    )(w_final)

    s_in = []
    for step in range(1, n_seq):
        packed = pl.pallas_call(
            functools.partial(pack_kernel, dims + (step,)),
            out_shape=jax.ShapeDtypeStruct((n_res * n_right + n_res * n_col * own, LANES), bf16),
            in_specs=[VMEM] * (2 + len(z_in) + len(x_in)),
            out_specs=VMEM,
            compiler_params=params(),
            name="pack",
        )(right, left, *z_in, *x_in)
        s_in.append(lax.ppermute(packed, "seq", [(q, partner(q, step, n_seq)) for q in range(n_seq)]))

    turns = rows_dev * chans // LANES
    depth = turns * n_s * n_res * n_seq
    return pl.pallas_call(
        functools.partial(pair_kernel, dims + (chans,), float(n_s * n_res * n_seq)),
        out_shape=jax.ShapeDtypeStruct((n_col, rows_dev, span, pair_width), bf16),
        in_specs=[VMEM] * (4 + len(z_in) + len(x_in) + len(s_in)),
        out_specs=VMEM,
        scratch_shapes=[
            pltpu.VMEM((n_col * LANES, depth), bf16),
            pltpu.VMEM((chans * chans, n_col * (LANES // chans) * LANES), bf16),
        ],
        compiler_params=params(),
        name="pair",
    )(offset.reshape(1, -1), weights, right, left, *z_in, *x_in, *s_in)


def solution(mesh):
    return jax.shard_map(
        per_device,
        mesh=mesh,
        in_specs=(P(("groups", "res", "seq"), "col", None), P(), P(), P(), P(), P(), P(), P(), P()),
        out_specs=P("groups", ("res", "seq"), "col", None),
        check_vma=False,
    )
```

```python
import functools

import jax
import jax.numpy as jnp
from jax import lax
from jax.experimental import pallas as pl
from jax.experimental.pallas import tpu as pltpu
from jax.sharding import PartitionSpec as P

LANES = 128
SUBLANES = 8
VMEM = pl.BlockSpec(memory_space=pltpu.VMEM)
HBM = pl.BlockSpec(memory_space=pltpu.HBM)
ACROSS = (((1,), (1,)), ((), ()))


def partner(index, step, size):
    return index ^ step if size & (size - 1) == 0 else (index + step) % size


def lane_index(shape):
    return lax.broadcasted_iota(jnp.int32, shape, len(shape) - 1)


def project_kernel(dims, *refs):
    n_res, n_col, _, _ = dims
    n_in = 7
    sources, outs, scratch = refs[:n_in], refs[n_in : -n_in - 4], refs[-n_in - 4 :]
    landed, (rows_scr, lane_scr, right_scr, sems) = scratch[:n_in], scratch[n_in:]
    copies = [pltpu.make_async_copy(a, b, sems.at[i]) for i, (a, b) in enumerate(zip(sources, landed))]
    for copy in copies:
        copy.start()
    for copy in copies:
        copy.wait()
    x_ref, scale_ref, shift_ref, w1_ref, b1_ref, w2_ref, b2_ref = landed
    right_out, left_out = outs[0], outs[1]
    z_outs = outs[2 : 2 + n_res - 1]
    x_outs = outs[2 + n_res - 1 :]
    n_s, span, width = x_ref.shape
    chans = w1_ref.shape[0]
    fold = LANES // chans
    half = LANES // 2
    x = x_ref[...].reshape(n_s * span, width).astype(jnp.float32)
    mean = jnp.mean(x, axis=-1, keepdims=True)
    centred = x - mean
    variance = jnp.mean(centred * centred, axis=-1, keepdims=True)
    normed = (centred * lax.rsqrt(variance + 1e-05) * scale_ref[...] + shift_ref[...]).astype(jnp.bfloat16)

    w1 = jnp.concatenate([w1_ref[...]] * fold, axis=0)
    b1 = jnp.concatenate([b1_ref[...]] * fold, axis=1)
    rows_scr[...] = lax.dot_general(normed, w1, ACROSS, preferred_element_type=jnp.float32) + b1
    n_rows = n_s * span // fold
    owner = lane_index((n_rows, LANES)) // chans
    merged = rows_scr[pl.ds(0, n_rows, stride=fold), :]
    for turn in range(1, fold):
        merged = jnp.where(owner == turn, rows_scr[pl.ds(turn, n_rows, stride=fold), :], merged)
    groups = span // fold
    for s in range(n_s):
        lane_scr[pl.ds(s, groups, stride=n_s), :] = merged[s * groups : (s + 1) * groups]
    left_out[...] = lane_scr[...].astype(jnp.bfloat16)

    eye = lax.broadcasted_iota(jnp.int32, (chans, chans), 0) == lane_index((chans, chans))
    b2 = jnp.sum(jnp.where(eye, b2_ref[...], 0.0), axis=1, keepdims=True)
    right = lax.dot_general(w2_ref[...], normed, ACROSS, preferred_element_type=jnp.float32) + b2
    pairs = chans // 2
    low = lane_index((pairs, LANES)) < half
    blocks = span // half
    for tile in range(n_s * span // LANES):
        here = right[:, tile * LANES : (tile + 1) * LANES]
        there = pltpu.roll(here, half, 1)
        for side in range(2):
            s, block = divmod(2 * tile + side, blocks)
            first, second = (here, there) if side == 0 else (there, here)
            right_scr[pl.ds(block * pairs * n_s + s, pairs, stride=n_s), :] = jnp.where(
                low, first[:pairs], second[pairs:]
            )
    right_slab = right_scr[...].astype(jnp.bfloat16)
    right_out[...] = right_slab

    here = lax.axis_index("res")
    n_right = right_slab.shape[0]
    part = left_out.shape[0] // n_res
    for k, out in enumerate(z_outs):
        out[:n_right] = right_slab
        out[n_right:] = left_out[pl.ds(pl.multiple_of(partner(here, k + 1, n_res) * part, part), part), :]
    for k, out in enumerate(x_outs):
        out[...] = left_out[pl.ds(pl.multiple_of(partner(here, k % n_res, n_res) * part, part), part), :]


def pack_kernel(dims, right_ref, left_ref, *refs):
    n_res, n_col, n_seq, step = dims
    ins, out = refs[:-1], refs[-1]
    z_ins, x_ins = ins[: n_res - 1], ins[n_res - 1 :]
    n_right = right_ref.shape[0]
    part = left_ref.shape[0] // n_res
    own = part // n_seq
    other = partner(lax.axis_index("seq"), step, n_seq)
    out[:n_right] = right_ref[...]
    for k, ref in enumerate(z_ins):
        out[(k + 1) * n_right : (k + 2) * n_right] = ref[:n_right]
    base = n_res * n_right
    start = pl.multiple_of(lax.axis_index("res") * part + other * own, own)
    out[base : base + own] = left_ref[pl.ds(start, own), :]
    for k, ref in enumerate(z_ins):
        at = base + (k + 1) * own
        out[at : at + own] = ref[pl.ds(pl.multiple_of(n_right + other * own, own), own), :]
    for k, ref in enumerate(x_ins):
        at = base + (n_res + k) * own
        out[at : at + own] = ref[pl.ds(pl.multiple_of(other * own, own), own), :]


def weight_kernel(w_ref, out_ref, scr):
    chans_sq, width = w_ref.shape
    chans = int(round(chans_sq**0.5))
    scr[...] = w_ref[...].astype(jnp.float32)
    pairs = chans // 2
    fold = LANES // chans
    order = [side * pairs + pair for pair in range(pairs) for side in range(2)]
    for tile in range(chans // fold):
        piece = jnp.concatenate(
            [scr[pl.ds(e, chans, stride=chans), :] for e in order[tile * fold : (tile + 1) * fold]], axis=0
        )
        out_ref[:, tile * LANES : (tile + 1) * LANES] = piece.T.astype(jnp.bfloat16)


def pair_kernel(dims, total, offset_ref, w_ref, right_ref, left_ref, *refs):
    n_res, n_col, n_seq, chans = dims
    out_ref, left_scr, outer_scr = refs[-3], refs[-2], refs[-1]
    ins = refs[:-3]
    z_ins = ins[: n_res - 1]
    x_ins = ins[n_res - 1 : n_res - 1 + (n_col - 1) * n_res]
    s_ins = ins[n_res - 1 + (n_col - 1) * n_res :]
    n_right = right_ref.shape[0]
    part = left_ref.shape[0] // n_res
    own = part // n_seq
    me = lax.axis_index("seq")
    half = LANES // 2
    fold = LANES // chans
    pairs = chans // 2
    rows_dev = out_ref.shape[1]
    turns = rows_dev // fold
    n_s = own // turns

    start = pl.multiple_of(lax.axis_index("res") * part + me * own, own)
    mine = pl.multiple_of(me * own, own)
    rights = [(right_ref, 0)] + [(ref, 0) for ref in z_ins]
    lefts = [[(left_ref, start)] + [(ref, pl.multiple_of(n_right + mine, own)) for ref in z_ins]]
    for u in range(n_col - 1):
        lefts.append([(x_ins[u * n_res + k], mine) for k in range(n_res)])
    for ref in s_ins:
        rights += [(ref, k * n_right) for k in range(n_res)]
        base = n_res * n_right
        for u in range(n_col):
            lefts[u] += [(ref, base + (u * n_res + k) * own) for k in range(n_res)]

    for u in range(n_col):
        slabs = [ref[pl.ds(at, own), :].astype(jnp.float32) for ref, at in lefts[u]]
        for turn in range(turns):
            column = jnp.concatenate([slab[turn * n_s : (turn + 1) * n_s] for slab in slabs], axis=0)
            depth = column.shape[0]
            left_scr[u * LANES : (u + 1) * LANES, turn * depth : (turn + 1) * depth] = column.T.astype(jnp.bfloat16)

    n_blocks = n_right // (pairs * n_s)
    offset = offset_ref[...]
    col = lax.axis_index("col")

    def block_of_columns(block):
        at_block = block * pairs * n_s
        slabs = [ref[pl.ds(at + at_block, pairs * n_s), :].astype(jnp.float32) for ref, at in rights]
        left = left_scr[...]
        for pair in range(pairs):
            here = jnp.concatenate([slab[pair * n_s : (pair + 1) * n_s] for slab in slabs], axis=0)
            there = pltpu.roll(here, half, 1)
            low = lane_index(here.shape) < half
            weights = jnp.concatenate(
                [
                    jnp.concatenate([jnp.where(low, here, 0.0), jnp.where(low, 0.0, there)], axis=0),
                    jnp.concatenate([jnp.where(low, there, 0.0), jnp.where(low, 0.0, here)], axis=0),
                ],
                axis=1,
            ).astype(jnp.bfloat16)
            outer = jnp.dot(left, weights, preferred_element_type=jnp.float32).astype(jnp.bfloat16)
            for side in range(2):
                at = (2 * pair + side) * chans
                for tile in range(n_col * fold):
                    outer_scr[at : at + chans, tile * LANES : (tile + 1) * LANES] = outer[
                        tile * chans : (tile + 1) * chans, side * LANES : (side + 1) * LANES
                    ]
        for u in range(n_col):
            summed = jnp.dot(
                w_ref[...],
                outer_scr[:, u * fold * LANES : (u + 1) * fold * LANES],
                preferred_element_type=jnp.float32,
            )
            to = partner(col, u, n_col) if n_col & (n_col - 1) == 0 else (col - u + n_col) % n_col
            for residue in range(fold):
                piece = summed[:, residue * LANES : (residue + 1) * LANES].T
                piece = (piece / total + offset).astype(jnp.bfloat16)
                for turn in range(turns):
                    out_ref[to, turn * fold + residue, pl.ds(block * half, half), :] = piece[
                        turn * half : (turn + 1) * half
                    ]

    if n_blocks == 1:
        block_of_columns(0)
    else:
        pl.loop(0, n_blocks)(block_of_columns)


def per_device(alignment, scale, shift, w1, b1, w2, b2, w_final, offset):
    n_s, span, width = alignment.shape
    n_res, n_col, n_seq = lax.axis_size("res"), lax.axis_size("col"), lax.axis_size("seq")
    chans, pair_width = w1.shape[1], w_final.shape[1]
    bf16 = jnp.bfloat16
    n_right = span * chans * n_s // LANES
    n_left = span * chans * n_s // LANES
    part = n_left // n_res
    own = part // n_seq
    rows_dev = span // (n_res * n_seq)
    slab = jax.ShapeDtypeStruct((n_right, LANES), bf16)
    z_slab = jax.ShapeDtypeStruct((n_right + part, LANES), bf16)
    x_slab = jax.ShapeDtypeStruct((part, LANES), bf16)
    n_x = (n_col - 1) * n_res
    dims = (n_res, n_col, n_seq)
    params = functools.partial(pltpu.CompilerParams, vmem_limit_bytes=32 * 1024 * 1024)

    taken = (alignment, scale.reshape(1, -1), shift.reshape(1, -1), w1.T, b1.reshape(1, -1), w2.T, b2.reshape(1, -1))
    made = pl.pallas_call(
        functools.partial(project_kernel, dims + (chans,)),
        out_shape=[slab, slab] + [z_slab] * (n_res - 1) + [x_slab] * n_x,
        in_specs=[HBM] * len(taken),
        out_specs=[VMEM] * (2 + n_res - 1 + n_x),
        scratch_shapes=[pltpu.VMEM(a.shape, a.dtype) for a in taken]
        + [
            pltpu.VMEM((n_s * span, LANES), jnp.float32),
            pltpu.VMEM((n_left, LANES), jnp.float32),
            pltpu.VMEM((n_right, LANES), jnp.float32),
            pltpu.SemaphoreType.DMA((len(taken),)),
        ],
        compiler_params=params(),
        name="project",
    )(*[pltpu.with_memory_space_constraint(a, pltpu.HBM) for a in taken])
    right, left = made[0], made[1]

    def to_chip(array, step_col, step_res):
        pairs = []
        for r in range(n_res):
            for c in range(n_col):
                to = partner(r, step_res, n_res) * n_col + partner(c, step_col, n_col)
                pairs.append((r * n_col + c, to))
        return lax.ppermute(array, ("res", "col"), pairs)

    z_in = [to_chip(made[2 + k], 0, k + 1) for k in range(n_res - 1)]
    x_in = [to_chip(made[1 + n_res + k], 1 + k // n_res, k % n_res) for k in range(n_x)]

    weights = pl.pallas_call(
        weight_kernel,
        out_shape=jax.ShapeDtypeStruct((pair_width, chans * chans), bf16),
        in_specs=[VMEM],
        out_specs=VMEM,
        scratch_shapes=[pltpu.VMEM((chans * chans, pair_width), jnp.float32)],
        compiler_params=params(),
        name="weights",
    )(w_final)

    s_in = []
    for step in range(1, n_seq):
        packed = pl.pallas_call(
            functools.partial(pack_kernel, dims + (step,)),
            out_shape=jax.ShapeDtypeStruct((n_res * n_right + n_res * n_col * own, LANES), bf16),
            in_specs=[VMEM] * (2 + len(z_in) + len(x_in)),
            out_specs=VMEM,
            compiler_params=params(),
            name="pack",
        )(right, left, *z_in, *x_in)
        s_in.append(lax.ppermute(packed, "seq", [(q, partner(q, step, n_seq)) for q in range(n_seq)]))

    turns = rows_dev * chans // LANES
    depth = turns * n_s * n_res * n_seq
    return pl.pallas_call(
        functools.partial(pair_kernel, dims + (chans,), float(n_s * n_res * n_seq)),
        out_shape=jax.ShapeDtypeStruct((n_col, rows_dev, span, pair_width), bf16),
        in_specs=[VMEM] * (4 + len(z_in) + len(x_in) + len(s_in)),
        out_specs=VMEM,
        scratch_shapes=[
            pltpu.VMEM((n_col * LANES, depth), bf16),
            pltpu.VMEM((chans * chans, n_col * (LANES // chans) * LANES), bf16),
        ],
        compiler_params=params(),
        name="pair",
    )(offset.reshape(1, -1), weights, right, left, *z_in, *x_in, *s_in)


def solution(mesh):
    return jax.shard_map(
        per_device,
        mesh=mesh,
        in_specs=(P(("groups", "res", "seq"), "col", None), P(), P(), P(), P(), P(), P(), P(), P()),
        out_specs=P("groups", ("res", "seq"), "col", None),
        check_vma=False,
    )
```

```python
import functools

import jax
import jax.numpy as jnp
from jax import lax
from jax.experimental import pallas as pl
from jax.experimental.pallas import tpu as pltpu
from jax.sharding import PartitionSpec as P

LANES = 128
SUBLANES = 8
VMEM = pl.BlockSpec(memory_space=pltpu.VMEM)
HBM = pl.BlockSpec(memory_space=pltpu.HBM)
ACROSS = (((1,), (1,)), ((), ()))


def partner(index, step, size):
    return index ^ step if size & (size - 1) == 0 else (index + step) % size


def lane_index(shape):
    return lax.broadcasted_iota(jnp.int32, shape, len(shape) - 1)


def project_kernel(n_res, solo, *refs):
    n_in = 7
    sources, outs, scratch = refs[:n_in], refs[n_in : -n_in - 4], refs[-n_in - 4 :]
    landed, (rows_scr, lane_scr, right_scr, sems) = scratch[:n_in], scratch[n_in:]
    copies = [pltpu.make_async_copy(a, b, sems.at[i]) for i, (a, b) in enumerate(zip(sources, landed))]
    for copy in copies:
        copy.start()
    for copy in copies:
        copy.wait()
    x_ref, scale_ref, shift_ref, w1_ref, b1_ref, w2_ref, b2_ref = landed
    slab_out, solo_out = outs
    n_s, span, width = x_ref.shape
    chans = w1_ref.shape[0]
    fold = LANES // chans
    half = LANES // 2
    x = x_ref[...].reshape(n_s * span, width).astype(jnp.float32)
    mean = jnp.mean(x, axis=-1, keepdims=True)
    centred = x - mean
    variance = jnp.mean(centred * centred, axis=-1, keepdims=True)
    normed = (centred * lax.rsqrt(variance + 1e-05) * scale_ref[...] + shift_ref[...]).astype(jnp.bfloat16)

    w1 = jnp.concatenate([w1_ref[...]] * fold, axis=0)
    b1 = jnp.concatenate([b1_ref[...]] * fold, axis=1)
    rows_scr[...] = lax.dot_general(normed, w1, ACROSS, preferred_element_type=jnp.float32) + b1
    n_rows = n_s * span // fold
    owner = lane_index((n_rows, LANES)) // chans
    merged = rows_scr[pl.ds(0, n_rows, stride=fold), :]
    for turn in range(1, fold):
        merged = jnp.where(owner == turn, rows_scr[pl.ds(turn, n_rows, stride=fold), :], merged)
    groups = span // fold
    for s in range(n_s):
        lane_scr[pl.ds(s, groups, stride=n_s), :] = merged[s * groups : (s + 1) * groups]

    eye = lax.broadcasted_iota(jnp.int32, (chans, chans), 0) == lane_index((chans, chans))
    b2 = jnp.sum(jnp.where(eye, b2_ref[...], 0.0), axis=1, keepdims=True)
    right = lax.dot_general(w2_ref[...], normed, ACROSS, preferred_element_type=jnp.float32) + b2
    pairs = chans // 2
    low = lane_index((pairs, LANES)) < half
    blocks = span // half
    for tile in range(n_s * span // LANES):
        here = right[:, tile * LANES : (tile + 1) * LANES]
        there = pltpu.roll(here, half, 1)
        for side in range(2):
            s, block = divmod(2 * tile + side, blocks)
            first, second = (here, there) if side == 0 else (there, here)
            right_scr[pl.ds(block * pairs * n_s + s, pairs, stride=n_s), :] = jnp.where(
                low, first[:pairs], second[pairs:]
            )
    right_slab = right_scr[...].astype(jnp.bfloat16)
    n_right, n_left = right_scr.shape[0], lane_scr.shape[0]
    part = n_left // n_res
    slab_out[:n_right] = right_slab
    slab_out[n_right:] = lane_scr[...].astype(jnp.bfloat16)
    to = partner(lax.axis_index("res"), solo, n_res)
    solo_out[:n_right] = right_slab
    solo_out[n_right:] = lane_scr[pl.ds(pl.multiple_of(to * part, part), part), :].astype(jnp.bfloat16)


def chip_kernel(n_res, steps, own_ref, other_ref, *outs):
    n_right = own_ref.shape[0] // 2
    part = n_right // n_res
    me, here = lax.axis_index("seq"), lax.axis_index("res")
    for (first, second), out in zip(steps, outs):
        to = partner(here, jnp.where(me == 0, first, second), n_res)
        start = pl.multiple_of(n_right + to * part, part)
        at = out.shape[0] - 2 * part
        if at:
            out[:n_right] = own_ref[:n_right]
            out[n_right:at] = other_ref[:n_right]
        out[at : at + part] = own_ref[pl.ds(start, part), :]
        out[at + part :] = other_ref[pl.ds(start, part), :]


def core_kernel(parts, part, own, *refs):
    ins, out = refs[:-1], refs[-1]
    mine = pl.multiple_of((1 - lax.axis_index("seq")) * own, own)
    at = 0
    for ref, n_parts in zip(ins, parts):
        body = ref.shape[0] - n_parts * part
        if body:
            out[at : at + body] = ref[:body]
            at += body
        for k in range(n_parts):
            out[at : at + own] = ref[pl.ds(pl.multiple_of(body + k * part + mine, own), own), :]
            at += own


def weight_kernel(w_ref, out_ref, scr):
    chans_sq, width = w_ref.shape
    chans = int(round(chans_sq**0.5))
    scr[...] = w_ref[...].astype(jnp.float32)
    pairs = chans // 2
    fold = LANES // chans
    order = [side * pairs + pair for pair in range(pairs) for side in range(2)]
    for tile in range(chans // fold):
        piece = jnp.concatenate(
            [scr[pl.ds(e, chans, stride=chans), :] for e in order[tile * fold : (tile + 1) * fold]], axis=0
        )
        out_ref[:, tile * LANES : (tile + 1) * LANES] = piece.T.astype(jnp.bfloat16)


def pair_kernel(plan, total, offset_ref, w_ref, *refs):
    out_ref, left_scr, outer_scr = refs[-3], refs[-2], refs[-1]
    n_col, chans, part, own = plan["n_col"], plan["chans"], plan["part"], plan["own"]
    n_right = part * plan["n_res"]
    me = lax.axis_index("seq")
    half = LANES // 2
    fold = LANES // chans
    pairs = chans // 2
    rows_dev = out_ref.shape[1]
    turns = rows_dev // fold
    n_s = own // turns

    own_ref, other_ref, solo_ref = refs[:3]
    n_pairs = plan["n_pairs"]
    b_refs = refs[3 : 3 + n_pairs]
    x_refs = refs[3 + n_pairs : 3 + n_pairs + (n_col - 1) * (n_pairs + 1)]
    z_other, x_other = refs[3 + n_pairs + (n_col - 1) * (n_pairs + 1) : -3]
    mine = pl.multiple_of(me * own, own)

    def rows_of(ref, at):
        return ref[pl.ds(at, own), :].astype(jnp.float32)

    start = pl.multiple_of(n_right + lax.axis_index("res") * part + mine, own)
    rights = [(own_ref, 0), (other_ref, 0), (solo_ref, 0), (z_other, 0)]
    lefts = [[rows_of(own_ref, start), rows_of(other_ref, start)]]
    lefts[0] += [rows_of(solo_ref, pl.multiple_of(n_right + mine, own)), rows_of(z_other, n_right)]
    for k, ref in enumerate(b_refs):
        at = n_right + own + k * 2 * (n_right + own)
        rights += [(ref, 0), (ref, n_right), (z_other, at + n_right), (z_other, at)]
        lefts[0] += [rows_of(ref, pl.multiple_of(2 * n_right + h * part + mine, own)) for h in range(2)]
        lefts[0] += [rows_of(z_other, at + 2 * n_right + (1 - h) * own) for h in range(2)]
    for u in range(n_col - 1):
        chunks = []
        for k in range(n_pairs + 1):
            place = u * (n_pairs + 1) + k
            heard = [rows_of(x_refs[place], pl.multiple_of(h * part + mine, own)) for h in range(2)]
            told = [rows_of(x_other, (2 * place + 1 - h) * own) for h in range(2)]
            if k < n_pairs:
                chunks += heard + told
            else:
                near = [jnp.where(me == 0, a, b) for a, b in zip(heard, told)]
                far = [jnp.where(me == 0, b, a) for a, b in zip(heard, told)]
                chunks = near + far + chunks
        lefts.append(chunks)

    for u in range(n_col):
        for turn in range(turns):
            column = jnp.concatenate([slab[turn * n_s : (turn + 1) * n_s] for slab in lefts[u]], axis=0)
            depth = column.shape[0]
            left_scr[u * LANES : (u + 1) * LANES, turn * depth : (turn + 1) * depth] = column.T.astype(jnp.bfloat16)

    n_blocks = n_right // (pairs * n_s)
    offset = offset_ref[...]
    col = lax.axis_index("col")

    def block_of_columns(block):
        at_block = block * pairs * n_s
        slabs = [ref[pl.ds(at + at_block, pairs * n_s), :].astype(jnp.float32) for ref, at in rights]
        left = left_scr[...]
        for pair in range(pairs):
            here = jnp.concatenate([slab[pair * n_s : (pair + 1) * n_s] for slab in slabs], axis=0)
            there = pltpu.roll(here, half, 1)
            low = lane_index(here.shape) < half
            weights = jnp.concatenate(
                [
                    jnp.concatenate([jnp.where(low, here, 0.0), jnp.where(low, 0.0, there)], axis=0),
                    jnp.concatenate([jnp.where(low, there, 0.0), jnp.where(low, 0.0, here)], axis=0),
                ],
                axis=1,
            ).astype(jnp.bfloat16)
            outer = jnp.dot(left, weights, preferred_element_type=jnp.float32).astype(jnp.bfloat16)
            for side in range(2):
                at = (2 * pair + side) * chans
                for tile in range(n_col * fold):
                    outer_scr[at : at + chans, tile * LANES : (tile + 1) * LANES] = outer[
                        tile * chans : (tile + 1) * chans, side * LANES : (side + 1) * LANES
                    ]
        for u in range(n_col):
            summed = jnp.dot(
                w_ref[...],
                outer_scr[:, u * fold * LANES : (u + 1) * fold * LANES],
                preferred_element_type=jnp.float32,
            )
            to = partner(col, u, n_col) if n_col & (n_col - 1) == 0 else (col - u + n_col) % n_col
            for residue in range(fold):
                piece = summed[:, residue * LANES : (residue + 1) * LANES].T
                piece = (piece / total + offset).astype(jnp.bfloat16)
                for turn in range(turns):
                    out_ref[to, turn * fold + residue, pl.ds(block * half, half), :] = piece[
                        turn * half : (turn + 1) * half
                    ]

    if n_blocks == 1:
        block_of_columns(0)
    else:
        pl.loop(0, n_blocks)(block_of_columns)


def per_device(alignment, scale, shift, w1, b1, w2, b2, w_final, offset):
    n_s, span, width = alignment.shape
    n_res, n_col, n_seq = lax.axis_size("res"), lax.axis_size("col"), lax.axis_size("seq")
    chans, pair_width = w1.shape[1], w_final.shape[1]
    bf16 = jnp.bfloat16
    n_right = span * chans * n_s // LANES
    n_left = span * chans * n_s // LANES
    part = n_left // n_res
    own = part // n_seq
    rows_dev = span // (n_res * n_seq)
    params = pltpu.CompilerParams(vmem_limit_bytes=32 * 1024 * 1024)

    def rows(n):
        return jax.ShapeDtypeStruct((n, LANES), bf16)

    solo = n_res - 1
    pairs = [(k, k + 1) for k in range(1, solo, 2)]

    taken = (alignment, scale.reshape(1, -1), shift.reshape(1, -1), w1.T, b1.reshape(1, -1), w2.T, b2.reshape(1, -1))
    slab, solo_out = pl.pallas_call(
        functools.partial(project_kernel, n_res, solo),
        out_shape=[rows(n_right + n_left), rows(n_right + part)],
        in_specs=[HBM] * len(taken),
        out_specs=[VMEM] * 2,
        scratch_shapes=[pltpu.VMEM(a.shape, a.dtype) for a in taken]
        + [
            pltpu.VMEM((n_s * span, LANES), jnp.float32),
            pltpu.VMEM((n_left, LANES), jnp.float32),
            pltpu.VMEM((n_right, LANES), jnp.float32),
            pltpu.SemaphoreType.DMA((len(taken),)),
        ],
        compiler_params=params,
        name="project",
    )(*[pltpu.with_memory_space_constraint(a, pltpu.HBM) for a in taken])

    def to_core(array):
        return lax.ppermute(array, "seq", [(q, 1 - q) for q in range(n_seq)])

    def to_chip(array, step_col, steps):
        route = []
        for r in range(n_res):
            for c in range(n_col):
                for q in range(n_seq):
                    to = partner(r, steps[q], n_res) * n_col + partner(c, step_col, n_col)
                    route.append(((r * n_col + c) * n_seq + q, to * n_seq + q))
        return lax.ppermute(array, ("res", "col", "seq"), route)

    slab_in = to_core(slab)
    solo_in = to_chip(solo_out, 0, (solo, solo))
    sends = [(0, steps) for steps in pairs]
    sends += [(u, steps) for u in range(1, n_col) for steps in pairs + [(0, solo)]]
    messages = pl.pallas_call(
        functools.partial(chip_kernel, n_res, [steps for _, steps in sends]),
        out_shape=[rows(2 * part + (0 if u else 2 * n_right)) for u, _ in sends],
        in_specs=[VMEM] * 2,
        out_specs=[VMEM] * len(sends),
        compiler_params=params,
        name="chip",
    )(slab, slab_in)
    heard = [to_chip(message, u, steps) for message, (u, steps) in zip(messages, sends)]

    weights = pl.pallas_call(
        weight_kernel,
        out_shape=jax.ShapeDtypeStruct((pair_width, chans * chans), bf16),
        in_specs=[VMEM],
        out_specs=VMEM,
        scratch_shapes=[pltpu.VMEM((chans * chans, pair_width), jnp.float32)],
        compiler_params=params,
        name="weights",
    )(w_final)

    def share(arrays, parts, n_rows):
        packed = pl.pallas_call(
            functools.partial(core_kernel, parts, part, own),
            out_shape=rows(n_rows),
            in_specs=[VMEM] * len(arrays),
            out_specs=VMEM,
            compiler_params=params,
            name="core",
        )(*arrays)
        return to_core(packed)

    z_in, x_in = heard[: len(pairs)], heard[len(pairs) :]
    z_other = share([solo_in] + z_in, [1] + [2] * len(z_in), (2 * len(pairs) + 1) * (n_right + own))
    x_other = share(x_in, [2] * len(x_in), 2 * own * len(x_in))

    turns = rows_dev * chans // LANES
    depth = turns * n_s * n_res * n_seq
    plan = dict(n_res=n_res, n_col=n_col, chans=chans, part=part, own=own, n_pairs=len(pairs))
    operands = (offset.reshape(1, -1), weights, slab, slab_in, solo_in, *heard, z_other, x_other)
    return pl.pallas_call(
        functools.partial(pair_kernel, plan, float(n_s * n_res * n_seq)),
        out_shape=jax.ShapeDtypeStruct((n_col, rows_dev, span, pair_width), bf16),
        in_specs=[VMEM] * len(operands),
        out_specs=VMEM,
        scratch_shapes=[
            pltpu.VMEM((n_col * LANES, depth), bf16),
            pltpu.VMEM((chans * chans, n_col * (LANES // chans) * LANES), bf16),
        ],
        compiler_params=params,
        name="pair",
    )(*operands)


def solution(mesh):
    return jax.shard_map(
        per_device,
        mesh=mesh,
        in_specs=(P(("groups", "res", "seq"), "col", None), P(), P(), P(), P(), P(), P(), P(), P()),
        out_specs=P("groups", ("res", "seq"), "col", None),
        check_vma=False,
    )
```

```python
import functools

import jax
import jax.numpy as jnp
from jax import lax
from jax.experimental import pallas as pl
from jax.experimental.pallas import tpu as pltpu
from jax.sharding import PartitionSpec as P

LANES = 128
SUBLANES = 8
VMEM = pl.BlockSpec(memory_space=pltpu.VMEM)
HBM = pl.BlockSpec(memory_space=pltpu.HBM)
ACROSS = (((1,), (1,)), ((), ()))


def partner(index, step, size):
    return index ^ step if size & (size - 1) == 0 else (index + step) % size


def lane_index(shape):
    return lax.broadcasted_iota(jnp.int32, shape, len(shape) - 1)


def project_kernel(n_res, steps, *refs):
    n_in = 7
    sources, (slab_out, *z_outs), scratch = refs[:n_in], refs[n_in : -n_in - 4], refs[-n_in - 4 :]
    landed, (rows_scr, lane_scr, right_scr, sems) = scratch[:n_in], scratch[n_in:]
    copies = [pltpu.make_async_copy(a, b, sems.at[i]) for i, (a, b) in enumerate(zip(sources, landed))]
    for copy in copies:
        copy.start()
    for copy in copies:
        copy.wait()
    x_ref, scale_ref, shift_ref, w1_ref, b1_ref, w2_ref, b2_ref = landed
    n_s, span, width = x_ref.shape
    chans = w1_ref.shape[0]
    fold = LANES // chans
    half = LANES // 2
    x = x_ref[...].reshape(n_s * span, width).astype(jnp.float32)
    mean = jnp.mean(x, axis=-1, keepdims=True)
    centred = x - mean
    variance = jnp.mean(centred * centred, axis=-1, keepdims=True)
    normed = (centred * lax.rsqrt(variance + 1e-05) * scale_ref[...] + shift_ref[...]).astype(jnp.bfloat16)

    w1 = jnp.concatenate([w1_ref[...]] * fold, axis=0)
    b1 = jnp.concatenate([b1_ref[...]] * fold, axis=1)
    rows_scr[...] = lax.dot_general(normed, w1, ACROSS, preferred_element_type=jnp.float32) + b1
    n_rows = n_s * span // fold
    owner = lane_index((n_rows, LANES)) // chans
    merged = rows_scr[pl.ds(0, n_rows, stride=fold), :]
    for turn in range(1, fold):
        merged = jnp.where(owner == turn, rows_scr[pl.ds(turn, n_rows, stride=fold), :], merged)
    groups = span // fold
    for s in range(n_s):
        lane_scr[pl.ds(s, groups, stride=n_s), :] = merged[s * groups : (s + 1) * groups]

    eye = lax.broadcasted_iota(jnp.int32, (chans, chans), 0) == lane_index((chans, chans))
    b2 = jnp.sum(jnp.where(eye, b2_ref[...], 0.0), axis=1, keepdims=True)
    right = lax.dot_general(w2_ref[...], normed, ACROSS, preferred_element_type=jnp.float32) + b2
    pairs = chans // 2
    low = lane_index((pairs, LANES)) < half
    blocks = span // half
    for tile in range(n_s * span // LANES):
        here = right[:, tile * LANES : (tile + 1) * LANES]
        there = pltpu.roll(here, half, 1)
        for side in range(2):
            s, block = divmod(2 * tile + side, blocks)
            first, second = (here, there) if side == 0 else (there, here)
            right_scr[pl.ds(block * pairs * n_s + s, pairs, stride=n_s), :] = jnp.where(
                low, first[:pairs], second[pairs:]
            )
    right_slab = right_scr[...].astype(jnp.bfloat16)
    n_right, n_left = right_scr.shape[0], lane_scr.shape[0]
    part = n_left // n_res
    slab_out[:n_right] = right_slab
    slab_out[n_right:] = lane_scr[...].astype(jnp.bfloat16)
    for step, out in zip(steps, z_outs):
        to = partner(lax.axis_index("res"), step, n_res)
        out[:n_right] = right_slab
        out[n_right:] = lane_scr[pl.ds(pl.multiple_of(to * part, part), part), :].astype(jnp.bfloat16)


def chip_kernel(n_res, steps, own_ref, other_ref, *outs):
    n_right = own_ref.shape[0] // 2
    part = n_right // n_res
    me, here = lax.axis_index("seq"), lax.axis_index("res")
    for (first, second), out in zip(steps, outs):
        to = partner(here, jnp.where(me == 0, first, second), n_res)
        start = pl.multiple_of(n_right + to * part, part)
        out[:part] = own_ref[pl.ds(start, part), :]
        out[part:] = other_ref[pl.ds(start, part), :]


def core_kernel(n_z, part, own, *refs):
    ins, out = refs[:-1], refs[-1]
    mine = (1 - lax.axis_index("seq")) * own
    at = 0
    for k, ref in enumerate(ins):
        body = ref.shape[0] - part if k < n_z else 0
        if body:
            out[at : at + body] = ref[:body]
            at += body
        for start in range(body, ref.shape[0], part):
            out[at : at + own] = ref[pl.ds(pl.multiple_of(start + mine, own), own), :]
            at += own


def weight_kernel(w_ref, out_ref, scr):
    chans_sq, width = w_ref.shape
    chans = int(round(chans_sq**0.5))
    scr[...] = w_ref[...].astype(jnp.float32)
    pairs = chans // 2
    fold = LANES // chans
    order = [side * pairs + pair for pair in range(pairs) for side in range(2)]
    for tile in range(chans // fold):
        piece = jnp.concatenate(
            [scr[pl.ds(e, chans, stride=chans), :] for e in order[tile * fold : (tile + 1) * fold]], axis=0
        )
        out_ref[:, tile * LANES : (tile + 1) * LANES] = piece.T.astype(jnp.bfloat16)


def pair_kernel(plan, total, offset_ref, w_ref, *refs):
    out_ref, left_scr, outer_scr = refs[-3], refs[-2], refs[-1]
    n_col, chans, part, own = plan["n_col"], plan["chans"], plan["part"], plan["own"]
    n_res, pairs_of = plan["n_res"], plan["pairs"]
    n_right = part * n_res
    me = lax.axis_index("seq")
    half = LANES // 2
    fold = LANES // chans
    pairs = chans // 2
    rows_dev = out_ref.shape[1]
    turns = rows_dev // fold
    n_s = own // turns

    own_ref, other_ref = refs[:2]
    z_refs = refs[2 : 1 + n_res]
    x_refs = refs[1 + n_res : 1 + n_res + (n_col - 1) * len(pairs_of)]
    other_in = refs[-4]
    mine = pl.multiple_of(me * own, own)

    def rows_of(ref, at):
        return ref[pl.ds(at, own), :].astype(jnp.float32)

    start = pl.multiple_of(n_right + lax.axis_index("res") * part + mine, own)
    rights = [(own_ref, 0), (other_ref, 0)]
    lefts = [[rows_of(own_ref, start), rows_of(other_ref, start)]]
    for k, ref in enumerate(z_refs):
        at = k * (n_right + own)
        rights += [(ref, 0), (other_in, at)]
        lefts[0] += [rows_of(ref, pl.multiple_of(n_right + mine, own)), rows_of(other_in, at + n_right)]
    for u in range(n_col - 1):
        chunks = [None] * n_res
        for k, (first, second) in enumerate(pairs_of):
            place = u * len(pairs_of) + k
            at = (n_res - 1) * (n_right + own) + 2 * place * own
            heard = [rows_of(x_refs[place], pl.multiple_of(h * part + mine, own)) for h in range(2)]
            told = [rows_of(other_in, at + (1 - h) * own) for h in range(2)]
            chunks[first] = [jnp.where(me == 0, a, b) for a, b in zip(heard, told)]
            chunks[second] = [jnp.where(me == 0, b, a) for a, b in zip(heard, told)]
        order = [0] + plan["z_steps"]
        lefts.append([slab for step in order for slab in chunks[step]])

    for u in range(n_col):
        for turn in range(turns):
            column = jnp.concatenate([slab[turn * n_s : (turn + 1) * n_s] for slab in lefts[u]], axis=0)
            depth = column.shape[0]
            left_scr[u * LANES : (u + 1) * LANES, turn * depth : (turn + 1) * depth] = column.T.astype(jnp.bfloat16)

    n_blocks = n_right // (pairs * n_s)
    offset = offset_ref[...]
    col = lax.axis_index("col")

    def block_of_columns(block):
        at_block = block * pairs * n_s
        slabs = [ref[pl.ds(at + at_block, pairs * n_s), :].astype(jnp.float32) for ref, at in rights]
        left = left_scr[...]
        for pair in range(pairs):
            here = jnp.concatenate([slab[pair * n_s : (pair + 1) * n_s] for slab in slabs], axis=0)
            there = pltpu.roll(here, half, 1)
            low = lane_index(here.shape) < half
            weights = jnp.concatenate(
                [
                    jnp.concatenate([jnp.where(low, here, 0.0), jnp.where(low, 0.0, there)], axis=0),
                    jnp.concatenate([jnp.where(low, there, 0.0), jnp.where(low, 0.0, here)], axis=0),
                ],
                axis=1,
            ).astype(jnp.bfloat16)
            outer = jnp.dot(left, weights, preferred_element_type=jnp.float32).astype(jnp.bfloat16)
            for side in range(2):
                at = (2 * pair + side) * chans
                for tile in range(n_col * fold):
                    outer_scr[at : at + chans, tile * LANES : (tile + 1) * LANES] = outer[
                        tile * chans : (tile + 1) * chans, side * LANES : (side + 1) * LANES
                    ]
        for u in range(n_col):
            summed = jnp.dot(
                w_ref[...],
                outer_scr[:, u * fold * LANES : (u + 1) * fold * LANES],
                preferred_element_type=jnp.float32,
            )
            to = partner(col, u, n_col) if n_col & (n_col - 1) == 0 else (col - u + n_col) % n_col
            for residue in range(fold):
                piece = summed[:, residue * LANES : (residue + 1) * LANES].T
                piece = (piece / total + offset).astype(jnp.bfloat16)
                for turn in range(turns):
                    out_ref[to, turn * fold + residue, pl.ds(block * half, half), :] = piece[
                        turn * half : (turn + 1) * half
                    ]

    if n_blocks == 1:
        block_of_columns(0)
    else:
        pl.loop(0, n_blocks)(block_of_columns)


def per_device(alignment, scale, shift, w1, b1, w2, b2, w_final, offset):
    n_s, span, width = alignment.shape
    n_res, n_col, n_seq = lax.axis_size("res"), lax.axis_size("col"), lax.axis_size("seq")
    chans, pair_width = w1.shape[1], w_final.shape[1]
    bf16 = jnp.bfloat16
    n_right = span * chans * n_s // LANES
    n_left = span * chans * n_s // LANES
    part = n_left // n_res
    own = part // n_seq
    rows_dev = span // (n_res * n_seq)
    params = pltpu.CompilerParams(vmem_limit_bytes=32 * 1024 * 1024)

    def rows(n):
        return jax.ShapeDtypeStruct((n, LANES), bf16)

    z_steps = [k for k in range(1, n_res) if k > 1] + [1] * (n_res > 1)
    pairs = [(k, k + 1) for k in range(1, n_res - 1, 2)] + [(0, n_res - 1)]

    taken = (alignment, scale.reshape(1, -1), shift.reshape(1, -1), w1.T, b1.reshape(1, -1), w2.T, b2.reshape(1, -1))
    slab, *z_out = pl.pallas_call(
        functools.partial(project_kernel, n_res, z_steps),
        out_shape=[rows(n_right + n_left)] + [rows(n_right + part)] * len(z_steps),
        in_specs=[HBM] * len(taken),
        out_specs=[VMEM] * n_res,
        scratch_shapes=[pltpu.VMEM(a.shape, a.dtype) for a in taken]
        + [
            pltpu.VMEM((n_s * span, LANES), jnp.float32),
            pltpu.VMEM((n_left, LANES), jnp.float32),
            pltpu.VMEM((n_right, LANES), jnp.float32),
            pltpu.SemaphoreType.DMA((len(taken),)),
        ],
        compiler_params=params,
        name="project",
    )(*[pltpu.with_memory_space_constraint(a, pltpu.HBM) for a in taken])

    def to_core(array):
        return lax.ppermute(array, "seq", [(q, 1 - q) for q in range(n_seq)])

    def to_chip(array, step_col, steps):
        route = []
        for r in range(n_res):
            for c in range(n_col):
                for q in range(n_seq):
                    to = partner(r, steps[q], n_res) * n_col + partner(c, step_col, n_col)
                    route.append(((r * n_col + c) * n_seq + q, to * n_seq + q))
        return lax.ppermute(array, ("res", "col", "seq"), route)

    slab_in = to_core(slab)
    z_in = [to_chip(array, 0, (step, step)) for array, step in zip(z_out, z_steps)]
    sends = [(u, steps) for u in range(1, n_col) for steps in pairs]
    messages = pl.pallas_call(
        functools.partial(chip_kernel, n_res, [steps for _, steps in sends]),
        out_shape=[rows(2 * part)] * len(sends),
        in_specs=[VMEM] * 2,
        out_specs=[VMEM] * len(sends),
        compiler_params=params,
        name="chip",
    )(slab, slab_in)
    x_in = [to_chip(message, u, steps) for message, (u, steps) in zip(messages, sends)]

    weights = pl.pallas_call(
        weight_kernel,
        out_shape=jax.ShapeDtypeStruct((pair_width, chans * chans), bf16),
        in_specs=[VMEM],
        out_specs=VMEM,
        scratch_shapes=[pltpu.VMEM((chans * chans, pair_width), jnp.float32)],
        compiler_params=params,
        name="weights",
    )(w_final)

    def share(n_z, arrays):
        packed = pl.pallas_call(
            functools.partial(core_kernel, n_z, part, own),
            out_shape=rows(n_z * (n_right + own) + (len(arrays) - n_z) * 2 * own),
            in_specs=[VMEM] * len(arrays),
            out_specs=VMEM,
            compiler_params=params,
            name="core",
        )(*arrays)
        return to_core(packed)

    other_in = share(len(z_in), z_in + x_in)

    turns = rows_dev * chans // LANES
    depth = turns * n_s * n_res * n_seq
    plan = dict(n_res=n_res, n_col=n_col, chans=chans, part=part, own=own, pairs=pairs, z_steps=z_steps)
    operands = (offset.reshape(1, -1), weights, slab, slab_in, *z_in, *x_in, other_in)
    return pl.pallas_call(
        functools.partial(pair_kernel, plan, float(n_s * n_res * n_seq)),
        out_shape=jax.ShapeDtypeStruct((n_col, rows_dev, span, pair_width), bf16),
        in_specs=[VMEM] * len(operands),
        out_specs=VMEM,
        scratch_shapes=[
            pltpu.VMEM((n_col * LANES, depth), bf16),
            pltpu.VMEM((chans * chans, n_col * (LANES // chans) * LANES), bf16),
        ],
        compiler_params=params,
        name="pair",
    )(*operands)


def solution(mesh):
    return jax.shard_map(
        per_device,
        mesh=mesh,
        in_specs=(P(("groups", "res", "seq"), "col", None), P(), P(), P(), P(), P(), P(), P(), P()),
        out_specs=P("groups", ("res", "seq"), "col", None),
        check_vma=False,
    )
```

```python
import functools

import jax
import jax.numpy as jnp
from jax import lax
from jax.experimental import pallas as pl
from jax.experimental.pallas import tpu as pltpu
from jax.sharding import PartitionSpec as P

LANES = 128
SUBLANES = 8
VMEM = pl.BlockSpec(memory_space=pltpu.VMEM)
HBM = pl.BlockSpec(memory_space=pltpu.HBM)
ACROSS = (((1,), (1,)), ((), ()))


def partner(index, step, size):
    return index ^ step if size & (size - 1) == 0 else (index + step) % size


def lane_index(shape):
    return lax.broadcasted_iota(jnp.int32, shape, len(shape) - 1)


def project_kernel(n_res, steps, *refs):
    n_in = 7
    sources, (slab_out, *z_outs), scratch = refs[:n_in], refs[n_in : -n_in - 4], refs[-n_in - 4 :]
    landed, (rows_scr, lane_scr, right_scr, sems) = scratch[:n_in], scratch[n_in:]
    copies = [pltpu.make_async_copy(a, b, sems.at[i]) for i, (a, b) in enumerate(zip(sources, landed))]
    for copy in copies:
        copy.start()
    for copy in copies:
        copy.wait()
    x_ref, scale_ref, shift_ref, w1_ref, b1_ref, w2_ref, b2_ref = landed
    n_s, span, width = x_ref.shape
    chans = w1_ref.shape[0]
    fold = LANES // chans
    half = LANES // 2
    x = x_ref[...].reshape(n_s * span, width).astype(jnp.float32)
    mean = jnp.mean(x, axis=-1, keepdims=True)
    centred = x - mean
    variance = jnp.mean(centred * centred, axis=-1, keepdims=True)
    normed = (centred * lax.rsqrt(variance + 1e-05) * scale_ref[...] + shift_ref[...]).astype(jnp.bfloat16)

    w1 = jnp.concatenate([w1_ref[...]] * fold, axis=0)
    b1 = jnp.concatenate([b1_ref[...]] * fold, axis=1)
    rows_scr[...] = lax.dot_general(normed, w1, ACROSS, preferred_element_type=jnp.float32) + b1
    n_rows = n_s * span // fold
    owner = lane_index((n_rows, LANES)) // chans
    merged = rows_scr[pl.ds(0, n_rows, stride=fold), :]
    for turn in range(1, fold):
        merged = jnp.where(owner == turn, rows_scr[pl.ds(turn, n_rows, stride=fold), :], merged)
    groups = span // fold
    for s in range(n_s):
        lane_scr[pl.ds(s, groups, stride=n_s), :] = merged[s * groups : (s + 1) * groups]

    eye = lax.broadcasted_iota(jnp.int32, (chans, chans), 0) == lane_index((chans, chans))
    b2 = jnp.sum(jnp.where(eye, b2_ref[...], 0.0), axis=1, keepdims=True)
    right = lax.dot_general(w2_ref[...], normed, ACROSS, preferred_element_type=jnp.float32) + b2
    pairs = chans // 2
    low = lane_index((pairs, LANES)) < half
    blocks = span // half
    for tile in range(n_s * span // LANES):
        here = right[:, tile * LANES : (tile + 1) * LANES]
        there = pltpu.roll(here, half, 1)
        for side in range(2):
            s, block = divmod(2 * tile + side, blocks)
            first, second = (here, there) if side == 0 else (there, here)
            right_scr[pl.ds(block * pairs * n_s + s, pairs, stride=n_s), :] = jnp.where(
                low, first[:pairs], second[pairs:]
            )
    right_slab = right_scr[...].astype(jnp.bfloat16)
    n_right, n_left = right_scr.shape[0], lane_scr.shape[0]
    part = n_left // n_res
    slab_out[:n_right] = right_slab
    slab_out[n_right:] = lane_scr[...].astype(jnp.bfloat16)
    for step, out in zip(steps, z_outs):
        to = partner(lax.axis_index("res"), step, n_res)
        out[:n_right] = right_slab
        out[n_right:] = lane_scr[pl.ds(pl.multiple_of(to * part, part), part), :].astype(jnp.bfloat16)


def chip_kernel(n_res, steps, own_ref, other_ref, *outs):
    n_right = own_ref.shape[0] // 2
    part = n_right // n_res
    me, here = lax.axis_index("seq"), lax.axis_index("res")
    for (first, second), out in zip(steps, outs):
        to = partner(here, jnp.where(me == 0, first, second), n_res)
        start = pl.multiple_of(n_right + to * part, part)
        out[:part] = own_ref[pl.ds(start, part), :]
        out[part:] = other_ref[pl.ds(start, part), :]


def core_kernel(n_rights, part, own, *refs):
    ins, out = refs[:-1], refs[-1]
    mine = (1 - lax.axis_index("seq")) * own
    at = 0
    for ref in ins:
        if n_rights:
            out[at : at + n_rights] = ref[:n_rights]
            at += n_rights
        for start in range(n_rights, ref.shape[0], part):
            out[at : at + own] = ref[pl.ds(pl.multiple_of(start + mine, own), own), :]
            at += own


def weight_kernel(w_ref, out_ref, scr):
    chans_sq, width = w_ref.shape
    chans = int(round(chans_sq**0.5))
    scr[...] = w_ref[...].astype(jnp.float32)
    pairs = chans // 2
    fold = LANES // chans
    order = [side * pairs + pair for pair in range(pairs) for side in range(2)]
    for tile in range(chans // fold):
        piece = jnp.concatenate(
            [scr[pl.ds(e, chans, stride=chans), :] for e in order[tile * fold : (tile + 1) * fold]], axis=0
        )
        out_ref[:, tile * LANES : (tile + 1) * LANES] = piece.T.astype(jnp.bfloat16)


def fill_left(left_scr, u, slabs, n_s):
    turns = slabs[0].shape[0] // n_s
    for turn in range(turns):
        column = jnp.concatenate([slab[turn * n_s : (turn + 1) * n_s] for slab in slabs], axis=0)
        depth = column.shape[0]
        left_scr[u * LANES : (u + 1) * LANES, turn * depth : (turn + 1) * depth] = column.T.astype(jnp.bfloat16)


def loop_blocks(n_blocks, body):
    if n_blocks == 1:
        body(0)
    else:
        pl.loop(0, n_blocks)(body)


def update_block(plan, block, u_base, offset, w_ref, weight_of, left_scr, outer_scr, staged):
    chans, total = plan["chans"], plan["total"]
    half = LANES // 2
    fold = LANES // chans
    left = left_scr[...]
    n_u = left.shape[0] // LANES
    for pair in range(chans // 2):
        outer = jnp.dot(left, weight_of(pair), preferred_element_type=jnp.float32).astype(jnp.bfloat16)
        for side in range(2):
            at = (2 * pair + side) * chans
            for tile in range(n_u * fold):
                outer_scr[at : at + chans, tile * LANES : (tile + 1) * LANES] = outer[
                    tile * chans : (tile + 1) * chans, side * LANES : (side + 1) * LANES
                ]
    for u in range(n_u):
        summed = jnp.dot(
            w_ref[...], outer_scr[:, u * fold * LANES : (u + 1) * fold * LANES], preferred_element_type=jnp.float32
        )
        for residue in range(fold):
            piece = summed[:, residue * LANES : (residue + 1) * LANES].T
            piece = (piece / total + offset).astype(jnp.bfloat16)
            for turn in range(LANES // half):
                staged[u, turn * fold + residue, pl.ds(block * half, half), :] = piece[
                    turn * half : (turn + 1) * half
                ]


def write_out(plan, u_base, staged, out_ref, sems):
    n_col = plan["n_col"]
    col = lax.axis_index("col")
    copies = []
    for u in range(staged.shape[0]):
        step = u_base + u
        source = partner(col, step, n_col) if n_col & (n_col - 1) == 0 else (col - step + n_col) % n_col
        copies.append(pltpu.make_async_copy(staged.at[u], out_ref.at[source], sems.at[u]))
    for copy in copies:
        copy.start()
    for copy in copies:
        copy.wait()


def near_kernel(plan, offset_ref, w_ref, own_ref, other_ref, *refs):
    z_refs, (other_in, out_ref, weights_out, left_scr, outer_scr, staged, sems) = refs[:-7], refs[-7:]
    chans, part, own, n_s = plan["chans"], plan["part"], plan["own"], plan["n_s"]
    n_right = part * plan["n_res"]
    half = LANES // 2
    pairs = chans // 2
    mine = pl.multiple_of(lax.axis_index("seq") * own, own)

    def rows_of(ref, at):
        return ref[pl.ds(at, own), :].astype(jnp.float32)

    start = pl.multiple_of(n_right + lax.axis_index("res") * part + mine, own)
    rights = [(own_ref, 0), (other_ref, 0)]
    lefts = [rows_of(own_ref, start), rows_of(other_ref, start)]
    for k, ref in enumerate(z_refs):
        at = k * (n_right + own)
        rights += [(ref, 0), (other_in, at)]
        lefts += [rows_of(ref, pl.multiple_of(n_right + mine, own)), rows_of(other_in, at + n_right)]
    fill_left(left_scr, 0, lefts, n_s)
    depth = left_scr.shape[1]
    offset = offset_ref[...]

    def block_of_columns(block):
        at_block = block * pairs * n_s
        slabs = [ref[pl.ds(at + at_block, pairs * n_s), :].astype(jnp.float32) for ref, at in rights]

        def weight_of(pair):
            here = jnp.concatenate([slab[pair * n_s : (pair + 1) * n_s] for slab in slabs], axis=0)
            there = pltpu.roll(here, half, 1)
            low = lane_index(here.shape) < half
            weights = jnp.concatenate(
                [
                    jnp.concatenate([jnp.where(low, here, 0.0), jnp.where(low, 0.0, there)], axis=0),
                    jnp.concatenate([jnp.where(low, there, 0.0), jnp.where(low, 0.0, here)], axis=0),
                ],
                axis=1,
            ).astype(jnp.bfloat16)
            weights_out[pl.ds((block * pairs + pair) * depth, depth), :] = weights
            return weights

        update_block(plan, block, 0, offset, w_ref, weight_of, left_scr, outer_scr, staged)

    loop_blocks(n_right // (pairs * n_s), block_of_columns)
    write_out(plan, 0, staged, out_ref, sems)


def far_kernel(plan, offset_ref, w_ref, weights_ref, *refs):
    x_refs, (other_in, _, out_ref, left_scr, outer_scr, staged, sems) = refs[:-7], refs[-7:]
    chans, part, own, n_s, n_res = plan["chans"], plan["part"], plan["own"], plan["n_s"], plan["n_res"]
    pairs = chans // 2
    me = lax.axis_index("seq")

    def rows_of(ref, at):
        return ref[pl.ds(at, own), :].astype(jnp.float32)

    n_pairs = len(plan["pairs"])
    for u in range(plan["n_col"] - 1):
        chunks = [None] * n_res
        for k, (first, second) in enumerate(plan["pairs"]):
            place = u * n_pairs + k
            heard = [rows_of(x_refs[place], pl.multiple_of(h * part + me * own, own)) for h in range(2)]
            told = [rows_of(other_in, (2 * place + 1 - h) * own) for h in range(2)]
            chunks[first] = [jnp.where(me == 0, a, b) for a, b in zip(heard, told)]
            chunks[second] = [jnp.where(me == 0, b, a) for a, b in zip(heard, told)]
        order = [0] + plan["z_steps"]
        fill_left(left_scr, u, [slab for step in order for slab in chunks[step]], n_s)
    depth = left_scr.shape[1]
    offset = offset_ref[...]

    def block_of_columns(block):
        def weight_of(pair):
            return weights_ref[pl.ds((block * pairs + pair) * depth, depth), :]

        update_block(plan, block, 1, offset, w_ref, weight_of, left_scr, outer_scr, staged)

    loop_blocks(weights_ref.shape[0] // (pairs * depth), block_of_columns)
    write_out(plan, 1, staged, out_ref, sems)


def per_device(alignment, scale, shift, w1, b1, w2, b2, w_final, offset):
    n_s, span, width = alignment.shape
    n_res, n_col, n_seq = lax.axis_size("res"), lax.axis_size("col"), lax.axis_size("seq")
    chans, pair_width = w1.shape[1], w_final.shape[1]
    bf16 = jnp.bfloat16
    n_right = span * chans * n_s // LANES
    n_left = span * chans * n_s // LANES
    part = n_left // n_res
    own = part // n_seq
    rows_dev = span // (n_res * n_seq)
    params = pltpu.CompilerParams(vmem_limit_bytes=32 * 1024 * 1024)

    def rows(n):
        return jax.ShapeDtypeStruct((n, LANES), bf16)

    z_steps = [k for k in range(1, n_res) if k > 1] + [1] * (n_res > 1)
    pairs = [(k, k + 1) for k in range(1, n_res - 1, 2)] + [(0, n_res - 1)]

    taken = (alignment, scale.reshape(1, -1), shift.reshape(1, -1), w1.T, b1.reshape(1, -1), w2.T, b2.reshape(1, -1))
    slab, *z_out = pl.pallas_call(
        functools.partial(project_kernel, n_res, z_steps),
        out_shape=[rows(n_right + n_left)] + [rows(n_right + part)] * len(z_steps),
        in_specs=[HBM] * len(taken),
        out_specs=[VMEM] * n_res,
        scratch_shapes=[pltpu.VMEM(a.shape, a.dtype) for a in taken]
        + [
            pltpu.VMEM((n_s * span, LANES), jnp.float32),
            pltpu.VMEM((n_left, LANES), jnp.float32),
            pltpu.VMEM((n_right, LANES), jnp.float32),
            pltpu.SemaphoreType.DMA((len(taken),)),
        ],
        compiler_params=params,
        name="project",
    )(*[pltpu.with_memory_space_constraint(a, pltpu.HBM) for a in taken])

    def to_core(array):
        return lax.ppermute(array, "seq", [(q, 1 - q) for q in range(n_seq)])

    def to_chip(array, step_col, steps):
        route = []
        for r in range(n_res):
            for c in range(n_col):
                for q in range(n_seq):
                    to = partner(r, steps[q], n_res) * n_col + partner(c, step_col, n_col)
                    route.append(((r * n_col + c) * n_seq + q, to * n_seq + q))
        return lax.ppermute(array, ("res", "col", "seq"), route)

    slab_in = to_core(slab)
    z_in = [to_chip(array, 0, (step, step)) for array, step in zip(z_out, z_steps)]
    sends = [(u, steps) for u in range(1, n_col) for steps in pairs]
    messages = pl.pallas_call(
        functools.partial(chip_kernel, n_res, [steps for _, steps in sends]),
        out_shape=[rows(2 * part)] * len(sends),
        in_specs=[VMEM] * 2,
        out_specs=[VMEM] * len(sends),
        compiler_params=params,
        name="chip",
    )(slab, slab_in)
    x_in = [to_chip(message, u, steps) for message, (u, steps) in zip(messages, sends)]

    weights = pl.pallas_call(
        weight_kernel,
        out_shape=jax.ShapeDtypeStruct((pair_width, chans * chans), bf16),
        in_specs=[VMEM],
        out_specs=VMEM,
        scratch_shapes=[pltpu.VMEM((chans * chans, pair_width), jnp.float32)],
        compiler_params=params,
        name="weights",
    )(w_final)

    def share(arrays, n_rights, n_parts, cost):
        packed = pl.pallas_call(
            functools.partial(core_kernel, n_rights, part, own),
            out_shape=rows(len(arrays) * (n_rights + n_parts * own)),
            in_specs=[VMEM] * len(arrays),
            out_specs=VMEM,
            compiler_params=params,
            cost_estimate=cost,
            name="core",
        )(*arrays)
        return to_core(packed)

    other_z = share(z_in, n_right, 1, None)
    other_x = share(x_in, 0, 2, pl.CostEstimate(flops=20_000_000_000, bytes_accessed=0, transcendentals=0))

    turns = rows_dev * chans // LANES
    depth = turns * n_s * n_res * n_seq
    total = float(n_s * n_res * n_seq)
    plan = dict(
        n_res=n_res, n_col=n_col, chans=chans, part=part, own=own, n_s=n_s, pairs=pairs, z_steps=z_steps, total=total
    )
    out_type = jax.ShapeDtypeStruct((n_col, rows_dev, span, pair_width), bf16)
    n_blocks = n_right // (chans // 2 * n_s)

    def scratch(n_u):
        return [
            pltpu.VMEM((n_u * LANES, depth), bf16),
            pltpu.VMEM((chans * chans, n_u * (LANES // chans) * LANES), bf16),
            pltpu.VMEM((n_u, rows_dev, span, pair_width), bf16),
            pltpu.SemaphoreType.DMA((n_u,)),
        ]

    offset = offset.reshape(1, -1)
    operands = (offset, weights, slab, slab_in, *z_in, other_z)
    out, spread = pl.pallas_call(
        functools.partial(near_kernel, plan),
        out_shape=[out_type, jax.ShapeDtypeStruct((n_blocks * chans // 2 * depth, 2 * LANES), bf16)],
        in_specs=[VMEM] * len(operands),
        out_specs=[HBM, VMEM],
        scratch_shapes=scratch(1),
        compiler_params=params,
        name="near",
    )(*operands)
    operands = (offset, weights, spread, *x_in, other_x, out)
    return pl.pallas_call(
        functools.partial(far_kernel, plan),
        out_shape=out_type,
        in_specs=[VMEM] * (len(operands) - 1) + [HBM],
        out_specs=HBM,
        scratch_shapes=scratch(n_col - 1),
        input_output_aliases={len(operands) - 1: 0},
        compiler_params=params,
        name="far",
    )(*operands)


def solution(mesh):
    return jax.shard_map(
        per_device,
        mesh=mesh,
        in_specs=(P(("groups", "res", "seq"), "col", None), P(), P(), P(), P(), P(), P(), P(), P()),
        out_specs=P("groups", ("res", "seq"), "col", None),
        check_vma=False,
    )
```

```python
import functools

import jax
import jax.numpy as jnp
from jax import lax
from jax.experimental import pallas as pl
from jax.experimental.pallas import tpu as pltpu
from jax.sharding import PartitionSpec as P

LANES = 128
SUBLANES = 8
VMEM = pl.BlockSpec(memory_space=pltpu.VMEM)
HBM = pl.BlockSpec(memory_space=pltpu.HBM)
ACROSS = (((1,), (1,)), ((), ()))


def partner(index, step, size):
    return index ^ step if size & (size - 1) == 0 else (index + step) % size


def lane_index(shape):
    return lax.broadcasted_iota(jnp.int32, shape, len(shape) - 1)


def project_kernel(n_res, solo, *refs):
    n_in = 7
    sources, (slab_out, solo_out), scratch = refs[:n_in], refs[n_in : -n_in - 4], refs[-n_in - 4 :]
    landed, (rows_scr, lane_scr, right_scr, sems) = scratch[:n_in], scratch[n_in:]
    copies = [pltpu.make_async_copy(a, b, sems.at[i]) for i, (a, b) in enumerate(zip(sources, landed))]
    for copy in copies:
        copy.start()
    for copy in copies:
        copy.wait()
    x_ref, scale_ref, shift_ref, w1_ref, b1_ref, w2_ref, b2_ref = landed
    n_s, span, width = x_ref.shape
    chans = w1_ref.shape[0]
    fold = LANES // chans
    half = LANES // 2
    x = x_ref[...].reshape(n_s * span, width).astype(jnp.float32)
    mean = jnp.mean(x, axis=-1, keepdims=True)
    centred = x - mean
    variance = jnp.mean(centred * centred, axis=-1, keepdims=True)
    normed = (centred * lax.rsqrt(variance + 1e-05) * scale_ref[...] + shift_ref[...]).astype(jnp.bfloat16)

    w1 = jnp.concatenate([w1_ref[...]] * fold, axis=0)
    b1 = jnp.concatenate([b1_ref[...]] * fold, axis=1)
    rows_scr[...] = lax.dot_general(normed, w1, ACROSS, preferred_element_type=jnp.float32) + b1
    n_rows = n_s * span // fold
    owner = lane_index((n_rows, LANES)) // chans
    merged = rows_scr[pl.ds(0, n_rows, stride=fold), :]
    for turn in range(1, fold):
        merged = jnp.where(owner == turn, rows_scr[pl.ds(turn, n_rows, stride=fold), :], merged)
    groups = span // fold
    for s in range(n_s):
        lane_scr[pl.ds(s, groups, stride=n_s), :] = merged[s * groups : (s + 1) * groups]

    eye = lax.broadcasted_iota(jnp.int32, (chans, chans), 0) == lane_index((chans, chans))
    b2 = jnp.sum(jnp.where(eye, b2_ref[...], 0.0), axis=1, keepdims=True)
    right = lax.dot_general(w2_ref[...], normed, ACROSS, preferred_element_type=jnp.float32) + b2
    pairs = chans // 2
    low = lane_index((pairs, LANES)) < half
    blocks = span // half
    for tile in range(n_s * span // LANES):
        here = right[:, tile * LANES : (tile + 1) * LANES]
        there = pltpu.roll(here, half, 1)
        for side in range(2):
            s, block = divmod(2 * tile + side, blocks)
            first, second = (here, there) if side == 0 else (there, here)
            right_scr[pl.ds(block * pairs * n_s + s, pairs, stride=n_s), :] = jnp.where(
                low, first[:pairs], second[pairs:]
            )
    right_slab = right_scr[...].astype(jnp.bfloat16)
    n_right, n_left = right_scr.shape[0], lane_scr.shape[0]
    part = n_left // n_res
    slab_out[:n_right] = right_slab
    slab_out[n_right:] = lane_scr[...].astype(jnp.bfloat16)
    to = partner(lax.axis_index("res"), solo, n_res)
    solo_out[:n_right] = right_slab
    solo_out[n_right:] = lane_scr[pl.ds(pl.multiple_of(to * part, part), part), :].astype(jnp.bfloat16)


def chip_kernel(n_res, steps, own_ref, other_ref, *outs):
    n_right = own_ref.shape[0] // 2
    part = n_right // n_res
    me, here = lax.axis_index("seq"), lax.axis_index("res")
    for (first, second), out in zip(steps, outs):
        to = partner(here, jnp.where(me == 0, first, second), n_res)
        start = pl.multiple_of(n_right + to * part, part)
        at = out.shape[0] - 2 * part
        if at:
            out[:n_right] = own_ref[:n_right]
            out[n_right:at] = other_ref[:n_right]
        out[at : at + part] = own_ref[pl.ds(start, part), :]
        out[at + part :] = other_ref[pl.ds(start, part), :]


def core_kernel(bodies, part, own, *refs):
    ins, out = refs[:-1], refs[-1]
    mine = (1 - lax.axis_index("seq")) * own
    at = 0
    for body, ref in zip(bodies, ins):
        if body:
            out[at : at + body] = ref[:body]
            at += body
        for start in range(body, ref.shape[0], part):
            out[at : at + own] = ref[pl.ds(pl.multiple_of(start + mine, own), own), :]
            at += own


def weight_kernel(w_ref, out_ref, scr):
    chans_sq, width = w_ref.shape
    chans = int(round(chans_sq**0.5))
    scr[...] = w_ref[...].astype(jnp.float32)
    pairs = chans // 2
    fold = LANES // chans
    order = [side * pairs + pair for pair in range(pairs) for side in range(2)]
    for tile in range(chans // fold):
        piece = jnp.concatenate(
            [scr[pl.ds(e, chans, stride=chans), :] for e in order[tile * fold : (tile + 1) * fold]], axis=0
        )
        out_ref[:, tile * LANES : (tile + 1) * LANES] = piece.T.astype(jnp.bfloat16)


def pair_kernel(plan, total, offset_ref, w_ref, *refs):
    out_ref, left_scr, outer_scr = refs[-3], refs[-2], refs[-1]
    n_col, chans, part, own = plan["n_col"], plan["chans"], plan["part"], plan["own"]
    n_res = plan["n_res"]
    n_right = part * n_res
    me = lax.axis_index("seq")
    half = LANES // 2
    fold = LANES // chans
    pairs = chans // 2
    rows_dev = out_ref.shape[1]
    turns = rows_dev // fold
    n_s = own // turns

    z_pairs, x_pairs = plan["z_pairs"], plan["x_pairs"]
    own_ref, other_ref, solo_ref = refs[:3]
    z_refs = refs[3 : 3 + len(z_pairs)]
    x_refs, other_in = refs[3 + len(z_pairs) : -4], refs[-4]
    mine = pl.multiple_of(me * own, own)

    def rows_of(ref, at):
        return ref[pl.ds(at, own), :].astype(jnp.float32)

    start = pl.multiple_of(n_right + lax.axis_index("res") * part + mine, own)
    rights = [(own_ref, 0), (other_ref, 0), (solo_ref, 0), (other_in, 0)]
    lefts = [[rows_of(own_ref, start), rows_of(other_ref, start)]]
    lefts[0] += [rows_of(solo_ref, pl.multiple_of(n_right + mine, own)), rows_of(other_in, n_right)]
    at = n_right + own
    for ref in z_refs:
        rights += [(ref, 0), (ref, n_right), (other_in, at + n_right), (other_in, at)]
        lefts[0] += [rows_of(ref, pl.multiple_of(2 * n_right + h * part + mine, own)) for h in range(2)]
        lefts[0] += [rows_of(other_in, at + 2 * n_right + (1 - h) * own) for h in range(2)]
        at += 2 * (n_right + own)

    def pick(first, second):
        return [jnp.where(me == 0, a, b) for a, b in zip(first, second)]

    for u in range(n_col - 1):
        chunks = [None] * n_res
        for k, (first, second) in enumerate(x_pairs):
            place = u * len(x_pairs) + k
            heard = [rows_of(x_refs[place], pl.multiple_of(h * part + mine, own)) for h in range(2)]
            told = [rows_of(other_in, at + (2 * place + 1 - h) * own) for h in range(2)]
            chunks[first], chunks[second] = pick(heard, told), pick(told, heard)
        order = chunks[0] + chunks[plan["solo"]]
        for first, second in z_pairs:
            order += pick(chunks[first], chunks[second]) + pick(chunks[second], chunks[first])
        lefts.append(order)

    for u in range(n_col):
        for turn in range(turns):
            column = jnp.concatenate([slab[turn * n_s : (turn + 1) * n_s] for slab in lefts[u]], axis=0)
            depth = column.shape[0]
            left_scr[u * LANES : (u + 1) * LANES, turn * depth : (turn + 1) * depth] = column.T.astype(jnp.bfloat16)

    n_blocks = n_right // (pairs * n_s)
    offset = offset_ref[...]
    col = lax.axis_index("col")

    def block_of_columns(block):
        at_block = block * pairs * n_s
        slabs = [ref[pl.ds(at + at_block, pairs * n_s), :].astype(jnp.float32) for ref, at in rights]
        left = left_scr[...]
        for pair in range(pairs):
            here = jnp.concatenate([slab[pair * n_s : (pair + 1) * n_s] for slab in slabs], axis=0)
            there = pltpu.roll(here, half, 1)
            low = lane_index(here.shape) < half
            weights = jnp.concatenate(
                [
                    jnp.concatenate([jnp.where(low, here, 0.0), jnp.where(low, 0.0, there)], axis=0),
                    jnp.concatenate([jnp.where(low, there, 0.0), jnp.where(low, 0.0, here)], axis=0),
                ],
                axis=1,
            ).astype(jnp.bfloat16)
            outer = jnp.dot(left, weights, preferred_element_type=jnp.float32).astype(jnp.bfloat16)
            for side in range(2):
                at = (2 * pair + side) * chans
                for tile in range(n_col * fold):
                    outer_scr[at : at + chans, tile * LANES : (tile + 1) * LANES] = outer[
                        tile * chans : (tile + 1) * chans, side * LANES : (side + 1) * LANES
                    ]
        for u in range(n_col):
            summed = jnp.dot(
                w_ref[...],
                outer_scr[:, u * fold * LANES : (u + 1) * fold * LANES],
                preferred_element_type=jnp.float32,
            )
            to = partner(col, u, n_col) if n_col & (n_col - 1) == 0 else (col - u + n_col) % n_col
            for residue in range(fold):
                piece = summed[:, residue * LANES : (residue + 1) * LANES].T
                piece = (piece / total + offset).astype(jnp.bfloat16)
                for turn in range(turns):
                    out_ref[to, turn * fold + residue, pl.ds(block * half, half), :] = piece[
                        turn * half : (turn + 1) * half
                    ]

    if n_blocks == 1:
        block_of_columns(0)
    else:
        pl.loop(0, n_blocks)(block_of_columns)


def per_device(alignment, scale, shift, w1, b1, w2, b2, w_final, offset):
    n_s, span, width = alignment.shape
    n_res, n_col, n_seq = lax.axis_size("res"), lax.axis_size("col"), lax.axis_size("seq")
    chans, pair_width = w1.shape[1], w_final.shape[1]
    bf16 = jnp.bfloat16
    n_right = span * chans * n_s // LANES
    n_left = span * chans * n_s // LANES
    part = n_left // n_res
    own = part // n_seq
    rows_dev = span // (n_res * n_seq)
    params = pltpu.CompilerParams(vmem_limit_bytes=32 * 1024 * 1024)

    def rows(n):
        return jax.ShapeDtypeStruct((n, LANES), bf16)

    solo = n_res - 1
    z_pairs = [(k, k + 1) for k in range(1, solo, 2)]
    x_pairs = [(k, k + 1) for k in range(n_res - 2, -1, -2)]

    taken = (alignment, scale.reshape(1, -1), shift.reshape(1, -1), w1.T, b1.reshape(1, -1), w2.T, b2.reshape(1, -1))
    slab, solo_out = pl.pallas_call(
        functools.partial(project_kernel, n_res, solo),
        out_shape=[rows(n_right + n_left), rows(n_right + part)],
        in_specs=[HBM] * len(taken),
        out_specs=[VMEM] * 2,
        scratch_shapes=[pltpu.VMEM(a.shape, a.dtype) for a in taken]
        + [
            pltpu.VMEM((n_s * span, LANES), jnp.float32),
            pltpu.VMEM((n_left, LANES), jnp.float32),
            pltpu.VMEM((n_right, LANES), jnp.float32),
            pltpu.SemaphoreType.DMA((len(taken),)),
        ],
        compiler_params=params,
        name="project",
    )(*[pltpu.with_memory_space_constraint(a, pltpu.HBM) for a in taken])

    def to_core(array):
        return lax.ppermute(array, "seq", [(q, 1 - q) for q in range(n_seq)])

    def to_chip(array, step_col, steps):
        route = []
        for r in range(n_res):
            for c in range(n_col):
                for q in range(n_seq):
                    to = partner(r, steps[q], n_res) * n_col + partner(c, step_col, n_col)
                    route.append(((r * n_col + c) * n_seq + q, to * n_seq + q))
        return lax.ppermute(array, ("res", "col", "seq"), route)

    slab_in = to_core(slab)
    solo_in = to_chip(solo_out, 0, (solo, solo))
    sends = [(0, steps) for steps in z_pairs] + [(u, steps) for u in range(1, n_col) for steps in x_pairs]
    messages = pl.pallas_call(
        functools.partial(chip_kernel, n_res, [steps for _, steps in sends]),
        out_shape=[rows(2 * part + (0 if u else 2 * n_right)) for u, _ in sends],
        in_specs=[VMEM] * 2,
        out_specs=[VMEM] * len(sends),
        compiler_params=params,
        name="chip",
    )(slab, slab_in)
    heard = [to_chip(message, u, steps) for message, (u, steps) in zip(messages, sends)]

    weights = pl.pallas_call(
        weight_kernel,
        out_shape=jax.ShapeDtypeStruct((pair_width, chans * chans), bf16),
        in_specs=[VMEM],
        out_specs=VMEM,
        scratch_shapes=[pltpu.VMEM((chans * chans, pair_width), jnp.float32)],
        compiler_params=params,
        name="weights",
    )(w_final)

    def pack(arrays, bodies, flops):
        return pl.pallas_call(
            functools.partial(core_kernel, bodies, part, own),
            out_shape=rows(sum(b + (a.shape[0] - b) // part * own for a, b in zip(arrays, bodies))),
            in_specs=[VMEM] * len(arrays),
            out_specs=VMEM,
            compiler_params=params,
            cost_estimate=pl.CostEstimate(flops=flops, bytes_accessed=0, transcendentals=0),
            name="core",
        )(*arrays)

    arrays = [pack([solo_in], [n_right], 500_000_000)] + heard
    bodies = [n_right + own] + [array.shape[0] // part // n_res * n_right for array in heard]
    other_in = to_core(pack(arrays, bodies, 0))

    turns = rows_dev * chans // LANES
    depth = turns * n_s * n_res * n_seq
    plan = dict(
        n_res=n_res, n_col=n_col, chans=chans, part=part, own=own, solo=solo, z_pairs=z_pairs, x_pairs=x_pairs
    )
    operands = (offset.reshape(1, -1), weights, slab, slab_in, solo_in, *heard, other_in)
    return pl.pallas_call(
        functools.partial(pair_kernel, plan, float(n_s * n_res * n_seq)),
        out_shape=jax.ShapeDtypeStruct((n_col, rows_dev, span, pair_width), bf16),
        in_specs=[VMEM] * len(operands),
        out_specs=VMEM,
        scratch_shapes=[
            pltpu.VMEM((n_col * LANES, depth), bf16),
            pltpu.VMEM((chans * chans, n_col * (LANES // chans) * LANES), bf16),
        ],
        compiler_params=params,
        name="pair",
    )(*operands)


def solution(mesh):
    return jax.shard_map(
        per_device,
        mesh=mesh,
        in_specs=(P(("groups", "res", "seq"), "col", None), P(), P(), P(), P(), P(), P(), P(), P()),
        out_specs=P("groups", ("res", "seq"), "col", None),
        check_vma=False,
    )
```

```python
import functools

import jax
import jax.numpy as jnp
from jax import lax
from jax.experimental import pallas as pl
from jax.experimental.pallas import tpu as pltpu
from jax.sharding import PartitionSpec as P

LANES = 128
SUBLANES = 8
VMEM = pl.BlockSpec(memory_space=pltpu.VMEM)
HBM = pl.BlockSpec(memory_space=pltpu.HBM)
ACROSS = (((1,), (1,)), ((), ()))


def partner(index, step, size):
    return index ^ step if size & (size - 1) == 0 else (index + step) % size


def lane_index(shape):
    return lax.broadcasted_iota(jnp.int32, shape, len(shape) - 1)


def project_kernel(n_res, solo, *refs):
    n_in = 7
    sources, (slab_out, solo_out), scratch = refs[:n_in], refs[n_in : -n_in - 4], refs[-n_in - 4 :]
    landed, (rows_scr, lane_scr, right_scr, sems) = scratch[:n_in], scratch[n_in:]
    copies = [pltpu.make_async_copy(a, b, sems.at[i]) for i, (a, b) in enumerate(zip(sources, landed))]
    for copy in copies:
        copy.start()
    for copy in copies:
        copy.wait()
    x_ref, scale_ref, shift_ref, w1_ref, b1_ref, w2_ref, b2_ref = landed
    n_s, span, width = x_ref.shape
    chans = w1_ref.shape[0]
    fold = LANES // chans
    half = LANES // 2
    x = x_ref[...].reshape(n_s * span, width).astype(jnp.float32)
    mean = jnp.mean(x, axis=-1, keepdims=True)
    centred = x - mean
    variance = jnp.mean(centred * centred, axis=-1, keepdims=True)
    normed = (centred * lax.rsqrt(variance + 1e-05) * scale_ref[...] + shift_ref[...]).astype(jnp.bfloat16)

    w1 = jnp.concatenate([w1_ref[...]] * fold, axis=0)
    b1 = jnp.concatenate([b1_ref[...]] * fold, axis=1)
    rows_scr[...] = lax.dot_general(normed, w1, ACROSS, preferred_element_type=jnp.float32) + b1
    n_rows = n_s * span // fold
    owner = lane_index((n_rows, LANES)) // chans
    merged = rows_scr[pl.ds(0, n_rows, stride=fold), :]
    for turn in range(1, fold):
        merged = jnp.where(owner == turn, rows_scr[pl.ds(turn, n_rows, stride=fold), :], merged)
    groups = span // fold
    for s in range(n_s):
        lane_scr[pl.ds(s, groups, stride=n_s), :] = merged[s * groups : (s + 1) * groups]

    eye = lax.broadcasted_iota(jnp.int32, (chans, chans), 0) == lane_index((chans, chans))
    b2 = jnp.sum(jnp.where(eye, b2_ref[...], 0.0), axis=1, keepdims=True)
    right = lax.dot_general(w2_ref[...], normed, ACROSS, preferred_element_type=jnp.float32) + b2
    pairs = chans // 2
    low = lane_index((pairs, LANES)) < half
    blocks = span // half
    for tile in range(n_s * span // LANES):
        here = right[:, tile * LANES : (tile + 1) * LANES]
        there = pltpu.roll(here, half, 1)
        for side in range(2):
            s, block = divmod(2 * tile + side, blocks)
            first, second = (here, there) if side == 0 else (there, here)
            right_scr[pl.ds(block * pairs * n_s + s, pairs, stride=n_s), :] = jnp.where(
                low, first[:pairs], second[pairs:]
            )
    right_slab = right_scr[...].astype(jnp.bfloat16)
    n_right, n_left = right_scr.shape[0], lane_scr.shape[0]
    part = n_left // n_res
    slab_out[:n_right] = right_slab
    slab_out[n_right:] = lane_scr[...].astype(jnp.bfloat16)
    to = partner(lax.axis_index("res"), solo, n_res)
    solo_out[:n_right] = right_slab
    solo_out[n_right:] = lane_scr[pl.ds(pl.multiple_of(to * part, part), part), :].astype(jnp.bfloat16)


def chip_kernel(n_res, steps, own_ref, other_ref, *outs):
    n_right = own_ref.shape[0] // 2
    part = n_right // n_res
    me, here = lax.axis_index("seq"), lax.axis_index("res")
    for (first, second), out in zip(steps, outs):
        to = partner(here, jnp.where(me == 0, first, second), n_res)
        start = pl.multiple_of(n_right + to * part, part)
        at = out.shape[0] - 2 * part
        if at:
            out[:n_right] = own_ref[:n_right]
            out[n_right:at] = other_ref[:n_right]
        out[at : at + part] = own_ref[pl.ds(start, part), :]
        out[at + part :] = other_ref[pl.ds(start, part), :]


def core_kernel(bodies, part, own, *refs):
    ins, out = refs[: len(bodies)], refs[-1]
    mine = (1 - lax.axis_index("seq")) * own
    at = 0
    for body, ref in zip(bodies, ins):
        if body:
            out[at : at + body] = ref[:body]
            at += body
        for start in range(body, ref.shape[0], part):
            out[at : at + own] = ref[pl.ds(pl.multiple_of(start + mine, own), own), :]
            at += own


def weight_kernel(w_ref, _, out_ref, scr):
    chans_sq, width = w_ref.shape
    chans = int(round(chans_sq**0.5))
    scr[...] = w_ref[...].astype(jnp.float32)
    pairs = chans // 2
    fold = LANES // chans
    order = [side * pairs + pair for pair in range(pairs) for side in range(2)]
    for tile in range(chans // fold):
        piece = jnp.concatenate(
            [scr[pl.ds(e, chans, stride=chans), :] for e in order[tile * fold : (tile + 1) * fold]], axis=0
        )
        out_ref[:, tile * LANES : (tile + 1) * LANES] = piece.T.astype(jnp.bfloat16)


def fill_left(left_scr, u, slabs, n_s):
    turns = slabs[0].shape[0] // n_s
    for turn in range(turns):
        column = jnp.concatenate([slab[turn * n_s : (turn + 1) * n_s] for slab in slabs], axis=0)
        depth = column.shape[0]
        left_scr[u * LANES : (u + 1) * LANES, turn * depth : (turn + 1) * depth] = column.T.astype(jnp.bfloat16)


def loop_blocks(n_blocks, body):
    if n_blocks == 1:
        body(0)
    else:
        pl.loop(0, n_blocks)(body)


def update_block(plan, block, offset, w_ref, weight_of, left_scr, outer_scr, staged):
    chans, total = plan["chans"], plan["total"]
    half = LANES // 2
    fold = LANES // chans
    left = left_scr[...]
    n_u = left.shape[0] // LANES
    for pair in range(chans // 2):
        outer = jnp.dot(left, weight_of(pair), preferred_element_type=jnp.float32).astype(jnp.bfloat16)
        for side in range(2):
            at = (2 * pair + side) * chans
            for tile in range(n_u * fold):
                outer_scr[at : at + chans, tile * LANES : (tile + 1) * LANES] = outer[
                    tile * chans : (tile + 1) * chans, side * LANES : (side + 1) * LANES
                ]
    for u in range(n_u):
        summed = jnp.dot(
            w_ref[...], outer_scr[:, u * fold * LANES : (u + 1) * fold * LANES], preferred_element_type=jnp.float32
        )
        for residue in range(fold):
            piece = summed[:, residue * LANES : (residue + 1) * LANES].T
            piece = (piece / total + offset[...]).astype(jnp.bfloat16)
            for turn in range(LANES // half):
                staged[u, turn * fold + residue, pl.ds(block * half, half), :] = piece[
                    turn * half : (turn + 1) * half
                ]


def start_out(plan, u_base, staged, out_ref, sems):
    n_col = plan["n_col"]
    col = lax.axis_index("col")
    copies = []
    for u in range(staged.shape[0]):
        step = u_base + u
        source = partner(col, step, n_col) if n_col & (n_col - 1) == 0 else (col - step + n_col) % n_col
        copies.append(pltpu.make_async_copy(staged.at[u], out_ref.at[source], sems.at[step]))
        copies[-1].start()
    return copies


def near_kernel(plan, offset_ref, w_ref, own_ref, other_ref, solo_ref, *refs):
    z_refs, (other_in, staged, weights_out, offset, left_scr, outer_scr, sem) = refs[:-7], refs[-7:]
    chans, part, own, n_s = plan["chans"], plan["part"], plan["own"], plan["n_s"]
    n_right = part * plan["n_res"]
    half = LANES // 2
    pairs = chans // 2
    mine = pl.multiple_of(lax.axis_index("seq") * own, own)
    fetch = pltpu.make_async_copy(offset_ref, offset, sem)
    fetch.start()

    def rows_of(ref, at):
        return ref[pl.ds(at, own), :].astype(jnp.float32)

    start = pl.multiple_of(n_right + lax.axis_index("res") * part + mine, own)
    rights = [(own_ref, 0), (other_ref, 0), (solo_ref, 0), (other_in, 0)]
    lefts = [rows_of(own_ref, start), rows_of(other_ref, start)]
    lefts += [rows_of(solo_ref, pl.multiple_of(n_right + mine, own)), rows_of(other_in, n_right)]
    at = n_right + own
    for ref in z_refs:
        rights += [(ref, 0), (ref, n_right), (other_in, at + n_right), (other_in, at)]
        lefts += [rows_of(ref, pl.multiple_of(2 * n_right + h * part + mine, own)) for h in range(2)]
        lefts += [rows_of(other_in, at + 2 * n_right + (1 - h) * own) for h in range(2)]
        at += 2 * (n_right + own)
    fill_left(left_scr, 0, lefts, n_s)
    depth = left_scr.shape[1]

    def block_of_columns(block):
        at_block = block * pairs * n_s
        slabs = [ref[pl.ds(at + at_block, pairs * n_s), :].astype(jnp.float32) for ref, at in rights]

        def weight_of(pair):
            here = jnp.concatenate([slab[pair * n_s : (pair + 1) * n_s] for slab in slabs], axis=0)
            there = pltpu.roll(here, half, 1)
            low = lane_index(here.shape) < half
            weights = jnp.concatenate(
                [
                    jnp.concatenate([jnp.where(low, here, 0.0), jnp.where(low, 0.0, there)], axis=0),
                    jnp.concatenate([jnp.where(low, there, 0.0), jnp.where(low, 0.0, here)], axis=0),
                ],
                axis=1,
            ).astype(jnp.bfloat16)
            weights_out[pl.ds((block * pairs + pair) * depth, depth), :] = weights
            return weights

        update_block(plan, block, offset, w_ref, weight_of, left_scr, outer_scr, staged)

    fetch.wait()
    loop_blocks(n_right // (pairs * n_s), block_of_columns)


def far_kernel(plan, offset_ref, w_ref, weights_ref, near_ref, *refs):
    x_refs, (other_in, out_ref, left_scr, outer_scr, staged, sems) = refs[:-6], refs[-6:]
    chans, part, own, n_s, n_res = plan["chans"], plan["part"], plan["own"], plan["n_s"], plan["n_res"]
    pairs = chans // 2
    me = lax.axis_index("seq")
    copies = start_out(plan, 0, near_ref, out_ref, sems)

    def rows_of(ref, at):
        return ref[pl.ds(at, own), :].astype(jnp.float32)

    def pick(first, second):
        return [jnp.where(me == 0, a, b) for a, b in zip(first, second)]

    x_pairs = plan["x_pairs"]
    for u in range(plan["n_col"] - 1):
        chunks = [None] * n_res
        for k, (first, second) in enumerate(x_pairs):
            place = u * len(x_pairs) + k
            heard = [rows_of(x_refs[place], pl.multiple_of(h * part + me * own, own)) for h in range(2)]
            told = [rows_of(other_in, (2 * place + 1 - h) * own) for h in range(2)]
            chunks[first], chunks[second] = pick(heard, told), pick(told, heard)
        order = chunks[0] + chunks[plan["solo"]]
        for first, second in plan["z_pairs"]:
            order += pick(chunks[first], chunks[second]) + pick(chunks[second], chunks[first])
        fill_left(left_scr, u, order, n_s)
    depth = left_scr.shape[1]

    def block_of_columns(block):
        def weight_of(pair):
            return weights_ref[pl.ds((block * pairs + pair) * depth, depth), :]

        update_block(plan, block, offset_ref, w_ref, weight_of, left_scr, outer_scr, staged)

    loop_blocks(weights_ref.shape[0] // (pairs * depth), block_of_columns)
    copies += start_out(plan, 1, staged, out_ref, sems)
    for copy in copies:
        copy.wait()


def per_device(alignment, scale, shift, w1, b1, w2, b2, w_final, offset):
    n_s, span, width = alignment.shape
    n_res, n_col, n_seq = lax.axis_size("res"), lax.axis_size("col"), lax.axis_size("seq")
    chans, pair_width = w1.shape[1], w_final.shape[1]
    bf16 = jnp.bfloat16
    n_right = span * chans * n_s // LANES
    n_left = span * chans * n_s // LANES
    part = n_left // n_res
    own = part // n_seq
    rows_dev = span // (n_res * n_seq)
    params = pltpu.CompilerParams(vmem_limit_bytes=32 * 1024 * 1024)

    def rows(n):
        return jax.ShapeDtypeStruct((n, LANES), bf16)

    solo = n_res - 1
    z_pairs = [(k, k + 1) for k in range(1, solo, 2)]
    x_pairs = [(k, k + 1) for k in range(n_res - 2, -1, -2)]

    taken = (alignment, scale.reshape(1, -1), shift.reshape(1, -1), w1.T, b1.reshape(1, -1), w2.T, b2.reshape(1, -1))
    slab, solo_out = pl.pallas_call(
        functools.partial(project_kernel, n_res, solo),
        out_shape=[rows(n_right + n_left), rows(n_right + part)],
        in_specs=[HBM] * len(taken),
        out_specs=[VMEM] * 2,
        scratch_shapes=[pltpu.VMEM(a.shape, a.dtype) for a in taken]
        + [
            pltpu.VMEM((n_s * span, LANES), jnp.float32),
            pltpu.VMEM((n_left, LANES), jnp.float32),
            pltpu.VMEM((n_right, LANES), jnp.float32),
            pltpu.SemaphoreType.DMA((len(taken),)),
        ],
        compiler_params=params,
        name="project",
    )(*[pltpu.with_memory_space_constraint(a, pltpu.HBM) for a in taken])

    def to_core(array):
        return lax.ppermute(array, "seq", [(q, 1 - q) for q in range(n_seq)])

    def to_chip(array, step_col, steps):
        route = []
        for r in range(n_res):
            for c in range(n_col):
                for q in range(n_seq):
                    to = partner(r, steps[q], n_res) * n_col + partner(c, step_col, n_col)
                    route.append(((r * n_col + c) * n_seq + q, to * n_seq + q))
        return lax.ppermute(array, ("res", "col", "seq"), route)

    slab_in = to_core(slab)
    solo_in = to_chip(solo_out, 0, (solo, solo))
    sends = [(0, steps) for steps in z_pairs] + [(u, steps) for u in range(1, n_col) for steps in x_pairs]
    messages = pl.pallas_call(
        functools.partial(chip_kernel, n_res, [steps for _, steps in sends]),
        out_shape=[rows(2 * part + (0 if u else 2 * n_right)) for u, _ in sends],
        in_specs=[VMEM] * 2,
        out_specs=[VMEM] * len(sends),
        compiler_params=params,
        name="chip",
    )(slab, slab_in)
    heard = [to_chip(message, u, steps) for message, (u, steps) in zip(messages, sends)]

    def pack(arrays, bodies, flops, after=()):
        return pl.pallas_call(
            functools.partial(core_kernel, bodies, part, own),
            out_shape=rows(sum(b + (a.shape[0] - b) // part * own for a, b in zip(arrays, bodies))),
            in_specs=[VMEM] * (len(arrays) + len(after)),
            out_specs=VMEM,
            compiler_params=params,
            cost_estimate=pl.CostEstimate(flops=flops, bytes_accessed=0, transcendentals=0),
            name="core",
        )(*arrays, *after)

    z_in, x_in = heard[: len(z_pairs)], heard[len(z_pairs) :]
    arrays = [pack([solo_in], [n_right], 500_000_000)] + z_in
    weights = pl.pallas_call(
        weight_kernel,
        out_shape=jax.ShapeDtypeStruct((pair_width, chans * chans), bf16),
        in_specs=[VMEM] * 2,
        out_specs=VMEM,
        scratch_shapes=[pltpu.VMEM((chans * chans, pair_width), jnp.float32)],
        compiler_params=params,
        name="weights",
    )(w_final, arrays[0])

    other_z = to_core(pack(arrays, [n_right + own] + [2 * n_right] * len(z_in), 0))
    other_x = to_core(pack(x_in, [0] * len(x_in), 20_000_000_000, (weights,)))

    turns = rows_dev * chans // LANES
    depth = turns * n_s * n_res * n_seq
    plan = dict(n_res=n_res, n_col=n_col, chans=chans, part=part, own=own, n_s=n_s, total=float(n_s * n_res * n_seq))
    plan.update(solo=solo, z_pairs=z_pairs, x_pairs=x_pairs)
    n_blocks = n_right // (chans // 2 * n_s)

    def scratch(n_u):
        return [
            pltpu.VMEM((n_u * LANES, depth), bf16),
            pltpu.VMEM((chans * chans, n_u * (LANES // chans) * LANES), bf16),
        ]

    def rows_type(n_u):
        return jax.ShapeDtypeStruct((n_u, rows_dev, span, pair_width), bf16)

    offset = pltpu.with_memory_space_constraint(offset.reshape(1, -1), pltpu.HBM)
    operands = (offset, weights, slab, slab_in, solo_in, *z_in, other_z)
    near, spread, offset = pl.pallas_call(
        functools.partial(near_kernel, plan),
        out_shape=[
            rows_type(1),
            jax.ShapeDtypeStruct((n_blocks * chans // 2 * depth, 2 * LANES), bf16),
            jax.ShapeDtypeStruct(offset.shape, offset.dtype),
        ],
        in_specs=[HBM] + [VMEM] * (len(operands) - 1),
        out_specs=[VMEM] * 3,
        scratch_shapes=scratch(1) + [pltpu.SemaphoreType.DMA(())],
        compiler_params=params,
        name="near",
    )(*operands)
    operands = (offset, weights, spread, near, *x_in, other_x)
    return pl.pallas_call(
        functools.partial(far_kernel, plan),
        out_shape=rows_type(n_col),
        in_specs=[VMEM] * len(operands),
        out_specs=HBM,
        scratch_shapes=scratch(n_col - 1)
        + [pltpu.VMEM((n_col - 1, rows_dev, span, pair_width), bf16), pltpu.SemaphoreType.DMA((n_col,))],
        compiler_params=params,
        name="far",
    )(*operands)


def solution(mesh):
    return jax.shard_map(
        per_device,
        mesh=mesh,
        in_specs=(P(("groups", "res", "seq"), "col", None), P(), P(), P(), P(), P(), P(), P(), P()),
        out_specs=P("groups", ("res", "seq"), "col", None),
        check_vma=False,
    )
```

```python
import functools

import jax
import jax.numpy as jnp
from jax import lax
from jax.experimental import pallas as pl
from jax.experimental.pallas import tpu as pltpu
from jax.sharding import PartitionSpec as P

LANES = 128
SUBLANES = 8
VMEM = pl.BlockSpec(memory_space=pltpu.VMEM)
HBM = pl.BlockSpec(memory_space=pltpu.HBM)
ACROSS = (((1,), (1,)), ((), ()))


def partner(index, step, size):
    return index ^ step if size & (size - 1) == 0 else (index + step) % size


def lane_index(shape):
    return lax.broadcasted_iota(jnp.int32, shape, len(shape) - 1)


def project_kernel(n_res, solo, *refs):
    n_in = 7
    sources, (slab_out, solo_out), scratch = refs[:n_in], refs[n_in : -n_in - 4], refs[-n_in - 4 :]
    landed, (rows_scr, lane_scr, right_scr, sems) = scratch[:n_in], scratch[n_in:]
    copies = [pltpu.make_async_copy(a, b, sems.at[i]) for i, (a, b) in enumerate(zip(sources, landed))]
    for copy in copies:
        copy.start()
    for copy in copies:
        copy.wait()
    x_ref, scale_ref, shift_ref, w1_ref, b1_ref, w2_ref, b2_ref = landed
    n_s, span, width = x_ref.shape
    chans = w1_ref.shape[0]
    fold = LANES // chans
    half = LANES // 2
    x = x_ref[...].reshape(n_s * span, width).astype(jnp.float32)
    mean = jnp.mean(x, axis=-1, keepdims=True)
    centred = x - mean
    variance = jnp.mean(centred * centred, axis=-1, keepdims=True)
    normed = (centred * lax.rsqrt(variance + 1e-05) * scale_ref[...] + shift_ref[...]).astype(jnp.bfloat16)

    w1 = jnp.concatenate([w1_ref[...]] * fold, axis=0)
    b1 = jnp.concatenate([b1_ref[...]] * fold, axis=1)
    rows_scr[...] = lax.dot_general(normed, w1, ACROSS, preferred_element_type=jnp.float32) + b1
    n_rows = n_s * span // fold
    owner = lane_index((n_rows, LANES)) // chans
    merged = rows_scr[pl.ds(0, n_rows, stride=fold), :]
    for turn in range(1, fold):
        merged = jnp.where(owner == turn, rows_scr[pl.ds(turn, n_rows, stride=fold), :], merged)
    groups = span // fold
    for s in range(n_s):
        lane_scr[pl.ds(s, groups, stride=n_s), :] = merged[s * groups : (s + 1) * groups]

    eye = lax.broadcasted_iota(jnp.int32, (chans, chans), 0) == lane_index((chans, chans))
    b2 = jnp.sum(jnp.where(eye, b2_ref[...], 0.0), axis=1, keepdims=True)
    right = lax.dot_general(w2_ref[...], normed, ACROSS, preferred_element_type=jnp.float32) + b2
    pairs = chans // 2
    low = lane_index((pairs, LANES)) < half
    blocks = span // half
    for tile in range(n_s * span // LANES):
        here = right[:, tile * LANES : (tile + 1) * LANES]
        there = pltpu.roll(here, half, 1)
        for side in range(2):
            s, block = divmod(2 * tile + side, blocks)
            first, second = (here, there) if side == 0 else (there, here)
            right_scr[pl.ds(block * pairs * n_s + s, pairs, stride=n_s), :] = jnp.where(
                low, first[:pairs], second[pairs:]
            )
    right_slab = right_scr[...].astype(jnp.bfloat16)
    n_right, n_left = right_scr.shape[0], lane_scr.shape[0]
    part = n_left // n_res
    slab_out[:n_right] = right_slab
    slab_out[n_right:] = lane_scr[...].astype(jnp.bfloat16)
    to = partner(lax.axis_index("res"), solo, n_res)
    solo_out[:n_right] = right_slab
    solo_out[n_right:] = lane_scr[pl.ds(pl.multiple_of(to * part, part), part), :].astype(jnp.bfloat16)


def chip_kernel(n_res, steps, own_ref, other_ref, *outs):
    n_right = own_ref.shape[0] // 2
    part = n_right // n_res
    me, here = lax.axis_index("seq"), lax.axis_index("res")
    for (first, second), out in zip(steps, outs):
        to = partner(here, jnp.where(me == 0, first, second), n_res)
        start = pl.multiple_of(n_right + to * part, part)
        at = out.shape[0] - 2 * part
        if at:
            out[:n_right] = own_ref[:n_right]
            out[n_right:at] = other_ref[:n_right]
        out[at : at + part] = own_ref[pl.ds(start, part), :]
        out[at + part :] = other_ref[pl.ds(start, part), :]


def core_kernel(bodies, part, own, *refs):
    ins, out = refs[: len(bodies)], refs[-1]
    mine = (1 - lax.axis_index("seq")) * own
    at = 0
    for body, ref in zip(bodies, ins):
        if body:
            out[at : at + body] = ref[:body]
            at += body
        for start in range(body, ref.shape[0], part):
            out[at : at + own] = ref[pl.ds(pl.multiple_of(start + mine, own), own), :]
            at += own


def weight_kernel(w_ref, offset_ref, _, out_ref, offset_out, scr):
    chans_sq, width = w_ref.shape
    chans = int(round(chans_sq**0.5))
    offset_out[...] = offset_ref[...]
    scr[...] = w_ref[...].astype(jnp.float32)
    pairs = chans // 2
    fold = LANES // chans
    order = [side * pairs + pair for pair in range(pairs) for side in range(2)]
    for tile in range(chans // fold):
        piece = jnp.concatenate(
            [scr[pl.ds(e, chans, stride=chans), :] for e in order[tile * fold : (tile + 1) * fold]], axis=0
        )
        out_ref[:, tile * LANES : (tile + 1) * LANES] = piece.T.astype(jnp.bfloat16)


def fill_left(left_scr, u, slabs, n_s):
    turns = slabs[0].shape[0] // n_s
    for turn in range(turns):
        column = jnp.concatenate([slab[turn * n_s : (turn + 1) * n_s] for slab in slabs], axis=0)
        depth = column.shape[0]
        left_scr[u * LANES : (u + 1) * LANES, turn * depth : (turn + 1) * depth] = column.T.astype(jnp.bfloat16)


def loop_blocks(n_blocks, body):
    if n_blocks == 1:
        body(0)
    else:
        pl.loop(0, n_blocks)(body)


def update_block(plan, block, offset, w_ref, weight_of, left_scr, outer_scr, staged):
    chans, total = plan["chans"], plan["total"]
    half = LANES // 2
    fold = LANES // chans
    left = left_scr[...]
    n_u = left.shape[0] // LANES
    for pair in range(chans // 2):
        outer = jnp.dot(left, weight_of(pair), preferred_element_type=jnp.float32).astype(jnp.bfloat16)
        for side in range(2):
            at = (2 * pair + side) * chans
            for tile in range(n_u * fold):
                outer_scr[at : at + chans, tile * LANES : (tile + 1) * LANES] = outer[
                    tile * chans : (tile + 1) * chans, side * LANES : (side + 1) * LANES
                ]
    for u in range(n_u):
        summed = jnp.dot(
            w_ref[...], outer_scr[:, u * fold * LANES : (u + 1) * fold * LANES], preferred_element_type=jnp.float32
        )
        for residue in range(fold):
            piece = summed[:, residue * LANES : (residue + 1) * LANES].T
            piece = (piece / total + offset[...]).astype(jnp.bfloat16)
            for turn in range(LANES // half):
                staged[u, turn * fold + residue, pl.ds(block * half, half), :] = piece[
                    turn * half : (turn + 1) * half
                ]


def start_out(plan, u_base, staged, out_ref, sems):
    n_col = plan["n_col"]
    col = lax.axis_index("col")
    copies = []
    for u in range(staged.shape[0]):
        step = u_base + u
        source = partner(col, step, n_col) if n_col & (n_col - 1) == 0 else (col - step + n_col) % n_col
        copies.append(pltpu.make_async_copy(staged.at[u], out_ref.at[source], sems.at[step]))
        copies[-1].start()
    return copies


def near_kernel(plan, offset, w_ref, own_ref, other_ref, solo_ref, *refs):
    z_refs, (other_in, staged, weights_out, left_scr, outer_scr) = refs[:-5], refs[-5:]
    chans, part, own, n_s = plan["chans"], plan["part"], plan["own"], plan["n_s"]
    n_right = part * plan["n_res"]
    half = LANES // 2
    pairs = chans // 2
    mine = pl.multiple_of(lax.axis_index("seq") * own, own)

    def rows_of(ref, at):
        return ref[pl.ds(at, own), :].astype(jnp.float32)

    start = pl.multiple_of(n_right + lax.axis_index("res") * part + mine, own)
    rights = [(own_ref, 0), (other_ref, 0), (solo_ref, 0), (other_in, 0)]
    lefts = [rows_of(own_ref, start), rows_of(other_ref, start)]
    lefts += [rows_of(solo_ref, pl.multiple_of(n_right + mine, own)), rows_of(other_in, n_right)]
    at = n_right + own
    for ref in z_refs:
        rights += [(ref, 0), (ref, n_right), (other_in, at + n_right), (other_in, at)]
        lefts += [rows_of(ref, pl.multiple_of(2 * n_right + h * part + mine, own)) for h in range(2)]
        lefts += [rows_of(other_in, at + 2 * n_right + (1 - h) * own) for h in range(2)]
        at += 2 * (n_right + own)
    fill_left(left_scr, 0, lefts, n_s)
    depth = left_scr.shape[1]

    def block_of_columns(block):
        at_block = block * pairs * n_s
        slabs = [ref[pl.ds(at + at_block, pairs * n_s), :].astype(jnp.float32) for ref, at in rights]

        def weight_of(pair):
            here = jnp.concatenate([slab[pair * n_s : (pair + 1) * n_s] for slab in slabs], axis=0)
            there = pltpu.roll(here, half, 1)
            low = lane_index(here.shape) < half
            weights = jnp.concatenate(
                [
                    jnp.concatenate([jnp.where(low, here, 0.0), jnp.where(low, 0.0, there)], axis=0),
                    jnp.concatenate([jnp.where(low, there, 0.0), jnp.where(low, 0.0, here)], axis=0),
                ],
                axis=1,
            ).astype(jnp.bfloat16)
            weights_out[pl.ds((block * pairs + pair) * depth, depth), :] = weights
            return weights

        update_block(plan, block, offset, w_ref, weight_of, left_scr, outer_scr, staged)

    loop_blocks(n_right // (pairs * n_s), block_of_columns)


def far_kernel(plan, offset_ref, w_ref, weights_ref, near_ref, *refs):
    x_refs, (other_in, out_ref, left_scr, outer_scr, staged, sems) = refs[:-6], refs[-6:]
    chans, part, own, n_s, n_res = plan["chans"], plan["part"], plan["own"], plan["n_s"], plan["n_res"]
    pairs = chans // 2
    me = lax.axis_index("seq")
    copies = start_out(plan, 0, near_ref, out_ref, sems)

    def rows_of(ref, at):
        return ref[pl.ds(at, own), :].astype(jnp.float32)

    def pick(first, second):
        return [jnp.where(me == 0, a, b) for a, b in zip(first, second)]

    x_pairs = plan["x_pairs"]
    for u in range(plan["n_col"] - 1):
        chunks = [None] * n_res
        for k, (first, second) in enumerate(x_pairs):
            place = u * len(x_pairs) + k
            heard = [rows_of(x_refs[place], pl.multiple_of(h * part + me * own, own)) for h in range(2)]
            told = [rows_of(other_in, (2 * place + 1 - h) * own) for h in range(2)]
            chunks[first], chunks[second] = pick(heard, told), pick(told, heard)
        order = chunks[0] + chunks[plan["solo"]]
        for first, second in plan["z_pairs"]:
            order += pick(chunks[first], chunks[second]) + pick(chunks[second], chunks[first])
        fill_left(left_scr, u, order, n_s)
    depth = left_scr.shape[1]

    def block_of_columns(block):
        def weight_of(pair):
            return weights_ref[pl.ds((block * pairs + pair) * depth, depth), :]

        update_block(plan, block, offset_ref, w_ref, weight_of, left_scr, outer_scr, staged)

    loop_blocks(weights_ref.shape[0] // (pairs * depth), block_of_columns)
    copies += start_out(plan, 1, staged, out_ref, sems)
    for copy in copies:
        copy.wait()


def per_device(alignment, scale, shift, w1, b1, w2, b2, w_final, offset):
    n_s, span, width = alignment.shape
    n_res, n_col, n_seq = lax.axis_size("res"), lax.axis_size("col"), lax.axis_size("seq")
    chans, pair_width = w1.shape[1], w_final.shape[1]
    bf16 = jnp.bfloat16
    n_right = span * chans * n_s // LANES
    n_left = span * chans * n_s // LANES
    part = n_left // n_res
    own = part // n_seq
    rows_dev = span // (n_res * n_seq)
    params = pltpu.CompilerParams(vmem_limit_bytes=32 * 1024 * 1024)

    def rows(n):
        return jax.ShapeDtypeStruct((n, LANES), bf16)

    solo = n_res - 1
    z_pairs = [(k, k + 1) for k in range(1, solo, 2)]
    x_pairs = [(k, k + 1) for k in range(n_res - 2, -1, -2)]

    taken = (alignment, scale.reshape(1, -1), shift.reshape(1, -1), w1.T, b1.reshape(1, -1), w2.T, b2.reshape(1, -1))
    slab, solo_out = pl.pallas_call(
        functools.partial(project_kernel, n_res, solo),
        out_shape=[rows(n_right + n_left), rows(n_right + part)],
        in_specs=[HBM] * len(taken),
        out_specs=[VMEM] * 2,
        scratch_shapes=[pltpu.VMEM(a.shape, a.dtype) for a in taken]
        + [
            pltpu.VMEM((n_s * span, LANES), jnp.float32),
            pltpu.VMEM((n_left, LANES), jnp.float32),
            pltpu.VMEM((n_right, LANES), jnp.float32),
            pltpu.SemaphoreType.DMA((len(taken),)),
        ],
        compiler_params=params,
        name="project",
    )(*[pltpu.with_memory_space_constraint(a, pltpu.HBM) for a in taken])

    def to_core(array):
        return lax.ppermute(array, "seq", [(q, 1 - q) for q in range(n_seq)])

    def to_chip(array, step_col, steps):
        route = []
        for r in range(n_res):
            for c in range(n_col):
                for q in range(n_seq):
                    to = partner(r, steps[q], n_res) * n_col + partner(c, step_col, n_col)
                    route.append(((r * n_col + c) * n_seq + q, to * n_seq + q))
        return lax.ppermute(array, ("res", "col", "seq"), route)

    slab_in = to_core(slab)
    solo_in = to_chip(solo_out, 0, (solo, solo))
    sends = [(0, steps) for steps in z_pairs] + [(u, steps) for u in range(1, n_col) for steps in x_pairs]
    messages = pl.pallas_call(
        functools.partial(chip_kernel, n_res, [steps for _, steps in sends]),
        out_shape=[rows(2 * part + (0 if u else 2 * n_right)) for u, _ in sends],
        in_specs=[VMEM] * 2,
        out_specs=[VMEM] * len(sends),
        compiler_params=params,
        name="chip",
    )(slab, slab_in)
    heard = [to_chip(message, u, steps) for message, (u, steps) in zip(messages, sends)]

    def pack(arrays, bodies, flops, after=()):
        return pl.pallas_call(
            functools.partial(core_kernel, bodies, part, own),
            out_shape=rows(sum(b + (a.shape[0] - b) // part * own for a, b in zip(arrays, bodies))),
            in_specs=[VMEM] * (len(arrays) + len(after)),
            out_specs=VMEM,
            compiler_params=params,
            cost_estimate=pl.CostEstimate(flops=flops, bytes_accessed=0, transcendentals=0),
            name="core",
        )(*arrays, *after)

    z_in, x_in = heard[: len(z_pairs)], heard[len(z_pairs) :]
    arrays = [pack([solo_in], [n_right], 500_000_000)] + z_in
    offset = offset.reshape(1, -1)
    weights, offset = pl.pallas_call(
        weight_kernel,
        out_shape=[
            jax.ShapeDtypeStruct((pair_width, chans * chans), bf16),
            jax.ShapeDtypeStruct(offset.shape, offset.dtype),
        ],
        in_specs=[VMEM] * 3,
        out_specs=[VMEM] * 2,
        scratch_shapes=[pltpu.VMEM((chans * chans, pair_width), jnp.float32)],
        compiler_params=params,
        name="weights",
    )(w_final, offset, arrays[0])
    other_z = to_core(pack(arrays, [n_right + own] + [2 * n_right] * len(z_in), 0))
    other_x = to_core(pack(x_in, [0] * len(x_in), 20_000_000_000, (weights,)))

    turns = rows_dev * chans // LANES
    depth = turns * n_s * n_res * n_seq
    plan = dict(n_res=n_res, n_col=n_col, chans=chans, part=part, own=own, n_s=n_s, total=float(n_s * n_res * n_seq))
    plan.update(solo=solo, z_pairs=z_pairs, x_pairs=x_pairs)
    n_blocks = n_right // (chans // 2 * n_s)

    def scratch(n_u):
        return [
            pltpu.VMEM((n_u * LANES, depth), bf16),
            pltpu.VMEM((chans * chans, n_u * (LANES // chans) * LANES), bf16),
        ]

    def rows_type(n_u):
        return jax.ShapeDtypeStruct((n_u, rows_dev, span, pair_width), bf16)

    operands = (offset, weights, slab, slab_in, solo_in, *z_in, other_z)
    near, spread = pl.pallas_call(
        functools.partial(near_kernel, plan),
        out_shape=[
            rows_type(1),
            jax.ShapeDtypeStruct((n_blocks * chans // 2 * depth, 2 * LANES), bf16),
        ],
        in_specs=[VMEM] * len(operands),
        out_specs=[VMEM] * 2,
        scratch_shapes=scratch(1),
        compiler_params=params,
        name="near",
    )(*operands)
    operands = (offset, weights, spread, near, *x_in, other_x)
    return pl.pallas_call(
        functools.partial(far_kernel, plan),
        out_shape=rows_type(n_col),
        in_specs=[VMEM] * len(operands),
        out_specs=HBM,
        scratch_shapes=scratch(n_col - 1)
        + [pltpu.VMEM((n_col - 1, rows_dev, span, pair_width), bf16), pltpu.SemaphoreType.DMA((n_col,))],
        compiler_params=params,
        name="far",
    )(*operands)


def solution(mesh):
    return jax.shard_map(
        per_device,
        mesh=mesh,
        in_specs=(P(("groups", "res", "seq"), "col", None), P(), P(), P(), P(), P(), P(), P(), P()),
        out_specs=P("groups", ("res", "seq"), "col", None),
        check_vma=False,
    )
```

```python
import functools

import jax
import jax.numpy as jnp
from jax import lax
from jax.experimental import pallas as pl
from jax.experimental.pallas import tpu as pltpu
from jax.sharding import PartitionSpec as P

LANES = 128
SUBLANES = 8
VMEM = pl.BlockSpec(memory_space=pltpu.VMEM)
HBM = pl.BlockSpec(memory_space=pltpu.HBM)
ACROSS = (((1,), (1,)), ((), ()))


def partner(index, step, size):
    return index ^ step if size & (size - 1) == 0 else (index + step) % size


def lane_index(shape):
    return lax.broadcasted_iota(jnp.int32, shape, len(shape) - 1)


def project_kernel(n_res, solo, *refs):
    n_in = 7
    sources, (slab_out, solo_out), scratch = refs[:n_in], refs[n_in : -n_in - 4], refs[-n_in - 4 :]
    landed, (rows_scr, lane_scr, right_scr, sems) = scratch[:n_in], scratch[n_in:]
    copies = [pltpu.make_async_copy(a, b, sems.at[i]) for i, (a, b) in enumerate(zip(sources, landed))]
    for copy in copies:
        copy.start()
    for copy in copies:
        copy.wait()
    x_ref, scale_ref, shift_ref, w1_ref, b1_ref, w2_ref, b2_ref = landed
    n_s, span, width = x_ref.shape
    chans = w1_ref.shape[0]
    fold = LANES // chans
    half = LANES // 2
    x = x_ref[...].reshape(n_s * span, width).astype(jnp.float32)
    mean = jnp.mean(x, axis=-1, keepdims=True)
    centred = x - mean
    variance = jnp.mean(centred * centred, axis=-1, keepdims=True)
    normed = (centred * lax.rsqrt(variance + 1e-05) * scale_ref[...] + shift_ref[...]).astype(jnp.bfloat16)

    w1 = jnp.concatenate([w1_ref[...]] * fold, axis=0)
    b1 = jnp.concatenate([b1_ref[...]] * fold, axis=1)
    rows_scr[...] = lax.dot_general(normed, w1, ACROSS, preferred_element_type=jnp.float32) + b1
    n_rows = n_s * span // fold
    owner = lane_index((n_rows, LANES)) // chans
    merged = rows_scr[pl.ds(0, n_rows, stride=fold), :]
    for turn in range(1, fold):
        merged = jnp.where(owner == turn, rows_scr[pl.ds(turn, n_rows, stride=fold), :], merged)
    groups = span // fold
    for s in range(n_s):
        lane_scr[pl.ds(s, groups, stride=n_s), :] = merged[s * groups : (s + 1) * groups]

    eye = lax.broadcasted_iota(jnp.int32, (chans, chans), 0) == lane_index((chans, chans))
    b2 = jnp.sum(jnp.where(eye, b2_ref[...], 0.0), axis=1, keepdims=True)
    right = lax.dot_general(w2_ref[...], normed, ACROSS, preferred_element_type=jnp.float32) + b2
    pairs = chans // 2
    low = lane_index((pairs, LANES)) < half
    blocks = span // half
    for tile in range(n_s * span // LANES):
        here = right[:, tile * LANES : (tile + 1) * LANES]
        there = pltpu.roll(here, half, 1)
        for side in range(2):
            s, block = divmod(2 * tile + side, blocks)
            first, second = (here, there) if side == 0 else (there, here)
            right_scr[pl.ds(block * pairs * n_s + s, pairs, stride=n_s), :] = jnp.where(
                low, first[:pairs], second[pairs:]
            )
    right_slab = right_scr[...].astype(jnp.bfloat16)
    n_right, n_left = right_scr.shape[0], lane_scr.shape[0]
    part = n_left // n_res
    slab_out[:n_right] = right_slab
    slab_out[n_right:] = lane_scr[...].astype(jnp.bfloat16)
    to = partner(lax.axis_index("res"), solo, n_res)
    solo_out[:n_right] = right_slab
    solo_out[n_right:] = lane_scr[pl.ds(pl.multiple_of(to * part, part), part), :].astype(jnp.bfloat16)


def chip_kernel(n_res, steps, own_ref, other_ref, *outs):
    n_right = own_ref.shape[0] // 2
    part = n_right // n_res
    me, here = lax.axis_index("seq"), lax.axis_index("res")
    for (first, second), out in zip(steps, outs):
        to = partner(here, jnp.where(me == 0, first, second), n_res)
        start = pl.multiple_of(n_right + to * part, part)
        at = out.shape[0] - 2 * part
        if at:
            out[:n_right] = own_ref[:n_right]
            out[n_right:at] = other_ref[:n_right]
        out[at : at + part] = own_ref[pl.ds(start, part), :]
        out[at + part :] = other_ref[pl.ds(start, part), :]


def core_kernel(bodies, part, own, *refs):
    ins, out = refs[: len(bodies)], refs[-1]
    mine = (1 - lax.axis_index("seq")) * own
    at = 0
    for body, ref in zip(bodies, ins):
        if body:
            out[at : at + body] = ref[:body]
            at += body
        for start in range(body, ref.shape[0], part):
            out[at : at + own] = ref[pl.ds(pl.multiple_of(start + mine, own), own), :]
            at += own


def weight_kernel(w_ref, offset_ref, _, out_ref, offset_out, scr):
    chans_sq, width = w_ref.shape
    chans = int(round(chans_sq**0.5))
    offset_out[...] = offset_ref[...]
    scr[...] = w_ref[...].astype(jnp.float32)
    pairs = chans // 2
    fold = LANES // chans
    order = [side * pairs + pair for pair in range(pairs) for side in range(2)]
    for tile in range(chans // fold):
        piece = jnp.concatenate(
            [scr[pl.ds(e, chans, stride=chans), :] for e in order[tile * fold : (tile + 1) * fold]], axis=0
        )
        out_ref[:, tile * LANES : (tile + 1) * LANES] = piece.T.astype(jnp.bfloat16)


def fill_left(left_scr, u, slabs, n_s):
    turns = slabs[0].shape[0] // n_s
    for turn in range(turns):
        column = jnp.concatenate([slab[turn * n_s : (turn + 1) * n_s] for slab in slabs], axis=0)
        depth = column.shape[0]
        left_scr[u * LANES : (u + 1) * LANES, turn * depth : (turn + 1) * depth] = column.T.astype(jnp.bfloat16)


def loop_blocks(n_blocks, body):
    if n_blocks == 1:
        body(0)
    else:
        pl.loop(0, n_blocks)(body)


def update_block(plan, block, offset, w_ref, weight_of, left_scr, outer_scr, staged):
    chans, total = plan["chans"], plan["total"]
    half = LANES // 2
    fold = LANES // chans
    left = left_scr[...]
    n_u = left.shape[0] // LANES
    for pair in range(chans // 2):
        outer = jnp.dot(left, weight_of(pair), preferred_element_type=jnp.float32).astype(jnp.bfloat16)
        for side in range(2):
            at = (2 * pair + side) * chans
            for tile in range(n_u * fold):
                outer_scr[at : at + chans, tile * LANES : (tile + 1) * LANES] = outer[
                    tile * chans : (tile + 1) * chans, side * LANES : (side + 1) * LANES
                ]
    for u in range(n_u):
        summed = jnp.dot(
            w_ref[...], outer_scr[:, u * fold * LANES : (u + 1) * fold * LANES], preferred_element_type=jnp.float32
        )
        for residue in range(fold):
            piece = summed[:, residue * LANES : (residue + 1) * LANES].T
            piece = (piece / total + offset[...]).astype(jnp.bfloat16)
            for turn in range(LANES // half):
                staged[u, turn * fold + residue, pl.ds(block * half, half), :] = piece[
                    turn * half : (turn + 1) * half
                ]


def start_out(plan, u_base, staged, out_ref, sems):
    n_col = plan["n_col"]
    col = lax.axis_index("col")
    copies = []
    for u in range(staged.shape[0]):
        step = u_base + u
        source = partner(col, step, n_col) if n_col & (n_col - 1) == 0 else (col - step + n_col) % n_col
        copies.append(pltpu.make_async_copy(staged.at[u], out_ref.at[source], sems.at[step]))
        copies[-1].start()
    return copies


def near_kernel(plan, offset, w_ref, own_ref, other_ref, solo_ref, *refs):
    z_refs, (other_in, staged, weights_out, left_scr, outer_scr) = refs[:-5], refs[-5:]
    chans, part, own, n_s = plan["chans"], plan["part"], plan["own"], plan["n_s"]
    n_right = part * plan["n_res"]
    half = LANES // 2
    pairs = chans // 2
    mine = pl.multiple_of(lax.axis_index("seq") * own, own)

    def rows_of(ref, at):
        return ref[pl.ds(at, own), :].astype(jnp.float32)

    start = pl.multiple_of(n_right + lax.axis_index("res") * part + mine, own)
    rights = [(own_ref, 0), (other_ref, 0), (solo_ref, 0), (other_in, 0)]
    lefts = [rows_of(own_ref, start), rows_of(other_ref, start)]
    lefts += [rows_of(solo_ref, pl.multiple_of(n_right + mine, own)), rows_of(other_in, n_right)]
    at = n_right + own
    for ref in z_refs:
        rights += [(ref, 0), (ref, n_right), (other_in, at + n_right), (other_in, at)]
        lefts += [rows_of(ref, pl.multiple_of(2 * n_right + h * part + mine, own)) for h in range(2)]
        lefts += [rows_of(other_in, at + 2 * n_right + (1 - h) * own) for h in range(2)]
        at += 2 * (n_right + own)
    fill_left(left_scr, 0, lefts, n_s)
    depth = left_scr.shape[1]

    def block_of_columns(block):
        at_block = block * pairs * n_s
        slabs = [ref[pl.ds(at + at_block, pairs * n_s), :].astype(jnp.float32) for ref, at in rights]

        def weight_of(pair):
            here = jnp.concatenate([slab[pair * n_s : (pair + 1) * n_s] for slab in slabs], axis=0)
            there = pltpu.roll(here, half, 1)
            low = lane_index(here.shape) < half
            weights = jnp.concatenate(
                [
                    jnp.concatenate([jnp.where(low, here, 0.0), jnp.where(low, 0.0, there)], axis=0),
                    jnp.concatenate([jnp.where(low, there, 0.0), jnp.where(low, 0.0, here)], axis=0),
                ],
                axis=1,
            ).astype(jnp.bfloat16)
            weights_out[pl.ds((block * pairs + pair) * depth, depth), :] = weights
            return weights

        update_block(plan, block, offset, w_ref, weight_of, left_scr, outer_scr, staged)

    loop_blocks(n_right // (pairs * n_s), block_of_columns)


def far_kernel(plan, offset_ref, w_ref, weights_ref, near_ref, *refs):
    x_refs, (other_in, out_ref, left_scr, outer_scr, staged, sems) = refs[:-6], refs[-6:]
    chans, part, own, n_s, n_res = plan["chans"], plan["part"], plan["own"], plan["n_s"], plan["n_res"]
    pairs = chans // 2
    me = lax.axis_index("seq")
    copies = start_out(plan, 0, near_ref, out_ref, sems)

    def rows_of(ref, at):
        return ref[pl.ds(at, own), :].astype(jnp.float32)

    def pick(first, second):
        return [jnp.where(me == 0, a, b) for a, b in zip(first, second)]

    x_pairs = plan["x_pairs"]
    for u in range(plan["n_col"] - 1):
        chunks = [None] * n_res
        for k, (first, second) in enumerate(x_pairs):
            place = u * len(x_pairs) + k
            heard = [rows_of(x_refs[place], pl.multiple_of(h * part + me * own, own)) for h in range(2)]
            told = [rows_of(other_in, (2 * place + 1 - h) * own) for h in range(2)]
            chunks[first], chunks[second] = pick(heard, told), pick(told, heard)
        order = chunks[0] + chunks[plan["solo"]]
        for first, second in plan["z_pairs"]:
            order += pick(chunks[first], chunks[second]) + pick(chunks[second], chunks[first])
        fill_left(left_scr, u, order, n_s)
    depth = left_scr.shape[1]

    def block_of_columns(block):
        def weight_of(pair):
            return weights_ref[pl.ds((block * pairs + pair) * depth, depth), :]

        update_block(plan, block, offset_ref, w_ref, weight_of, left_scr, outer_scr, staged)

    loop_blocks(weights_ref.shape[0] // (pairs * depth), block_of_columns)
    copies += start_out(plan, 1, staged, out_ref, sems)
    for copy in copies:
        copy.wait()


def per_device(alignment, scale, shift, w1, b1, w2, b2, w_final, offset):
    n_s, span, width = alignment.shape
    n_res, n_col, n_seq = lax.axis_size("res"), lax.axis_size("col"), lax.axis_size("seq")
    chans, pair_width = w1.shape[1], w_final.shape[1]
    bf16 = jnp.bfloat16
    n_right = span * chans * n_s // LANES
    n_left = span * chans * n_s // LANES
    part = n_left // n_res
    own = part // n_seq
    rows_dev = span // (n_res * n_seq)
    params = pltpu.CompilerParams(vmem_limit_bytes=32 * 1024 * 1024)

    def rows(n):
        return jax.ShapeDtypeStruct((n, LANES), bf16)

    solo = n_res // 2
    others = [k for k in range(n_res - 1, 0, -1) if k != solo]
    z_pairs = list(zip(others[::2], others[1::2]))
    x_pairs = [(k, k + 1) for k in range(n_res - 2, -1, -2)]

    taken = (alignment, scale.reshape(1, -1), shift.reshape(1, -1), w1.T, b1.reshape(1, -1), w2.T, b2.reshape(1, -1))
    slab, solo_out = pl.pallas_call(
        functools.partial(project_kernel, n_res, solo),
        out_shape=[rows(n_right + n_left), rows(n_right + part)],
        in_specs=[HBM] * len(taken),
        out_specs=[VMEM] * 2,
        scratch_shapes=[pltpu.VMEM(a.shape, a.dtype) for a in taken]
        + [
            pltpu.VMEM((n_s * span, LANES), jnp.float32),
            pltpu.VMEM((n_left, LANES), jnp.float32),
            pltpu.VMEM((n_right, LANES), jnp.float32),
            pltpu.SemaphoreType.DMA((len(taken),)),
        ],
        compiler_params=params,
        name="project",
    )(*[pltpu.with_memory_space_constraint(a, pltpu.HBM) for a in taken])

    def to_core(array):
        return lax.ppermute(array, "seq", [(q, 1 - q) for q in range(n_seq)])

    def to_chip(array, step_col, steps):
        route = []
        for r in range(n_res):
            for c in range(n_col):
                for q in range(n_seq):
                    to = partner(r, steps[q], n_res) * n_col + partner(c, step_col, n_col)
                    route.append(((r * n_col + c) * n_seq + q, to * n_seq + q))
        return lax.ppermute(array, ("res", "col", "seq"), route)

    slab_in = to_core(slab)
    solo_in = to_chip(solo_out, 0, (solo, solo))
    sends = [(0, steps) for steps in z_pairs] + [(u, steps) for u in range(1, n_col) for steps in x_pairs]
    messages = pl.pallas_call(
        functools.partial(chip_kernel, n_res, [steps for _, steps in sends]),
        out_shape=[rows(2 * part + (0 if u else 2 * n_right)) for u, _ in sends],
        in_specs=[VMEM] * 2,
        out_specs=[VMEM] * len(sends),
        compiler_params=params,
        name="chip",
    )(slab, slab_in)
    heard = [to_chip(message, u, steps) for message, (u, steps) in zip(messages, sends)]

    def pack(arrays, bodies, flops, after=()):
        return pl.pallas_call(
            functools.partial(core_kernel, bodies, part, own),
            out_shape=rows(sum(b + (a.shape[0] - b) // part * own for a, b in zip(arrays, bodies))),
            in_specs=[VMEM] * (len(arrays) + len(after)),
            out_specs=VMEM,
            compiler_params=params,
            cost_estimate=pl.CostEstimate(flops=flops, bytes_accessed=0, transcendentals=0),
            name="core",
        )(*arrays, *after)

    z_in, x_in = heard[: len(z_pairs)], heard[len(z_pairs) :]
    arrays = [pack([solo_in], [n_right], 500_000_000)] + z_in
    offset = offset.reshape(1, -1)
    weights, offset = pl.pallas_call(
        weight_kernel,
        out_shape=[
            jax.ShapeDtypeStruct((pair_width, chans * chans), bf16),
            jax.ShapeDtypeStruct(offset.shape, offset.dtype),
        ],
        in_specs=[VMEM] * 3,
        out_specs=[VMEM] * 2,
        scratch_shapes=[pltpu.VMEM((chans * chans, pair_width), jnp.float32)],
        compiler_params=params,
        name="weights",
    )(w_final, offset, arrays[0])
    other_z = to_core(pack(arrays, [n_right + own] + [2 * n_right] * len(z_in), 0))
    other_x = to_core(pack(x_in, [0] * len(x_in), 20_000_000_000, (weights,)))

    turns = rows_dev * chans // LANES
    depth = turns * n_s * n_res * n_seq
    plan = dict(n_res=n_res, n_col=n_col, chans=chans, part=part, own=own, n_s=n_s, total=float(n_s * n_res * n_seq))
    plan.update(solo=solo, z_pairs=z_pairs, x_pairs=x_pairs)
    n_blocks = n_right // (chans // 2 * n_s)

    def scratch(n_u):
        return [
            pltpu.VMEM((n_u * LANES, depth), bf16),
            pltpu.VMEM((chans * chans, n_u * (LANES // chans) * LANES), bf16),
        ]

    def rows_type(n_u):
        return jax.ShapeDtypeStruct((n_u, rows_dev, span, pair_width), bf16)

    operands = (offset, weights, slab, slab_in, solo_in, *z_in, other_z)
    near, spread = pl.pallas_call(
        functools.partial(near_kernel, plan),
        out_shape=[
            rows_type(1),
            jax.ShapeDtypeStruct((n_blocks * chans // 2 * depth, 2 * LANES), bf16),
        ],
        in_specs=[VMEM] * len(operands),
        out_specs=[VMEM] * 2,
        scratch_shapes=scratch(1),
        compiler_params=params,
        name="near",
    )(*operands)
    operands = (offset, weights, spread, near, *x_in, other_x)
    return pl.pallas_call(
        functools.partial(far_kernel, plan),
        out_shape=rows_type(n_col),
        in_specs=[VMEM] * len(operands),
        out_specs=HBM,
        scratch_shapes=scratch(n_col - 1)
        + [pltpu.VMEM((n_col - 1, rows_dev, span, pair_width), bf16), pltpu.SemaphoreType.DMA((n_col,))],
        compiler_params=params,
        name="far",
    )(*operands)


def solution(mesh):
    return jax.shard_map(
        per_device,
        mesh=mesh,
        in_specs=(P(("groups", "res", "seq"), "col", None), P(), P(), P(), P(), P(), P(), P(), P()),
        out_specs=P("groups", ("res", "seq"), "col", None),
        check_vma=False,
    )
```

```python
import functools
import math

import jax
import jax.numpy as jnp
from jax import lax
from jax.experimental import pallas as pl
from jax.experimental.pallas import tpu as pltpu
from jax.sharding import PartitionSpec as P

LANES = 128
SUBLANES = 8
VMEM = pl.BlockSpec(memory_space=pltpu.VMEM)
HBM = pl.BlockSpec(memory_space=pltpu.HBM)
ACROSS = (((1,), (1,)), ((), ()))


def partner(index, step, size):
    return index ^ step if size & (size - 1) == 0 else (index + step) % size


def lane_index(shape):
    return lax.broadcasted_iota(jnp.int32, shape, len(shape) - 1)


def project_kernel(n_res, solo, *refs):
    n_in, n_later = 7, 2
    sources, refs = refs[: n_in + n_later], refs[n_in + n_later :]
    (slab_out, solo_out), later = refs[:2], refs[2 : 2 + n_later]
    landed, (rows_scr, lane_scr, right_scr, sems) = refs[2 + n_later : -4], refs[-4:]
    copies = [
        pltpu.make_async_copy(a, b, sems.at[i]) for i, (a, b) in enumerate(zip(sources, (*landed, *later)))
    ]
    for copy in copies:
        copy.start()
    for copy in copies[:n_in]:
        copy.wait()
    x_ref, scale_ref, shift_ref, w1_ref, b1_ref, w2_ref, b2_ref = landed
    n_s, span, width = x_ref.shape
    chans = w1_ref.shape[0]
    fold = LANES // chans
    half = LANES // 2
    x = x_ref[...].reshape(n_s * span, width).astype(jnp.float32)
    mean = jnp.mean(x, axis=-1, keepdims=True)
    centred = x - mean
    variance = jnp.mean(centred * centred, axis=-1, keepdims=True)
    normed = (centred * lax.rsqrt(variance + 1e-05) * scale_ref[...] + shift_ref[...]).astype(jnp.bfloat16)

    w1 = jnp.concatenate([w1_ref[...]] * fold, axis=0)
    b1 = jnp.concatenate([b1_ref[...]] * fold, axis=1)
    rows_scr[...] = lax.dot_general(normed, w1, ACROSS, preferred_element_type=jnp.float32) + b1
    n_rows = n_s * span // fold
    owner = lane_index((n_rows, LANES)) // chans
    merged = rows_scr[pl.ds(0, n_rows, stride=fold), :]
    for turn in range(1, fold):
        merged = jnp.where(owner == turn, rows_scr[pl.ds(turn, n_rows, stride=fold), :], merged)
    groups = span // fold
    for s in range(n_s):
        lane_scr[pl.ds(s, groups, stride=n_s), :] = merged[s * groups : (s + 1) * groups]

    eye = lax.broadcasted_iota(jnp.int32, (chans, chans), 0) == lane_index((chans, chans))
    b2 = jnp.sum(jnp.where(eye, b2_ref[...], 0.0), axis=1, keepdims=True)
    right = lax.dot_general(w2_ref[...], normed, ACROSS, preferred_element_type=jnp.float32) + b2
    pairs = chans // 2
    low = lane_index((pairs, LANES)) < half
    blocks = span // half
    for tile in range(n_s * span // LANES):
        here = right[:, tile * LANES : (tile + 1) * LANES]
        there = pltpu.roll(here, half, 1)
        for side in range(2):
            s, block = divmod(2 * tile + side, blocks)
            first, second = (here, there) if side == 0 else (there, here)
            right_scr[pl.ds(block * pairs * n_s + s, pairs, stride=n_s), :] = jnp.where(
                low, first[:pairs], second[pairs:]
            )
    right_slab = right_scr[...].astype(jnp.bfloat16)
    n_right, n_left = right_scr.shape[0], lane_scr.shape[0]
    part = n_left // n_res
    slab_out[:n_right] = right_slab
    slab_out[n_right:] = lane_scr[...].astype(jnp.bfloat16)
    to = partner(lax.axis_index("res"), solo, n_res)
    solo_out[:n_right] = right_slab
    solo_out[n_right:] = lane_scr[pl.ds(pl.multiple_of(to * part, part), part), :].astype(jnp.bfloat16)
    for copy in copies[n_in:]:
        copy.wait()


def chip_kernel(n_res, steps, own_ref, other_ref, *outs):
    n_right = own_ref.shape[0] // 2
    part = n_right // n_res
    me, here = lax.axis_index("seq"), lax.axis_index("res")
    for (first, second), out in zip(steps, outs):
        to = partner(here, jnp.where(me == 0, first, second), n_res)
        start = pl.multiple_of(n_right + to * part, part)
        at = out.shape[0] - 2 * part
        if at:
            out[:n_right] = own_ref[:n_right]
            out[n_right:at] = other_ref[:n_right]
        out[at : at + part] = own_ref[pl.ds(start, part), :]
        out[at + part :] = other_ref[pl.ds(start, part), :]


def core_kernel(bodies, part, own, *refs):
    ins, out = refs[: len(bodies)], refs[-1]
    mine = (1 - lax.axis_index("seq")) * own
    at = 0
    for body, ref in zip(bodies, ins):
        if body:
            out[at : at + body] = ref[:body]
            at += body
        for start in range(body, ref.shape[0], part):
            out[at : at + own] = ref[pl.ds(pl.multiple_of(start + mine, own), own), :]
            at += own


def weight_kernel(w_ref, _, out_ref, scr):
    chans_sq, width = w_ref.shape
    chans = int(round(chans_sq**0.5))
    scr[...] = w_ref[...].astype(jnp.float32)
    pairs = chans // 2
    fold = LANES // chans
    order = [side * pairs + pair for pair in range(pairs) for side in range(2)]
    for tile in range(chans // fold):
        piece = jnp.concatenate(
            [scr[pl.ds(e, chans, stride=chans), :] for e in order[tile * fold : (tile + 1) * fold]], axis=0
        )
        out_ref[:, tile * LANES : (tile + 1) * LANES] = piece.T.astype(jnp.bfloat16)


def fill_left(left_scr, u, slabs, n_s):
    turns = slabs[0].shape[0] // n_s
    for turn in range(turns):
        column = jnp.concatenate([slab[turn * n_s : (turn + 1) * n_s] for slab in slabs], axis=0)
        depth = column.shape[0]
        left_scr[u * LANES : (u + 1) * LANES, turn * depth : (turn + 1) * depth] = column.T.astype(jnp.bfloat16)


def loop_blocks(n_blocks, body):
    if n_blocks == 1:
        body(0)
    else:
        pl.loop(0, n_blocks)(body)


def update_block(plan, block, offset, w_ref, weight_of, left_scr, outer_scr, staged, finish=None):
    chans, total = plan["chans"], plan["total"]
    half = LANES // 2
    fold = LANES // chans
    left = left_scr[...]
    n_u = left.shape[0] // LANES
    for pair in range(chans // 2):
        outer = jnp.dot(left, weight_of(pair), preferred_element_type=jnp.float32).astype(jnp.bfloat16)
        for side in range(2):
            at = (2 * pair + side) * chans
            for tile in range(n_u * fold):
                outer_scr[at : at + chans, tile * LANES : (tile + 1) * LANES] = outer[
                    tile * chans : (tile + 1) * chans, side * LANES : (side + 1) * LANES
                ]
    inverse = 1.0 / total if math.frexp(total)[0] == 0.5 else None
    step = min(fold, 2)
    for u in range(n_u):
        for first in range(0, fold, step):
            at = (u * fold + first) * LANES
            summed = jnp.dot(
                w_ref[...], outer_scr[:, at : at + step * LANES], preferred_element_type=jnp.float32
            )
            for k in range(step):
                piece = summed[:, k * LANES : (k + 1) * LANES].T
                piece = piece / total if inverse is None else piece * inverse
                piece = (piece + offset[...]).astype(jnp.bfloat16)
                for turn in range(LANES // half):
                    staged[u, turn * fold + first + k, pl.ds(block * half, half), :] = piece[
                        turn * half : (turn + 1) * half
                    ]
            if finish is not None:
                for turn in range(LANES // half):
                    finish(u, turn * fold + first, step)


def row_copy(plan, step, staged, out_ref, sem):
    n_col = plan["n_col"]
    col = lax.axis_index("col")
    source = partner(col, step, n_col) if n_col & (n_col - 1) == 0 else (col - step + n_col) % n_col
    row, rows = staged[1]
    return pltpu.make_async_copy(staged[0].at[pl.ds(row, rows)], out_ref.at[source, pl.ds(row, rows)], sem)


def near_kernel(plan, offset, w_ref, own_ref, other_ref, solo_ref, *refs):
    z_refs, (other_in, staged, weights_out, left_scr, outer_scr) = refs[:-5], refs[-5:]
    chans, part, own, n_s = plan["chans"], plan["part"], plan["own"], plan["n_s"]
    n_right = part * plan["n_res"]
    half = LANES // 2
    pairs = chans // 2
    mine = pl.multiple_of(lax.axis_index("seq") * own, own)

    def rows_of(ref, at):
        return ref[pl.ds(at, own), :].astype(jnp.float32)

    start = pl.multiple_of(n_right + lax.axis_index("res") * part + mine, own)
    rights = [(own_ref, 0), (other_ref, 0), (solo_ref, 0), (other_in, 0)]
    lefts = [rows_of(own_ref, start), rows_of(other_ref, start)]
    lefts += [rows_of(solo_ref, pl.multiple_of(n_right + mine, own)), rows_of(other_in, n_right)]
    at = n_right + own
    for ref in z_refs:
        rights += [(ref, 0), (ref, n_right), (other_in, at + n_right), (other_in, at)]
        lefts += [rows_of(ref, pl.multiple_of(2 * n_right + h * part + mine, own)) for h in range(2)]
        lefts += [rows_of(other_in, at + 2 * n_right + (1 - h) * own) for h in range(2)]
        at += 2 * (n_right + own)
    fill_left(left_scr, 0, lefts, n_s)
    depth = left_scr.shape[1]

    def block_of_columns(block):
        at_block = block * pairs * n_s
        slabs = [ref[pl.ds(at + at_block, pairs * n_s), :].astype(jnp.float32) for ref, at in rights]

        def weight_of(pair):
            here = jnp.concatenate([slab[pair * n_s : (pair + 1) * n_s] for slab in slabs], axis=0)
            there = pltpu.roll(here, half, 1)
            low = lane_index(here.shape) < half
            weights = jnp.concatenate(
                [
                    jnp.concatenate([jnp.where(low, here, 0.0), jnp.where(low, 0.0, there)], axis=0),
                    jnp.concatenate([jnp.where(low, there, 0.0), jnp.where(low, 0.0, here)], axis=0),
                ],
                axis=1,
            ).astype(jnp.bfloat16)
            weights_out[pl.ds((block * pairs + pair) * depth, depth), :] = weights
            return weights

        update_block(plan, block, offset, w_ref, weight_of, left_scr, outer_scr, staged)

    loop_blocks(n_right // (pairs * n_s), block_of_columns)


def far_kernel(plan, offset_ref, w_ref, weights_ref, near_ref, *refs):
    x_refs, (other_in, out_ref, left_scr, outer_scr, staged, sems) = refs[:-6], refs[-6:]
    chans, part, own, n_s, n_res = plan["chans"], plan["part"], plan["own"], plan["n_s"], plan["n_res"]
    pairs = chans // 2
    me = lax.axis_index("seq")
    rows_dev = near_ref.shape[1]
    copies = [row_copy(plan, 0, (near_ref.at[0], (0, rows_dev)), out_ref, sems.at[0, 0])]
    copies[0].start()

    def rows_of(ref, at):
        return ref[pl.ds(at, own), :].astype(jnp.float32)

    def pick(first, second):
        return [jnp.where(me == 0, a, b) for a, b in zip(first, second)]

    x_pairs = plan["x_pairs"]
    for u in range(plan["n_col"] - 1):
        chunks = [None] * n_res
        for k, (first, second) in enumerate(x_pairs):
            place = u * len(x_pairs) + k
            heard = [rows_of(x_refs[place], pl.multiple_of(h * part + me * own, own)) for h in range(2)]
            told = [rows_of(other_in, (2 * place + 1 - h) * own) for h in range(2)]
            chunks[first], chunks[second] = pick(heard, told), pick(told, heard)
        order = chunks[0] + chunks[plan["solo"]]
        for first, second in plan["z_pairs"]:
            order += pick(chunks[first], chunks[second]) + pick(chunks[second], chunks[first])
        fill_left(left_scr, u, order, n_s)
    depth = left_scr.shape[1]

    def block_of_columns(block):
        def weight_of(pair):
            return weights_ref[pl.ds((block * pairs + pair) * depth, depth), :]

        update_block(
            plan, block, offset_ref, w_ref, weight_of, left_scr, outer_scr, staged, finish if n_blocks == 1 else None
        )

    def finish(u, row, rows):
        copies.append(row_copy(plan, 1 + u, (staged.at[u], (row, rows)), out_ref, sems.at[1 + u, row]))
        copies[-1].start()

    n_blocks = weights_ref.shape[0] // (pairs * depth)
    loop_blocks(n_blocks, block_of_columns)
    if n_blocks > 1:
        for u in range(staged.shape[0]):
            finish(u, 0, rows_dev)
    for copy in copies:
        copy.wait()


def per_device(alignment, scale, shift, w1, b1, w2, b2, w_final, offset):
    n_s, span, width = alignment.shape
    n_res, n_col, n_seq = lax.axis_size("res"), lax.axis_size("col"), lax.axis_size("seq")
    chans, pair_width = w1.shape[1], w_final.shape[1]
    bf16 = jnp.bfloat16
    n_right = span * chans * n_s // LANES
    n_left = span * chans * n_s // LANES
    part = n_left // n_res
    own = part // n_seq
    rows_dev = span // (n_res * n_seq)
    params = pltpu.CompilerParams(vmem_limit_bytes=32 * 1024 * 1024)

    def rows(n):
        return jax.ShapeDtypeStruct((n, LANES), bf16)

    solo = 1
    z_pairs = [(k, k + 1) for k in range(2, n_res, 2)]
    x_pairs = [(k, k + 1) for k in range(n_res - 2, -1, -2)]

    taken = (alignment, scale.reshape(1, -1), shift.reshape(1, -1), w1.T, b1.reshape(1, -1), w2.T, b2.reshape(1, -1))
    later = (w_final, offset.reshape(1, -1))
    slab, solo_out, w_final, offset = pl.pallas_call(
        functools.partial(project_kernel, n_res, solo),
        out_shape=[rows(n_right + n_left), rows(n_right + part)]
        + [jax.ShapeDtypeStruct(a.shape, a.dtype) for a in later],
        in_specs=[HBM] * len(taken + later),
        out_specs=[VMEM] * 4,
        scratch_shapes=[pltpu.VMEM(a.shape, a.dtype) for a in taken]
        + [
            pltpu.VMEM((n_s * span, LANES), jnp.float32),
            pltpu.VMEM((n_left, LANES), jnp.float32),
            pltpu.VMEM((n_right, LANES), jnp.float32),
            pltpu.SemaphoreType.DMA((len(taken + later),)),
        ],
        compiler_params=params,
        name="project",
    )(*[pltpu.with_memory_space_constraint(a, pltpu.HBM) for a in taken + later])

    def to_core(array):
        return lax.ppermute(array, "seq", [(q, 1 - q) for q in range(n_seq)])

    def to_chip(array, step_col, steps):
        route = []
        for r in range(n_res):
            for c in range(n_col):
                for q in range(n_seq):
                    to = partner(r, steps[q], n_res) * n_col + partner(c, step_col, n_col)
                    route.append(((r * n_col + c) * n_seq + q, to * n_seq + q))
        return lax.ppermute(array, ("res", "col", "seq"), route)

    slab_in = to_core(slab)
    solo_in = to_chip(solo_out, 0, (solo, solo))
    sends = [(0, steps) for steps in z_pairs] + [(u, steps) for u in range(1, n_col) for steps in x_pairs]
    messages = pl.pallas_call(
        functools.partial(chip_kernel, n_res, [steps for _, steps in sends]),
        out_shape=[rows(2 * part + (0 if u else 2 * n_right)) for u, _ in sends],
        in_specs=[VMEM] * 2,
        out_specs=[VMEM] * len(sends),
        compiler_params=params,
        name="chip",
    )(slab, slab_in)
    heard = [to_chip(message, u, steps) for message, (u, steps) in zip(messages, sends)]

    def pack(arrays, bodies, flops, after=()):
        return pl.pallas_call(
            functools.partial(core_kernel, bodies, part, own),
            out_shape=rows(sum(b + (a.shape[0] - b) // part * own for a, b in zip(arrays, bodies))),
            in_specs=[VMEM] * (len(arrays) + len(after)),
            out_specs=VMEM,
            compiler_params=params,
            cost_estimate=pl.CostEstimate(flops=flops, bytes_accessed=0, transcendentals=0),
            name="core",
        )(*arrays, *after)

    z_in, x_in = heard[: len(z_pairs)], heard[len(z_pairs) :]
    arrays = [pack([solo_in], [n_right], 500_000_000)] + z_in
    weights = pl.pallas_call(
        weight_kernel,
        out_shape=jax.ShapeDtypeStruct((pair_width, chans * chans), bf16),
        in_specs=[VMEM] * 2,
        out_specs=VMEM,
        scratch_shapes=[pltpu.VMEM((chans * chans, pair_width), jnp.float32)],
        compiler_params=params,
        name="weights",
    )(w_final, arrays[0])
    other_z = to_core(pack(arrays, [n_right + own] + [2 * n_right] * len(z_in), 0))
    other_x = to_core(pack(x_in, [0] * len(x_in), 20_000_000_000, (weights,)))

    turns = rows_dev * chans // LANES
    depth = turns * n_s * n_res * n_seq
    plan = dict(n_res=n_res, n_col=n_col, chans=chans, part=part, own=own, n_s=n_s, total=float(n_s * n_res * n_seq))
    plan.update(solo=solo, z_pairs=z_pairs, x_pairs=x_pairs)
    n_blocks = n_right // (chans // 2 * n_s)

    def scratch(n_u):
        return [
            pltpu.VMEM((n_u * LANES, depth), bf16),
            pltpu.VMEM((chans * chans, n_u * (LANES // chans) * LANES), bf16),
        ]

    def rows_type(n_u):
        return jax.ShapeDtypeStruct((n_u, rows_dev, span, pair_width), bf16)

    operands = (offset, weights, slab, slab_in, solo_in, *z_in, other_z)
    near, spread = pl.pallas_call(
        functools.partial(near_kernel, plan),
        out_shape=[
            rows_type(1),
            jax.ShapeDtypeStruct((n_blocks * chans // 2 * depth, 2 * LANES), bf16),
        ],
        in_specs=[VMEM] * len(operands),
        out_specs=[VMEM] * 2,
        scratch_shapes=scratch(1),
        compiler_params=params,
        name="near",
    )(*operands)
    operands = (offset, weights, spread, near, *x_in, other_x)
    return pl.pallas_call(
        functools.partial(far_kernel, plan),
        out_shape=rows_type(n_col),
        in_specs=[VMEM] * len(operands),
        out_specs=HBM,
        scratch_shapes=scratch(n_col - 1)
        + [pltpu.VMEM((n_col - 1, rows_dev, span, pair_width), bf16), pltpu.SemaphoreType.DMA((n_col, rows_dev))],
        compiler_params=params,
        name="far",
    )(*operands)


def solution(mesh):
    return jax.shard_map(
        per_device,
        mesh=mesh,
        in_specs=(P(("groups", "res", "seq"), "col", None), P(), P(), P(), P(), P(), P(), P(), P()),
        out_specs=P("groups", ("res", "seq"), "col", None),
        check_vma=False,
    )
```

```python
import functools
import math

import jax
import jax.numpy as jnp
from jax import lax
from jax.experimental import pallas as pl
from jax.experimental.pallas import tpu as pltpu
from jax.sharding import PartitionSpec as P

LANES = 128
SUBLANES = 8
VMEM = pl.BlockSpec(memory_space=pltpu.VMEM)
HBM = pl.BlockSpec(memory_space=pltpu.HBM)
ACROSS = (((1,), (1,)), ((), ()))


def partner(index, step, size):
    return index ^ step if size & (size - 1) == 0 else (index + step) % size


def routes(n_res):
    def turn(k):
        return [(z + k) % n_res for z in range(n_res)]

    def swap(k):
        return [partner(z, k, n_res) for z in range(n_res)]

    solo_route = [turn(1)] * 2
    z_routes = [[turn(k), turn(k + 1)] for k in range(2, n_res, 2)]
    x_routes = [[swap(k), swap(k + 1)] for k in range(n_res - 2, -1, -2)]
    return solo_route, z_routes, x_routes


def sources(route):
    return [[to.index(z) for z in range(len(to))] for to in route]


def look_up(route, core, chip):
    found = 0
    for k, (first, second) in enumerate(zip(*route)):
        found = jnp.where(chip == k, jnp.where(core == 0, first, second), found)
    return found


def lane_index(shape):
    return lax.broadcasted_iota(jnp.int32, shape, len(shape) - 1)


def project_kernel(n_res, solo_route, *refs):
    n_in, n_later = 7, 2
    sources, refs = refs[: n_in + n_later], refs[n_in + n_later :]
    (slab_out, solo_out), later = refs[:2], refs[2 : 2 + n_later]
    landed, (rows_scr, lane_scr, right_scr, sems) = refs[2 + n_later : -4], refs[-4:]
    copies = [
        pltpu.make_async_copy(a, b, sems.at[i]) for i, (a, b) in enumerate(zip(sources, (*landed, *later)))
    ]
    for copy in copies:
        copy.start()
    for copy in copies[:n_in]:
        copy.wait()
    x_ref, scale_ref, shift_ref, w1_ref, b1_ref, w2_ref, b2_ref = landed
    n_s, span, width = x_ref.shape
    chans = w1_ref.shape[0]
    fold = LANES // chans
    half = LANES // 2
    x = x_ref[...].reshape(n_s * span, width).astype(jnp.float32)
    mean = jnp.mean(x, axis=-1, keepdims=True)
    centred = x - mean
    variance = jnp.mean(centred * centred, axis=-1, keepdims=True)
    normed = (centred * lax.rsqrt(variance + 1e-05) * scale_ref[...] + shift_ref[...]).astype(jnp.bfloat16)

    w1 = jnp.concatenate([w1_ref[...]] * fold, axis=0)
    b1 = jnp.concatenate([b1_ref[...]] * fold, axis=1)
    rows_scr[...] = lax.dot_general(normed, w1, ACROSS, preferred_element_type=jnp.float32) + b1
    n_rows = n_s * span // fold
    owner = lane_index((n_rows, LANES)) // chans
    merged = rows_scr[pl.ds(0, n_rows, stride=fold), :]
    for turn in range(1, fold):
        merged = jnp.where(owner == turn, rows_scr[pl.ds(turn, n_rows, stride=fold), :], merged)
    groups = span // fold
    for s in range(n_s):
        lane_scr[pl.ds(s, groups, stride=n_s), :] = merged[s * groups : (s + 1) * groups]

    eye = lax.broadcasted_iota(jnp.int32, (chans, chans), 0) == lane_index((chans, chans))
    b2 = jnp.sum(jnp.where(eye, b2_ref[...], 0.0), axis=1, keepdims=True)
    right = lax.dot_general(w2_ref[...], normed, ACROSS, preferred_element_type=jnp.float32) + b2
    pairs = chans // 2
    low = lane_index((pairs, LANES)) < half
    blocks = span // half
    for tile in range(n_s * span // LANES):
        here = right[:, tile * LANES : (tile + 1) * LANES]
        there = pltpu.roll(here, half, 1)
        for side in range(2):
            s, block = divmod(2 * tile + side, blocks)
            first, second = (here, there) if side == 0 else (there, here)
            right_scr[pl.ds(block * pairs * n_s + s, pairs, stride=n_s), :] = jnp.where(
                low, first[:pairs], second[pairs:]
            )
    right_slab = right_scr[...].astype(jnp.bfloat16)
    n_right, n_left = right_scr.shape[0], lane_scr.shape[0]
    part = n_left // n_res
    slab_out[:n_right] = right_slab
    slab_out[n_right:] = lane_scr[...].astype(jnp.bfloat16)
    to = look_up(solo_route, 0, lax.axis_index("res"))
    solo_out[:n_right] = right_slab
    solo_out[n_right:] = lane_scr[pl.ds(pl.multiple_of(to * part, part), part), :].astype(jnp.bfloat16)
    for copy in copies[n_in:]:
        copy.wait()


def chip_kernel(n_res, ways, own_ref, other_ref, *outs):
    n_right = own_ref.shape[0] // 2
    part = n_right // n_res
    me, here = lax.axis_index("seq"), lax.axis_index("res")
    for route, out in zip(ways, outs):
        to = look_up(route, me, here)
        start = pl.multiple_of(n_right + to * part, part)
        at = out.shape[0] - 2 * part
        if at:
            out[:n_right] = own_ref[:n_right]
            out[n_right:at] = other_ref[:n_right]
        out[at : at + part] = own_ref[pl.ds(start, part), :]
        out[at + part :] = other_ref[pl.ds(start, part), :]


def core_kernel(bodies, part, own, *refs):
    ins, out = refs[: len(bodies)], refs[-1]
    mine = (1 - lax.axis_index("seq")) * own
    at = 0
    for body, ref in zip(bodies, ins):
        if body:
            out[at : at + body] = ref[:body]
            at += body
        for start in range(body, ref.shape[0], part):
            out[at : at + own] = ref[pl.ds(pl.multiple_of(start + mine, own), own), :]
            at += own


def weight_kernel(w_ref, _, out_ref, scr):
    chans_sq, width = w_ref.shape
    chans = int(round(chans_sq**0.5))
    scr[...] = w_ref[...].astype(jnp.float32)
    pairs = chans // 2
    fold = LANES // chans
    order = [side * pairs + pair for pair in range(pairs) for side in range(2)]
    for tile in range(chans // fold):
        piece = jnp.concatenate(
            [scr[pl.ds(e, chans, stride=chans), :] for e in order[tile * fold : (tile + 1) * fold]], axis=0
        )
        out_ref[:, tile * LANES : (tile + 1) * LANES] = piece.T.astype(jnp.bfloat16)


def fill_left(left_scr, u, slabs, n_s):
    turns = slabs[0].shape[0] // n_s
    for turn in range(turns):
        column = jnp.concatenate([slab[turn * n_s : (turn + 1) * n_s] for slab in slabs], axis=0)
        depth = column.shape[0]
        left_scr[u * LANES : (u + 1) * LANES, turn * depth : (turn + 1) * depth] = column.T.astype(jnp.bfloat16)


def loop_blocks(n_blocks, body):
    if n_blocks == 1:
        body(0)
    else:
        pl.loop(0, n_blocks)(body)


def update_block(plan, block, offset, w_ref, weight_of, left_scr, outer_scr, staged):
    chans, total = plan["chans"], plan["total"]
    half = LANES // 2
    fold = LANES // chans
    left = left_scr[...]
    n_u = left.shape[0] // LANES
    for pair in range(chans // 2):
        outer = jnp.dot(left, weight_of(pair), preferred_element_type=jnp.float32).astype(jnp.bfloat16)
        for side in range(2):
            at = (2 * pair + side) * chans
            for tile in range(n_u * fold):
                outer_scr[at : at + chans, tile * LANES : (tile + 1) * LANES] = outer[
                    tile * chans : (tile + 1) * chans, side * LANES : (side + 1) * LANES
                ]
    inverse = 1.0 / total if math.frexp(total)[0] == 0.5 else None
    step = min(fold, 2)
    for u in range(n_u):
        for first in range(0, fold, step):
            at = (u * fold + first) * LANES
            summed = jnp.dot(
                w_ref[...], outer_scr[:, at : at + step * LANES], preferred_element_type=jnp.float32
            )
            for k in range(step):
                piece = summed[:, k * LANES : (k + 1) * LANES].T
                piece = piece / total if inverse is None else piece * inverse
                piece = (piece + offset[...]).astype(jnp.bfloat16)
                for turn in range(LANES // half):
                    staged[u, turn * fold + first + k, pl.ds(block * half, half), :] = piece[
                        turn * half : (turn + 1) * half
                    ]


def row_copy(plan, step, staged, out_ref, sem):
    n_col = plan["n_col"]
    col = lax.axis_index("col")
    source = partner(col, step, n_col) if n_col & (n_col - 1) == 0 else (col - step + n_col) % n_col
    return pltpu.make_async_copy(staged, out_ref.at[source], sem)


def near_kernel(plan, offset, w_ref, own_ref, other_ref, solo_ref, *refs):
    z_refs, (other_in, staged, weights_out, left_scr, outer_scr) = refs[:-5], refs[-5:]
    chans, part, own, n_s = plan["chans"], plan["part"], plan["own"], plan["n_s"]
    n_right = part * plan["n_res"]
    half = LANES // 2
    pairs = chans // 2
    mine = pl.multiple_of(lax.axis_index("seq") * own, own)

    def rows_of(ref, at):
        return ref[pl.ds(at, own), :].astype(jnp.float32)

    start = pl.multiple_of(n_right + lax.axis_index("res") * part + mine, own)
    rights = [(own_ref, 0), (other_ref, 0), (solo_ref, 0), (other_in, 0)]
    lefts = [rows_of(own_ref, start), rows_of(other_ref, start)]
    lefts += [rows_of(solo_ref, pl.multiple_of(n_right + mine, own)), rows_of(other_in, n_right)]
    at = n_right + own
    for ref in z_refs:
        rights += [(ref, 0), (ref, n_right), (other_in, at + n_right), (other_in, at)]
        lefts += [rows_of(ref, pl.multiple_of(2 * n_right + h * part + mine, own)) for h in range(2)]
        lefts += [rows_of(other_in, at + 2 * n_right + (1 - h) * own) for h in range(2)]
        at += 2 * (n_right + own)
    fill_left(left_scr, 0, lefts, n_s)
    depth = left_scr.shape[1]

    def block_of_columns(block):
        at_block = block * pairs * n_s
        slabs = [ref[pl.ds(at + at_block, pairs * n_s), :].astype(jnp.float32) for ref, at in rights]

        def weight_of(pair):
            here = jnp.concatenate([slab[pair * n_s : (pair + 1) * n_s] for slab in slabs], axis=0)
            there = pltpu.roll(here, half, 1)
            low = lane_index(here.shape) < half
            weights = jnp.concatenate(
                [
                    jnp.concatenate([jnp.where(low, here, 0.0), jnp.where(low, 0.0, there)], axis=0),
                    jnp.concatenate([jnp.where(low, there, 0.0), jnp.where(low, 0.0, here)], axis=0),
                ],
                axis=1,
            ).astype(jnp.bfloat16)
            weights_out[pl.ds((block * pairs + pair) * depth, depth), :] = weights
            return weights

        update_block(plan, block, offset, w_ref, weight_of, left_scr, outer_scr, staged)

    loop_blocks(n_right // (pairs * n_s), block_of_columns)


def far_kernel(plan, offset_ref, w_ref, weights_ref, near_ref, *refs):
    x_refs, (other_in, out_ref, left_scr, outer_scr, staged, sems) = refs[:-6], refs[-6:]
    chans, part, own, n_s, n_res = plan["chans"], plan["part"], plan["own"], plan["n_s"], plan["n_res"]
    pairs = chans // 2
    me = lax.axis_index("seq")
    copies = [row_copy(plan, 0, near_ref.at[0], out_ref, sems.at[0])]
    copies[0].start()

    def rows_of(ref, at):
        return ref[pl.ds(at, own), :].astype(jnp.float32)

    here = lax.axis_index("res")
    order = [here, look_up(sources(plan["solo"]), me, here)]
    for route in plan["z_routes"]:
        order += [look_up(sources(route), core, here) for core in (me, 1 - me)]
    x_routes = plan["x_routes"]
    for u in range(plan["n_col"] - 1):
        held = []
        for k, route in enumerate(x_routes):
            place = u * len(x_routes) + k
            heard = [rows_of(x_refs[place], pl.multiple_of(h * part + me * own, own)) for h in range(2)]
            told = [rows_of(other_in, (2 * place + 1 - h) * own) for h in range(2)]
            held += [(look_up(sources(route), me, here), heard), (look_up(sources(route), 1 - me, here), told)]
        slabs = []
        for chip in order:
            for side in range(2):
                found = held[0][1][side]
                for source, slab in held[1:]:
                    found = jnp.where(source == chip, slab[side], found)
                slabs.append(found)
        fill_left(left_scr, u, slabs, n_s)
    depth = left_scr.shape[1]

    def block_of_columns(block):
        def weight_of(pair):
            return weights_ref[pl.ds((block * pairs + pair) * depth, depth), :]

        update_block(plan, block, offset_ref, w_ref, weight_of, left_scr, outer_scr, staged)

    loop_blocks(weights_ref.shape[0] // (pairs * depth), block_of_columns)
    for u in range(staged.shape[0]):
        copies.append(row_copy(plan, 1 + u, staged.at[u], out_ref, sems.at[1 + u]))
        copies[-1].start()
    for copy in copies:
        copy.wait()


def per_device(alignment, scale, shift, w1, b1, w2, b2, w_final, offset):
    n_s, span, width = alignment.shape
    n_res, n_col, n_seq = lax.axis_size("res"), lax.axis_size("col"), lax.axis_size("seq")
    chans, pair_width = w1.shape[1], w_final.shape[1]
    bf16 = jnp.bfloat16
    n_right = span * chans * n_s // LANES
    n_left = span * chans * n_s // LANES
    part = n_left // n_res
    own = part // n_seq
    rows_dev = span // (n_res * n_seq)
    params = pltpu.CompilerParams(vmem_limit_bytes=32 * 1024 * 1024)

    def rows(n):
        return jax.ShapeDtypeStruct((n, LANES), bf16)

    solo, z_routes, x_routes = routes(n_res)

    taken = (alignment, scale.reshape(1, -1), shift.reshape(1, -1), w1.T, b1.reshape(1, -1), w2.T, b2.reshape(1, -1))
    later = (w_final, offset.reshape(1, -1))
    slab, solo_out, w_final, offset = pl.pallas_call(
        functools.partial(project_kernel, n_res, solo),
        out_shape=[rows(n_right + n_left), rows(n_right + part)]
        + [jax.ShapeDtypeStruct(a.shape, a.dtype) for a in later],
        in_specs=[HBM] * len(taken + later),
        out_specs=[VMEM] * 4,
        scratch_shapes=[pltpu.VMEM(a.shape, a.dtype) for a in taken]
        + [
            pltpu.VMEM((n_s * span, LANES), jnp.float32),
            pltpu.VMEM((n_left, LANES), jnp.float32),
            pltpu.VMEM((n_right, LANES), jnp.float32),
            pltpu.SemaphoreType.DMA((len(taken + later),)),
        ],
        compiler_params=params,
        name="project",
    )(*[pltpu.with_memory_space_constraint(a, pltpu.HBM) for a in taken + later])

    def to_core(array):
        return lax.ppermute(array, "seq", [(q, 1 - q) for q in range(n_seq)])

    def to_chip(array, step_col, route):
        pairs = []
        for r in range(n_res):
            for c in range(n_col):
                for q in range(n_seq):
                    to = route[q][r] * n_col + partner(c, step_col, n_col)
                    pairs.append(((r * n_col + c) * n_seq + q, to * n_seq + q))
        return lax.ppermute(array, ("res", "col", "seq"), pairs)

    slab_in = to_core(slab)
    solo_in = to_chip(solo_out, 0, solo)
    sends = [(0, route) for route in z_routes] + [(u, route) for u in range(1, n_col) for route in x_routes]
    messages = pl.pallas_call(
        functools.partial(chip_kernel, n_res, [route for _, route in sends]),
        out_shape=[rows(2 * part + (0 if u else 2 * n_right)) for u, _ in sends],
        in_specs=[VMEM] * 2,
        out_specs=[VMEM] * len(sends),
        compiler_params=params,
        name="chip",
    )(slab, slab_in)
    heard = [to_chip(message, u, route) for message, (u, route) in zip(messages, sends)]

    def pack(arrays, bodies, flops, after=()):
        return pl.pallas_call(
            functools.partial(core_kernel, bodies, part, own),
            out_shape=rows(sum(b + (a.shape[0] - b) // part * own for a, b in zip(arrays, bodies))),
            in_specs=[VMEM] * (len(arrays) + len(after)),
            out_specs=VMEM,
            compiler_params=params,
            cost_estimate=pl.CostEstimate(flops=flops, bytes_accessed=0, transcendentals=0),
            name="core",
        )(*arrays, *after)

    z_in, x_in = heard[: len(z_routes)], heard[len(z_routes) :]
    arrays = [pack([solo_in], [n_right], 500_000_000)] + z_in
    weights = pl.pallas_call(
        weight_kernel,
        out_shape=jax.ShapeDtypeStruct((pair_width, chans * chans), bf16),
        in_specs=[VMEM] * 2,
        out_specs=VMEM,
        scratch_shapes=[pltpu.VMEM((chans * chans, pair_width), jnp.float32)],
        compiler_params=params,
        name="weights",
    )(w_final, arrays[0])
    other_z = to_core(pack(arrays, [n_right + own] + [2 * n_right] * len(z_in), 0))
    other_x = to_core(pack(x_in, [0] * len(x_in), 20_000_000_000, (weights,)))

    turns = rows_dev * chans // LANES
    depth = turns * n_s * n_res * n_seq
    plan = dict(n_res=n_res, n_col=n_col, chans=chans, part=part, own=own, n_s=n_s, total=float(n_s * n_res * n_seq))
    plan.update(solo=solo, z_routes=z_routes, x_routes=x_routes)
    n_blocks = n_right // (chans // 2 * n_s)

    def scratch(n_u):
        return [
            pltpu.VMEM((n_u * LANES, depth), bf16),
            pltpu.VMEM((chans * chans, n_u * (LANES // chans) * LANES), bf16),
        ]

    def rows_type(n_u):
        return jax.ShapeDtypeStruct((n_u, rows_dev, span, pair_width), bf16)

    operands = (offset, weights, slab, slab_in, solo_in, *z_in, other_z)
    near, spread = pl.pallas_call(
        functools.partial(near_kernel, plan),
        out_shape=[
            rows_type(1),
            jax.ShapeDtypeStruct((n_blocks * chans // 2 * depth, 2 * LANES), bf16),
        ],
        in_specs=[VMEM] * len(operands),
        out_specs=[VMEM] * 2,
        scratch_shapes=scratch(1),
        compiler_params=params,
        name="near",
    )(*operands)
    operands = (offset, weights, spread, near, *x_in, other_x)
    return pl.pallas_call(
        functools.partial(far_kernel, plan),
        out_shape=rows_type(n_col),
        in_specs=[VMEM] * len(operands),
        out_specs=HBM,
        scratch_shapes=scratch(n_col - 1)
        + [pltpu.VMEM((n_col - 1, rows_dev, span, pair_width), bf16), pltpu.SemaphoreType.DMA((n_col,))],
        compiler_params=params,
        name="far",
    )(*operands)


def solution(mesh):
    return jax.shard_map(
        per_device,
        mesh=mesh,
        in_specs=(P(("groups", "res", "seq"), "col", None), P(), P(), P(), P(), P(), P(), P(), P()),
        out_specs=P("groups", ("res", "seq"), "col", None),
        check_vma=False,
    )
```

```python
import functools
import math

import jax
import jax.numpy as jnp
from jax import lax
from jax.experimental import pallas as pl
from jax.experimental.pallas import tpu as pltpu
from jax.sharding import PartitionSpec as P

LANES = 128
SUBLANES = 8
VMEM = pl.BlockSpec(memory_space=pltpu.VMEM)
HBM = pl.BlockSpec(memory_space=pltpu.HBM)
ACROSS = (((1,), (1,)), ((), ()))


def partner(index, step, size):
    return index ^ step if size & (size - 1) == 0 else (index + step) % size


def routes(n_res):
    def turn(k):
        return [(z + k) % n_res for z in range(n_res)]

    def swap(k):
        return [partner(z, k, n_res) for z in range(n_res)]

    solo_route = [turn(1)] * 2
    z_routes = [[turn(k), turn(k + 1)] for k in range(2, n_res, 2)]
    x_routes = [[swap(k), swap(k + 1)] for k in range(n_res - 2, -1, -2)]
    return solo_route, z_routes, x_routes


def sources(route):
    return [[to.index(z) for z in range(len(to))] for to in route]


def look_up(route, core, chip):
    found = 0
    for k, (first, second) in enumerate(zip(*route)):
        found = jnp.where(chip == k, jnp.where(core == 0, first, second), found)
    return found


def lane_index(shape):
    return lax.broadcasted_iota(jnp.int32, shape, len(shape) - 1)


def project_kernel(n_res, solo_route, *refs):
    n_in, n_later = 7, 2
    sources, refs = refs[: n_in + n_later], refs[n_in + n_later :]
    (slab_out, solo_out), later = refs[:2], refs[2 : 2 + n_later]
    landed, (rows_scr, lane_scr, right_scr, sems) = refs[2 + n_later : -4], refs[-4:]
    copies = [
        pltpu.make_async_copy(a, b, sems.at[i]) for i, (a, b) in enumerate(zip(sources, (*landed, *later)))
    ]
    for copy in copies:
        copy.start()
    for copy in copies[:n_in]:
        copy.wait()
    x_ref, scale_ref, shift_ref, w1_ref, b1_ref, w2_ref, b2_ref = landed
    n_s, span, width = x_ref.shape
    chans = w1_ref.shape[0]
    fold = LANES // chans
    half = LANES // 2
    x = x_ref[...].reshape(n_s * span, width).astype(jnp.float32)
    mean = jnp.mean(x, axis=-1, keepdims=True)
    centred = x - mean
    variance = jnp.mean(centred * centred, axis=-1, keepdims=True)
    normed = (centred * lax.rsqrt(variance + 1e-05) * scale_ref[...] + shift_ref[...]).astype(jnp.bfloat16)

    w1 = jnp.concatenate([w1_ref[...]] * fold, axis=0)
    b1 = jnp.concatenate([b1_ref[...]] * fold, axis=1)
    rows_scr[...] = lax.dot_general(normed, w1, ACROSS, preferred_element_type=jnp.float32) + b1
    n_rows = n_s * span // fold
    owner = lane_index((n_rows, LANES)) // chans
    merged = rows_scr[pl.ds(0, n_rows, stride=fold), :]
    for turn in range(1, fold):
        merged = jnp.where(owner == turn, rows_scr[pl.ds(turn, n_rows, stride=fold), :], merged)
    groups = span // fold
    for s in range(n_s):
        lane_scr[pl.ds(s, groups, stride=n_s), :] = merged[s * groups : (s + 1) * groups]

    eye = lax.broadcasted_iota(jnp.int32, (chans, chans), 0) == lane_index((chans, chans))
    b2 = jnp.sum(jnp.where(eye, b2_ref[...], 0.0), axis=1, keepdims=True)
    right = lax.dot_general(w2_ref[...], normed, ACROSS, preferred_element_type=jnp.float32) + b2
    pairs = chans // 2
    low = lane_index((pairs, LANES)) < half
    blocks = span // half
    for tile in range(n_s * span // LANES):
        here = right[:, tile * LANES : (tile + 1) * LANES]
        there = pltpu.roll(here, half, 1)
        for side in range(2):
            s, block = divmod(2 * tile + side, blocks)
            first, second = (here, there) if side == 0 else (there, here)
            right_scr[pl.ds(block * pairs * n_s + s, pairs, stride=n_s), :] = jnp.where(
                low, first[:pairs], second[pairs:]
            )
    right_slab = right_scr[...].astype(jnp.bfloat16)
    n_right, n_left = right_scr.shape[0], lane_scr.shape[0]
    part = n_left // n_res
    slab_out[:n_right] = right_slab
    slab_out[n_right:] = lane_scr[...].astype(jnp.bfloat16)
    to = look_up(solo_route, 0, lax.axis_index("res"))
    solo_out[:n_right] = right_slab
    solo_out[n_right:] = lane_scr[pl.ds(pl.multiple_of(to * part, part), part), :].astype(jnp.bfloat16)
    for copy in copies[n_in:]:
        copy.wait()


def chip_kernel(n_res, ways, own_ref, other_ref, *outs):
    n_right = own_ref.shape[0] // 2
    part = n_right // n_res
    me, here = lax.axis_index("seq"), lax.axis_index("res")
    for route, out in zip(ways, outs):
        to = look_up(route, me, here)
        start = pl.multiple_of(n_right + to * part, part)
        at = out.shape[0] - 2 * part
        if at:
            out[:n_right] = own_ref[:n_right]
            out[n_right:at] = other_ref[:n_right]
        out[at : at + part] = own_ref[pl.ds(start, part), :]
        out[at + part :] = other_ref[pl.ds(start, part), :]


def core_kernel(bodies, part, own, *refs):
    ins, out = refs[: len(bodies)], refs[-1]
    mine = (1 - lax.axis_index("seq")) * own
    at = 0
    for body, ref in zip(bodies, ins):
        if body:
            out[at : at + body] = ref[:body]
            at += body
        for start in range(body, ref.shape[0], part):
            out[at : at + own] = ref[pl.ds(pl.multiple_of(start + mine, own), own), :]
            at += own


def weight_kernel(w_ref, _, out_ref, scr):
    chans_sq, width = w_ref.shape
    chans = int(round(chans_sq**0.5))
    scr[...] = w_ref[...].astype(jnp.float32)
    pairs = chans // 2
    fold = LANES // chans
    order = [side * pairs + pair for pair in range(pairs) for side in range(2)]
    for tile in range(chans // fold):
        piece = jnp.concatenate(
            [scr[pl.ds(e, chans, stride=chans), :] for e in order[tile * fold : (tile + 1) * fold]], axis=0
        )
        out_ref[:, tile * LANES : (tile + 1) * LANES] = piece.T.astype(jnp.bfloat16)


def fill_left(left_scr, u, slabs, n_s):
    turns = slabs[0].shape[0] // n_s
    for turn in range(turns):
        column = jnp.concatenate([slab[turn * n_s : (turn + 1) * n_s] for slab in slabs], axis=0)
        depth = column.shape[0]
        left_scr[u * LANES : (u + 1) * LANES, turn * depth : (turn + 1) * depth] = column.T.astype(jnp.bfloat16)


def loop_blocks(n_blocks, body):
    if n_blocks == 1:
        body(0)
    else:
        pl.loop(0, n_blocks)(body)


def update_block(plan, block, offset, w_ref, weight_of, left_scr, outer_scr, staged):
    chans, total = plan["chans"], plan["total"]
    half = LANES // 2
    fold = LANES // chans
    left = left_scr[...]
    n_u = left.shape[0] // LANES
    for pair in range(chans // 2):
        outer = jnp.dot(left, weight_of(pair), preferred_element_type=jnp.float32).astype(jnp.bfloat16)
        for side in range(2):
            at = (2 * pair + side) * chans
            for tile in range(n_u * fold):
                outer_scr[at : at + chans, tile * LANES : (tile + 1) * LANES] = outer[
                    tile * chans : (tile + 1) * chans, side * LANES : (side + 1) * LANES
                ]
    inverse = 1.0 / total if math.frexp(total)[0] == 0.5 else None
    step = min(fold, 2)
    for u in range(n_u):
        for first in range(0, fold, step):
            at = (u * fold + first) * LANES
            summed = jnp.dot(
                w_ref[...], outer_scr[:, at : at + step * LANES], preferred_element_type=jnp.float32
            )
            for k in range(step):
                piece = summed[:, k * LANES : (k + 1) * LANES].T
                piece = piece / total if inverse is None else piece * inverse
                piece = (piece + offset[...]).astype(jnp.bfloat16)
                for turn in range(LANES // half):
                    staged[u, turn * fold + first + k, pl.ds(block * half, half), :] = piece[
                        turn * half : (turn + 1) * half
                    ]


def row_copy(plan, step, staged, out_ref, sem):
    n_col = plan["n_col"]
    col = lax.axis_index("col")
    source = partner(col, step, n_col) if n_col & (n_col - 1) == 0 else (col - step + n_col) % n_col
    return pltpu.make_async_copy(staged, out_ref.at[source], sem)


def near_kernel(plan, offset, w_ref, own_ref, other_ref, solo_ref, *refs):
    z_refs, (other_in, staged, weights_out, left_scr, outer_scr) = refs[:-5], refs[-5:]
    chans, part, own, n_s = plan["chans"], plan["part"], plan["own"], plan["n_s"]
    n_right = part * plan["n_res"]
    half = LANES // 2
    pairs = chans // 2
    mine = pl.multiple_of(lax.axis_index("seq") * own, own)

    def rows_of(ref, at):
        return ref[pl.ds(at, own), :].astype(jnp.float32)

    start = pl.multiple_of(n_right + lax.axis_index("res") * part + mine, own)
    rights = [(own_ref, 0), (other_ref, 0), (solo_ref, 0), (other_in, 0)]
    lefts = [rows_of(own_ref, start), rows_of(other_ref, start)]
    lefts += [rows_of(solo_ref, pl.multiple_of(n_right + mine, own)), rows_of(other_in, n_right)]
    at = n_right + own
    for ref in z_refs:
        rights += [(ref, 0), (ref, n_right), (other_in, at + n_right), (other_in, at)]
        lefts += [rows_of(ref, pl.multiple_of(2 * n_right + h * part + mine, own)) for h in range(2)]
        lefts += [rows_of(other_in, at + 2 * n_right + (1 - h) * own) for h in range(2)]
        at += 2 * (n_right + own)
    fill_left(left_scr, 0, lefts, n_s)
    depth = left_scr.shape[1]

    def block_of_columns(block):
        at_block = block * pairs * n_s
        slabs = [ref[pl.ds(at + at_block, pairs * n_s), :].astype(jnp.float32) for ref, at in rights]

        below = lane_index((depth // (LANES // half), LANES)) < half
        low = below.astype(jnp.float32).astype(jnp.bfloat16)
        high = 1 - low

        def weight_of(pair):
            here = jnp.concatenate([slab[pair * n_s : (pair + 1) * n_s] for slab in slabs], axis=0)
            there = pltpu.roll(here, half, 1).astype(jnp.bfloat16)
            here = here.astype(jnp.bfloat16)
            weights = jnp.concatenate(
                [
                    jnp.concatenate([here * low, there * high], axis=0),
                    jnp.concatenate([there * low, here * high], axis=0),
                ],
                axis=1,
            )
            weights_out[pl.ds((block * pairs + pair) * depth, depth), :] = weights
            return weights

        update_block(plan, block, offset, w_ref, weight_of, left_scr, outer_scr, staged)

    loop_blocks(n_right // (pairs * n_s), block_of_columns)


def far_kernel(plan, offset_ref, w_ref, weights_ref, near_ref, *refs):
    x_refs, (other_in, out_ref, left_scr, outer_scr, staged, sems) = refs[:-6], refs[-6:]
    chans, part, own, n_s, n_res = plan["chans"], plan["part"], plan["own"], plan["n_s"], plan["n_res"]
    pairs = chans // 2
    me = lax.axis_index("seq")
    copies = [row_copy(plan, 0, near_ref.at[0], out_ref, sems.at[0])]
    copies[0].start()

    def rows_of(ref, at):
        return ref[pl.ds(at, own), :].astype(jnp.float32)

    here = lax.axis_index("res")
    order = [here, look_up(sources(plan["solo"]), me, here)]
    for route in plan["z_routes"]:
        order += [look_up(sources(route), core, here) for core in (me, 1 - me)]
    x_routes = plan["x_routes"]
    for u in range(plan["n_col"] - 1):
        held = []
        for k, route in enumerate(x_routes):
            place = u * len(x_routes) + k
            heard = [rows_of(x_refs[place], pl.multiple_of(h * part + me * own, own)) for h in range(2)]
            told = [rows_of(other_in, (2 * place + 1 - h) * own) for h in range(2)]
            held += [(look_up(sources(route), me, here), heard), (look_up(sources(route), 1 - me, here), told)]
        slabs = []
        for chip in order:
            for side in range(2):
                found = held[0][1][side]
                for source, slab in held[1:]:
                    found = jnp.where(source == chip, slab[side], found)
                slabs.append(found)
        fill_left(left_scr, u, slabs, n_s)
    depth = left_scr.shape[1]

    def block_of_columns(block):
        def weight_of(pair):
            return weights_ref[pl.ds((block * pairs + pair) * depth, depth), :]

        update_block(plan, block, offset_ref, w_ref, weight_of, left_scr, outer_scr, staged)

    loop_blocks(weights_ref.shape[0] // (pairs * depth), block_of_columns)
    for u in range(staged.shape[0]):
        copies.append(row_copy(plan, 1 + u, staged.at[u], out_ref, sems.at[1 + u]))
        copies[-1].start()
    for copy in copies:
        copy.wait()


def per_device(alignment, scale, shift, w1, b1, w2, b2, w_final, offset):
    n_s, span, width = alignment.shape
    n_res, n_col, n_seq = lax.axis_size("res"), lax.axis_size("col"), lax.axis_size("seq")
    chans, pair_width = w1.shape[1], w_final.shape[1]
    bf16 = jnp.bfloat16
    n_right = span * chans * n_s // LANES
    n_left = span * chans * n_s // LANES
    part = n_left // n_res
    own = part // n_seq
    rows_dev = span // (n_res * n_seq)
    params = pltpu.CompilerParams(vmem_limit_bytes=32 * 1024 * 1024)

    def rows(n):
        return jax.ShapeDtypeStruct((n, LANES), bf16)

    solo, z_routes, x_routes = routes(n_res)

    taken = (alignment, scale.reshape(1, -1), shift.reshape(1, -1), w1.T, b1.reshape(1, -1), w2.T, b2.reshape(1, -1))
    later = (w_final, offset.reshape(1, -1))
    slab, solo_out, w_final, offset = pl.pallas_call(
        functools.partial(project_kernel, n_res, solo),
        out_shape=[rows(n_right + n_left), rows(n_right + part)]
        + [jax.ShapeDtypeStruct(a.shape, a.dtype) for a in later],
        in_specs=[HBM] * len(taken + later),
        out_specs=[VMEM] * 4,
        scratch_shapes=[pltpu.VMEM(a.shape, a.dtype) for a in taken]
        + [
            pltpu.VMEM((n_s * span, LANES), jnp.float32),
            pltpu.VMEM((n_left, LANES), jnp.float32),
            pltpu.VMEM((n_right, LANES), jnp.float32),
            pltpu.SemaphoreType.DMA((len(taken + later),)),
        ],
        compiler_params=params,
        name="project",
    )(*[pltpu.with_memory_space_constraint(a, pltpu.HBM) for a in taken + later])

    def to_core(array):
        return lax.ppermute(array, "seq", [(q, 1 - q) for q in range(n_seq)])

    def to_chip(array, step_col, route):
        pairs = []
        for r in range(n_res):
            for c in range(n_col):
                for q in range(n_seq):
                    to = route[q][r] * n_col + partner(c, step_col, n_col)
                    pairs.append(((r * n_col + c) * n_seq + q, to * n_seq + q))
        return lax.ppermute(array, ("res", "col", "seq"), pairs)

    slab_in = to_core(slab)
    solo_in = to_chip(solo_out, 0, solo)
    sends = [(0, route) for route in z_routes] + [(u, route) for u in range(1, n_col) for route in x_routes]
    messages = pl.pallas_call(
        functools.partial(chip_kernel, n_res, [route for _, route in sends]),
        out_shape=[rows(2 * part + (0 if u else 2 * n_right)) for u, _ in sends],
        in_specs=[VMEM] * 2,
        out_specs=[VMEM] * len(sends),
        compiler_params=params,
        name="chip",
    )(slab, slab_in)
    heard = [to_chip(message, u, route) for message, (u, route) in zip(messages, sends)]

    def pack(arrays, bodies, flops, after=()):
        return pl.pallas_call(
            functools.partial(core_kernel, bodies, part, own),
            out_shape=rows(sum(b + (a.shape[0] - b) // part * own for a, b in zip(arrays, bodies))),
            in_specs=[VMEM] * (len(arrays) + len(after)),
            out_specs=VMEM,
            compiler_params=params,
            cost_estimate=pl.CostEstimate(flops=flops, bytes_accessed=0, transcendentals=0),
            name="core",
        )(*arrays, *after)

    z_in, x_in = heard[: len(z_routes)], heard[len(z_routes) :]
    arrays = [pack([solo_in], [n_right], 500_000_000)] + z_in
    weights = pl.pallas_call(
        weight_kernel,
        out_shape=jax.ShapeDtypeStruct((pair_width, chans * chans), bf16),
        in_specs=[VMEM] * 2,
        out_specs=VMEM,
        scratch_shapes=[pltpu.VMEM((chans * chans, pair_width), jnp.float32)],
        compiler_params=params,
        name="weights",
    )(w_final, arrays[0])
    other_z = to_core(pack(arrays, [n_right + own] + [2 * n_right] * len(z_in), 0))
    other_x = to_core(pack(x_in, [0] * len(x_in), 20_000_000_000, (weights,)))

    turns = rows_dev * chans // LANES
    depth = turns * n_s * n_res * n_seq
    plan = dict(n_res=n_res, n_col=n_col, chans=chans, part=part, own=own, n_s=n_s, total=float(n_s * n_res * n_seq))
    plan.update(solo=solo, z_routes=z_routes, x_routes=x_routes)
    n_blocks = n_right // (chans // 2 * n_s)

    def scratch(n_u):
        return [
            pltpu.VMEM((n_u * LANES, depth), bf16),
            pltpu.VMEM((chans * chans, n_u * (LANES // chans) * LANES), bf16),
        ]

    def rows_type(n_u):
        return jax.ShapeDtypeStruct((n_u, rows_dev, span, pair_width), bf16)

    operands = (offset, weights, slab, slab_in, solo_in, *z_in, other_z)
    near, spread = pl.pallas_call(
        functools.partial(near_kernel, plan),
        out_shape=[
            rows_type(1),
            jax.ShapeDtypeStruct((n_blocks * chans // 2 * depth, 2 * LANES), bf16),
        ],
        in_specs=[VMEM] * len(operands),
        out_specs=[VMEM] * 2,
        scratch_shapes=scratch(1),
        compiler_params=params,
        name="near",
    )(*operands)
    operands = (offset, weights, spread, near, *x_in, other_x)
    return pl.pallas_call(
        functools.partial(far_kernel, plan),
        out_shape=rows_type(n_col),
        in_specs=[VMEM] * len(operands),
        out_specs=HBM,
        scratch_shapes=scratch(n_col - 1)
        + [pltpu.VMEM((n_col - 1, rows_dev, span, pair_width), bf16), pltpu.SemaphoreType.DMA((n_col,))],
        compiler_params=params,
        name="far",
    )(*operands)


def solution(mesh):
    return jax.shard_map(
        per_device,
        mesh=mesh,
        in_specs=(P(("groups", "res", "seq"), "col", None), P(), P(), P(), P(), P(), P(), P(), P()),
        out_specs=P("groups", ("res", "seq"), "col", None),
        check_vma=False,
    )
```
